256 devices in a mesh: dp: 64 (over x, z, core), mp: 4 (over y).
Axes of the slice: x: 4, y: 4, z: 8, core: 2. Of those that a mesh axis runs over, the one named last changes fastest.
Arguments:
- pool_inputs: bfloat16 [8192, 8, 4096], P('dp', None, 'mp'), may hold values from -6 to 6
- pool_targets: bfloat16 [8192, 8, 4096], P('dp', None, 'mp'), may hold values from -6 to 6
- frozen: bfloat16 [4096, 4096], P(None, 'mp'), may hold values from -0.09375 to 0.09375
- gain: float32 [4096], P('mp'), may hold values from 0.5 to 1.5
- adapter_down: bfloat16 [64, 64, 4096], P('dp', None, 'mp'), may hold values from -0.09375 to 0.09375
- adapter_up: bfloat16 [64, 64, 4096], P('dp', None, 'mp'), may hold values from -0.75 to 0.75
- sample_ids: int32 [4096], P('dp'), may hold values from 0 to 127
- buckets: int32 [8192], P('dp'), may hold values from 0 to 15
- lengths: int32 [8192], P('dp'), may hold values from 1 to 8
- destinations: int32 [4096, 1], P('dp'), may hold values from 0 to 63; in each aligned block of 64 rows (0 to 63, 64 to 127, ...) at most 2 rows name the same one
- competence: float32 [1], replicated, may hold values from 0.3 to 0.7
Outputs:
- grad_down: float32 [64, 64, 4096], P('dp', None, 'mp')
- grad_up: float32 [64, 64, 4096], P('dp', None, 'mp')
- bucket_loss: float32 [16], replicated
- competence_next: float32 [1], replicated
The draws below stay inside these ranges and needn't reach their ends.
Inputs may be any that keep to these rules, and one draw needn't show every extreme that they name: `destinations`: of the 64 sampled slots of one holder, at most 2 name the same trainer. `sample_ids`: an index into the holder's own 128 stored blocks.
All inputs are finite; a program needn't handle non-finite values.
Results may differ from the reference program's by a relative error of at most 0.0056.
Values may be sent and summed in bfloat16 or wider, within the bound.
No kernel may reach another device: no remote copies, remote signals or barrier semaphores. Data moves between devices by JAX's collectives and lax.ppermute only.
A program may use at most 128 MiB of HBM per device.

```python
import math
import jax
import jax.numpy as jnp
import numpy as np
from jax import lax

D = 4096
R = 64
NB = 16
BLK = 8
SEQ_DEV = 64
POOL_DEV = 128
SAMPLED = 4096
POOLED = 8192
MOST = 2
N_DP = 64


def with_ends(array, rng, least, high):
    place = [jax.random.randint(jax.random.fold_in(rng, axis), (), 0, length) for axis, length in enumerate(array.shape)]
    widest = array.shape.index(max(array.shape))
    next_to = place[:widest] + [(place[widest] + 1) % array.shape[widest]] + place[widest + 1:]
    return array.at[tuple(place)].set(least).at[tuple(next_to)].set(high)


def steps_of(own_key, shape, split, low, high):
    def one(dim, blocks):
        draws = jax.random.uniform(jax.random.fold_in(jax.random.fold_in(own_key, 6), dim), (blocks,), jnp.float32, low / len(split), high / len(split))
        return jnp.repeat(jnp.exp(draws), shape[dim] // blocks).reshape((-1,) + (1,) * (len(shape) - dim - 1))

    level = one(*split[0])
    for cut in split[1:]:
        level = level * one(*cut)
    return level


def routed_block(rng, own, number, rows, count, top, reach, lean):
    sequence = jax.random.permutation(rng, count)
    heavy_load, common = portions_of(count, rows * top, reach, lean, True), portions_of(count, rows * top, reach, lean, False)
    places = jnp.arange(count)

    def named(sizes, offset_by):
        used = int((sizes > 0).sum())
        fixed = max(1, used // 4)
        shifted = fixed + (places - fixed + offset_by * (used - fixed)) % max(1, count - fixed)
        return jnp.zeros((count,), jnp.int32).at[sequence[jnp.where(places < fixed, places, shifted)]].set(jnp.asarray(sizes, jnp.int32))

    sizes = jnp.where(number % 4 == 0, named(heavy_load, number // 4), named(common, number - number // 4 - 1))
    mixed = jax.random.permutation(jax.random.fold_in(own, 3), count)
    source_of, sink = mixed[0:count // 2 * 2:2], mixed[1:count // 2 * 2:2]
    margin = jnp.minimum(sizes[source_of] - 1, reach - sizes[sink]) // 2
    margin = jnp.where((source_of == sequence[0]) | (sink == sequence[0]) | (sizes[sink] == 0), 0, jnp.maximum(margin, 0))
    shifted = jax.random.randint(jax.random.fold_in(own, 4), (count // 2,), 0, 1 << 20) % (margin + 1)
    sizes = sizes.at[source_of].add(-shifted).at[sink].add(shifted)
    members = jnp.searchsorted(jnp.cumsum(sizes), jnp.arange(rows * top), side="right").astype(jnp.int32)
    listing = members.reshape(top, rows).T
    listing = listing[jax.random.permutation(jax.random.fold_in(own, 1), rows)]
    offset_by = jax.random.randint(jax.random.fold_in(own, 2), (rows, 1), 0, top)
    return jnp.take_along_axis(listing, (jnp.arange(top)[None, :] + offset_by) % top, axis=1)


def portions_of(count, total, bound, lean, full):
    loads = [(1 << 20) // math.isqrt(standing ** lean) + 1 for standing in range(1, count + 1)]
    largest = bound if full else min(bound, max(-(-total // count), total * loads[0] // sum(loads)))
    least = 1 if total - largest >= count - 1 else 0
    holding, spare = [largest] + [least] * (count - 1), total - largest - least * (count - 1)
    while spare > 0:
        candidates = [i for i in range(1, count) if holding[i] < largest] or [i for i in range(1, count) if holding[i] < bound]
        whole, left = sum([loads[i] for i in candidates]), spare
        for i in candidates:
            more = min(bound - holding[i], max(1, left * loads[i] // whole), spare)
            holding[i] = holding[i] + more
            spare = spare - more
    return np.array(holding)


def gaussian(stream_key, extent, width, most, cuts=(), kind=jnp.bfloat16):
    loudness = steps_of(stream_key, extent, cuts, -0.22, 0.18) if cuts else 1.0
    drawn = jax.random.normal(stream_key, extent, jnp.float32) * width * loudness
    return jnp.minimum(jnp.maximum(drawn, -most), most).astype(kind)


def setup_inputs(seed: int = 0) -> dict:
    splits = jax.random.split(jax.random.key(seed), 12)
    pool_inputs = gaussian(splits[0], (POOLED, BLK, D), 1.0, 6.0, ((0, 64), (2, 4)))
    pool_targets = gaussian(splits[1], (POOLED, BLK, D), 1.0, 6.0, ((0, 64), (2, 4)))
    frozen = gaussian(splits[2], (D, D), D ** -0.5, 0.09375, ((1, 4),))
    gain = jnp.clip(1.0 + 0.1 * jax.random.normal(splits[3], (D,), jnp.float32), 0.5, 1.5)
    adapter_down = gaussian(splits[4], (N_DP, R, D), D ** -0.5, 0.09375, ((0, 64), (2, 4)))
    adapter_up = gaussian(splits[5], (N_DP, R, D), R ** -0.5, 0.75, ((0, 64), (2, 4)))
    sample_ids = with_ends(jax.random.randint(splits[6], (SAMPLED,), 0, POOL_DEV), jax.random.fold_in(splits[6], 1), 0, POOL_DEV - 1).astype(jnp.int32)
    buckets = with_ends(jax.random.randint(splits[7], (POOLED,), 0, NB), jax.random.fold_in(splits[7], 1), 0, NB - 1).astype(jnp.int32)
    lengths = with_ends(jax.random.randint(splits[8], (POOLED,), 1, BLK + 1), jax.random.fold_in(splits[8], 1), 1, BLK).astype(jnp.int32)
    destinations_keys = jax.random.split(jax.random.fold_in(splits[9], 1), SAMPLED // SEQ_DEV)
    destinations_turns = jax.random.permutation(jax.random.fold_in(splits[9], 3), SAMPLED // SEQ_DEV)
    destinations = jax.vmap(lambda own, number: routed_block(jax.random.fold_in(splits[9], 2), own, number, SEQ_DEV, N_DP, 1, MOST, 2))(destinations_keys, destinations_turns).reshape((SAMPLED, 1))
    competence = jnp.clip(jax.random.uniform(splits[10], (1,), jnp.float32, 0.3, 0.7), 0.3, 0.7)
    return {"pool_inputs": pool_inputs, "pool_targets": pool_targets, "frozen": frozen, "gain": gain, "adapter_down": adapter_down, "adapter_up": adapter_up, "sample_ids": sample_ids, "buckets": buckets, "lengths": lengths, "destinations": destinations, "competence": competence}


RMS_EPSILON = 1e-05
SHARPNESS = 12.0
ADAPTER_SCALING = 2.0

def normalize(values, gain):
    inverse_rms = lax.rsqrt(lax.optimization_barrier(jnp.mean(values * values, axis=-1, keepdims=True)) + RMS_EPSILON)
    return (values * inverse_rms * gain).astype(jnp.bfloat16)

def reference(pool_inputs, pool_targets, frozen, gain, adapter_down, adapter_up, sample_ids, buckets, lengths, destinations, competence):
    holder = (jnp.arange(SAMPLED) // SEQ_DEV).astype(jnp.int32)
    picked = (holder * POOL_DEV + sample_ids).astype(jnp.int32)
    inputs = jnp.take(pool_inputs, picked, axis=0).reshape(SAMPLED * BLK, D).astype(jnp.float32)
    normed = normalize(inputs, gain)
    targets = jnp.take(pool_targets, picked, axis=0).reshape(SAMPLED * BLK, D).astype(jnp.float32)
    base_gap = (inputs + jnp.dot(normed, frozen, preferred_element_type=jnp.float32) - targets).astype(jnp.bfloat16)
    normed = normed.reshape(SAMPLED, BLK, D)
    base_gap = base_gap.reshape(SAMPLED, BLK, D)
    block_bucket = jnp.take(buckets, picked)
    block_length = jnp.take(lengths, picked)
    bucket_onehot = (block_bucket[:, None] == jnp.arange(NB, dtype=jnp.int32)[None, :]).astype(jnp.float32)
    counts = lax.optimization_barrier(jnp.sum(bucket_onehot * block_length[:, None].astype(jnp.float32), axis=0))
    floor_counts = jnp.maximum(counts, 1.0)
    weights = jax.nn.sigmoid(SHARPNESS * (competence[0] - (jnp.arange(NB).astype(jnp.float32) + 0.5) / NB))
    block_coefficient = lax.optimization_barrier(jnp.sum(bucket_onehot * (weights / floor_counts)[None, :], axis=1))
    target_trainer = destinations[:, 0]
    by_trainer = jnp.argsort(target_trainer, stable=True).astype(jnp.int32)
    per_count = lax.optimization_barrier(jnp.sum((target_trainer[:, None] == jnp.arange(N_DP, dtype=jnp.int32)[None, :]).astype(jnp.int32), axis=0))
    first_block = (jnp.cumsum(per_count) - per_count).astype(jnp.int32)
    block_capacity = N_DP * MOST

    def trainer(trainer_position_index):
        slot_ids = jnp.arange(block_capacity, dtype=jnp.int32)
        occupied = slot_ids < per_count[trainer_position_index]
        block_ids = by_trainer[jnp.minimum(first_block[trainer_position_index] + slot_ids, SAMPLED - 1)]
        normed_rows = normed[block_ids].reshape(block_capacity * BLK, D)
        gap_rows = base_gap[block_ids].reshape(block_capacity * BLK, D).astype(jnp.float32)
        live_lengths = jnp.where(occupied, block_length[block_ids], 0)
        live_mask = (jnp.arange(BLK, dtype=jnp.int32)[None, :] < live_lengths[:, None]).astype(jnp.float32).reshape(-1)
        row_coefficient = jnp.repeat(block_coefficient[block_ids], BLK)
        down_map = adapter_down[trainer_position_index]
        up_map = adapter_up[trainer_position_index]
        latent_rows = jnp.dot(normed_rows, down_map.T, preferred_element_type=jnp.float32)
        lowered_rows = (ADAPTER_SCALING * latent_rows).astype(jnp.bfloat16)
        distance = gap_rows + jnp.dot(lowered_rows, up_map, preferred_element_type=jnp.float32)
        output_grad = ((2.0 * row_coefficient * live_mask)[:, None] * distance).astype(jnp.bfloat16)
        latent_gradient = jnp.dot(output_grad, up_map.T, preferred_element_type=jnp.float32)
        lowered_gradient = (ADAPTER_SCALING * latent_gradient).astype(jnp.bfloat16)
        up_gradient = jnp.dot(lowered_rows.T, output_grad, preferred_element_type=jnp.float32)
        down_gradient = jnp.dot(lowered_gradient.T, normed_rows, preferred_element_type=jnp.float32)
        block_square = lax.optimization_barrier(jnp.sum((lax.optimization_barrier(jnp.sum(distance * distance, axis=1)) * live_mask).reshape(block_capacity, BLK), axis=1))
        slot_onehot = bucket_onehot[block_ids] * occupied[:, None].astype(jnp.float32)
        partial_value = lax.optimization_barrier(jnp.sum(slot_onehot * block_square[:, None], axis=0))
        return (down_gradient, up_gradient, partial_value)
    grad_down, grad_up, partials = lax.map(trainer, jnp.arange(N_DP, dtype=jnp.int32))
    bucket_loss = lax.optimization_barrier(jnp.sum(partials, axis=0)) / (floor_counts * D)
    progress = jnp.sum(weights * bucket_loss) / jnp.sum(bucket_loss)
    competence_next = competence + 0.5 * (1.0 - competence) * progress
    return (grad_down, grad_up, bucket_loss, competence_next)
```

```python
import jax
import jax.numpy as jnp
from jax import lax
from jax.experimental import pallas as pl
from jax.experimental.pallas import tpu as pltpu
from jax.sharding import Mesh
from jax.sharding import PartitionSpec as P

NB = 16
DP = ("dp_0", "dp_1", "dp_2")
DP_MP = ("dp_0", "dp_1", "dp_2", "mp")

RMS_EPSILON = 1e-05
SHARPNESS = 12.0
ADAPTER_SCALING = 2.0
PER_PAIR = 2
VMEM_BYTES = 48 * 1024 * 1024
CONTRACT_LAST = (((1,), (1,)), ((), ()))
CONTRACT_FIRST = (((0,), (0,)), ((), ()))


def of_everyone(value, axis):
    peers = lax.axis_size(axis)
    everything = lax.all_to_all(
        jnp.broadcast_to(value[None], (peers, *value.shape)), axis, 0, 0, tiled=True
    )
    return jnp.sum(everything, axis=0)


def route_kernel(
    ids, dest, buckets, lengths, pool, send, own, info, counts, slot_of, arrived, source, sem
):
    sampled = ids.shape[0]
    slots = send.shape[0]

    def clear(k, carry):
        arrived[k] = 0
        for s in range(PER_PAIR):
            source[k * PER_PAIR + s] = ids[0]
            info[k, s] = 0
            info[k, PER_PAIR + s] = 0
        return carry

    def clear_counts(b, carry):
        counts[b] = 0
        return carry

    lax.fori_loop(0, slots // PER_PAIR, clear, 0)
    lax.fori_loop(0, NB, clear_counts, 0)

    def place(j, carry):
        block = ids[j]
        trainer = dest[j]
        pltpu.make_async_copy(pool.at[block], own.at[j], sem.at[0]).start()
        order = arrived[trainer]
        arrived[trainer] = order + 1
        slot = trainer * PER_PAIR + order
        slot_of[j] = slot
        source[slot] = block
        bucket = buckets[block]
        length = lengths[block]
        info[trainer, order] = bucket
        info[trainer, PER_PAIR + order] = length
        counts[bucket] = counts[bucket] + length
        return carry

    lax.fori_loop(0, sampled, place, 0)

    def copy(s, carry):
        pltpu.make_async_copy(pool.at[source[s]], send.at[s], sem.at[1]).start()
        return carry

    lax.fori_loop(0, slots, copy, 0)

    def list_free(k, found):
        for s in range(PER_PAIR):
            free = arrived[k] <= s

            @pl.when(free)
            def _():
                slot_of[sampled + found] = k * PER_PAIR + s

            found = found + jnp.where(free, 1, 0)
        return found

    lax.fori_loop(0, slots // PER_PAIR, list_free, 0)
    pltpu.make_async_copy(pool.at[pl.ds(0, sampled)], own, sem.at[0]).wait()
    pltpu.make_async_copy(send, send, sem.at[1]).wait()


def route(ids, dest, buckets, lengths, pool, trainers):
    sampled = ids.shape[0]
    slots = trainers * PER_PAIR
    block = pool.shape[1:]
    smem = pl.BlockSpec(memory_space=pltpu.SMEM)
    hbm = pl.BlockSpec(memory_space=pl.ANY)
    return pl.pallas_call(
        route_kernel,
        out_shape=(
            jax.ShapeDtypeStruct((slots, *block), pool.dtype),
            jax.ShapeDtypeStruct((sampled, *block), pool.dtype),
            jax.ShapeDtypeStruct((trainers, 2 * PER_PAIR), jnp.int32),
            jax.ShapeDtypeStruct((NB,), jnp.int32),
            jax.ShapeDtypeStruct((slots,), jnp.int32),
        ),
        in_specs=[smem, smem, smem, smem, hbm],
        out_specs=(hbm, hbm, smem, smem, smem),
        scratch_shapes=[
            pltpu.SMEM((trainers,), jnp.int32),
            pltpu.SMEM((slots,), jnp.int32),
            pltpu.SemaphoreType.DMA((2,)),
        ],
        cost_estimate=pl.CostEstimate(flops=0, bytes_accessed=6 << 20, transcendentals=0),
        name="route",
    )(ids, dest, buckets, lengths, pool)


def gap_kernel(
    ids, slot_of, gathered, own, gain, frozen, targets, send, normed, target_rows, gap, sem
):
    step = pl.program_id(0)
    parts, rows, part = gathered.shape
    sampled, block_len, columns = gap.shape
    width = frozen.shape[1]
    slots = send.shape[0]

    @pl.when(step == 0)
    def _():
        def fetch(j, carry):
            pltpu.make_async_copy(targets.at[ids[j]], target_rows.at[j], sem.at[0]).start()
            return carry

        lax.fori_loop(0, sampled, fetch, 0)
        chunk = 128

        def normalize(i, carry):
            at = pl.ds(pl.multiple_of(i * chunk, chunk), chunk)
            total = jnp.zeros((chunk, 1), jnp.float32)
            for p in range(parts):
                x = gathered[p, at, :].astype(jnp.float32)
                total = total + jnp.sum(x * x, axis=1, keepdims=True)
            inverse = lax.rsqrt(total / (parts * part) + RMS_EPSILON)
            for p in range(parts):
                x = gathered[p, at, :].astype(jnp.float32)
                normed[p, at, :] = (x * inverse * gain[p : p + 1, :]).astype(jnp.bfloat16)
            return carry

        lax.fori_loop(0, rows // chunk, normalize, 0)
        pltpu.make_async_copy(targets.at[pl.ds(0, sampled)], target_rows, sem.at[0]).wait()

    def multiply(p, total):
        weights = frozen[pl.ds(pl.multiple_of(p * part, part), part), :]
        return total + jnp.dot(normed[p], weights, preferred_element_type=jnp.float32)

    projected = lax.fori_loop(0, parts, multiply, jnp.zeros((rows, width), jnp.float32))
    at = pl.ds(pl.multiple_of(step * width, width), width)
    x = own[:, :, at].astype(jnp.float32)
    t = target_rows[:, :, at].astype(jnp.float32)
    gap[:, :, at] = (x + projected.reshape(sampled, block_len, width) - t).astype(jnp.bfloat16)

    @pl.when(step == pl.num_programs(0) - 1)
    def _():
        def place(j, carry):
            pltpu.make_async_copy(gap.at[j], send.at[slot_of[j]], sem.at[1]).start()
            return carry

        lax.fori_loop(0, sampled, place, 0)

        def fill(s, carry):
            pltpu.make_async_copy(gap.at[0], send.at[slot_of[sampled + s]], sem.at[1]).start()
            return carry

        lax.fori_loop(0, slots - sampled, fill, 0)
        pltpu.make_async_copy(send, send, sem.at[1]).wait()


def base_gap_slots(ids, slot_of, gathered, own, gain, frozen, targets):
    parts, rows, part = gathered.shape
    width, columns = frozen.shape
    slots = slot_of.shape[0]
    tile = 256
    smem = pl.BlockSpec(memory_space=pltpu.SMEM)
    hbm = pl.BlockSpec(memory_space=pl.ANY)
    return pl.pallas_call(
        gap_kernel,
        grid=(columns // tile,),
        out_shape=jax.ShapeDtypeStruct((slots, *own.shape[1:]), jnp.bfloat16),
        in_specs=[
            smem,
            smem,
            pl.BlockSpec(gathered.shape, lambda n: (0, 0, 0)),
            pl.BlockSpec(own.shape, lambda n: (0, 0, 0)),
            pl.BlockSpec(gain.shape, lambda n: (0, 0)),
            pl.BlockSpec((width, tile), lambda n: (0, n)),
            hbm,
        ],
        out_specs=hbm,
        scratch_shapes=[
            pltpu.VMEM(gathered.shape, jnp.bfloat16),
            pltpu.VMEM(own.shape, jnp.bfloat16),
            pltpu.VMEM(own.shape, jnp.bfloat16),
            pltpu.SemaphoreType.DMA((2,)),
        ],
        compiler_params=pltpu.CompilerParams(vmem_limit_bytes=VMEM_BYTES),
        cost_estimate=pl.CostEstimate(
            flops=2 * rows * width * columns, bytes_accessed=18 << 20, transcendentals=rows
        ),
        name="base_gap",
    )(ids, slot_of, gathered, own, gain, frozen, targets)


def trainer_kernel(gap, lowered, up, facts, grad_up, back, loss):
    step = pl.program_id(0)
    low = lowered[...]
    up_map = up[...]
    facts_now = facts[...]
    distance = gap[...].astype(jnp.float32) + lax.dot_general(
        low, up_map, CONTRACT_FIRST, preferred_element_type=jnp.float32
    )
    output_grad = (facts_now[:, NB : NB + 1] * distance).astype(jnp.bfloat16)
    squares = jnp.sum(distance * distance, axis=1, keepdims=True)
    part = jnp.sum(facts_now * squares, axis=0, keepdims=True)
    back[...] = lax.dot_general(
        up_map, output_grad, CONTRACT_LAST, preferred_element_type=jnp.float32
    )
    own = jnp.dot(low, output_grad, preferred_element_type=jnp.float32)

    @pl.when(step == 0)
    def _():
        grad_up[...] = own
        loss[...] = part

    @pl.when(step > 0)
    def _():
        grad_up[...] += own
        loss[...] += part


def trainer_step(gap, lowered, up, facts):
    rows, columns = gap.shape
    rank = up.shape[0]
    lanes = facts.shape[1]
    chunk = 256
    return pl.pallas_call(
        trainer_kernel,
        grid=(rows // chunk,),
        out_shape=(
            jax.ShapeDtypeStruct((rank, columns), jnp.float32),
            jax.ShapeDtypeStruct((rank, rows), jnp.float32),
            jax.ShapeDtypeStruct((1, lanes), jnp.float32),
        ),
        in_specs=[
            pl.BlockSpec((chunk, columns), lambda i: (i, 0)),
            pl.BlockSpec((rank, chunk), lambda i: (0, i)),
            pl.BlockSpec((rank, columns), lambda i: (0, 0)),
            pl.BlockSpec((chunk, lanes), lambda i: (i, 0)),
        ],
        out_specs=(
            pl.BlockSpec((rank, columns), lambda i: (0, 0)),
            pl.BlockSpec((rank, chunk), lambda i: (0, i)),
            pl.BlockSpec((1, lanes), lambda i: (0, 0)),
        ),
        compiler_params=pltpu.CompilerParams(vmem_limit_bytes=VMEM_BYTES),
        cost_estimate=pl.CostEstimate(
            flops=6 * rows * rank * columns, bytes_accessed=4 << 20, transcendentals=0
        ),
        name="trainer_step",
    )(gap, lowered, up, facts)


def on_device(
    pool_inputs,
    pool_targets,
    frozen,
    gain,
    adapter_down,
    adapter_up,
    sample_ids,
    buckets,
    lengths,
    destinations,
    competence,
):
    trainers = lax.axis_size(DP)
    parts = lax.axis_size("mp")
    sampled = sample_ids.shape[0]
    _, block_len, part = pool_inputs.shape
    width = frozen.shape[0]
    slots = trainers * PER_PAIR
    rows = slots * block_len
    per_peer = PER_PAIR * block_len
    down_map = adapter_down[0]
    up_map = adapter_up[0]
    bucket_range = jnp.arange(NB, dtype=jnp.int32)

    send_x, own_x, info, counts, slot_of = route(
        sample_ids, destinations[:, 0], buckets, lengths, pool_inputs, trainers
    )
    got_x = lax.all_to_all(
        send_x.reshape(trainers, per_peer, part), DP, 0, 0, tiled=True
    )
    whole_gain = lax.all_gather(gain, "mp")
    gathered = lax.all_gather(own_x.reshape(sampled * block_len, part), "mp")
    message = jnp.concatenate(
        [info, jnp.broadcast_to(counts[None, :], (trainers, NB))], axis=1
    )
    got_info = lax.all_to_all(message[:, None, :], DP, 0, 0, tiled=True)[:, 0, :]

    send_gap = base_gap_slots(
        sample_ids,
        slot_of,
        gathered,
        own_x,
        whole_gain,
        frozen,
        pool_targets,
    )
    got_gap = lax.all_to_all(
        send_gap.reshape(trainers, per_peer, part), DP, 0, 0, tiled=True
    )

    floor_counts = jnp.maximum(
        jnp.sum(got_info[:, 2 * PER_PAIR :], axis=0).astype(jnp.float32), 1.0
    )
    weights = jax.nn.sigmoid(
        SHARPNESS * (competence[0] - (bucket_range.astype(jnp.float32) + 0.5) / NB)
    )
    row_bucket = jnp.repeat(got_info[:, :PER_PAIR].reshape(slots), block_len)
    row_length = jnp.repeat(got_info[:, PER_PAIR : 2 * PER_PAIR].reshape(slots), block_len)
    live = (jnp.arange(rows, dtype=jnp.int32) % block_len < row_length).astype(jnp.float32)
    onehot = (row_bucket[:, None] == bucket_range[None, :]).astype(jnp.float32) * live[:, None]
    coefficient = 2.0 * jnp.sum(onehot * (weights / floor_counts)[None, :], axis=1)
    facts = jnp.concatenate(
        [onehot, coefficient[:, None], jnp.zeros((rows, 128 - NB - 1), jnp.float32)], axis=1
    )

    values = got_x.reshape(rows, part).astype(jnp.float32)
    square_total = of_everyone(jnp.sum(values * values, axis=1), "mp")
    inverse_rms = lax.rsqrt(square_total / width + RMS_EPSILON)
    normed = (values * inverse_rms[:, None] * gain[None, :]).astype(jnp.bfloat16)
    latent_part = lax.dot_general(
        down_map, normed, CONTRACT_LAST, preferred_element_type=jnp.float32
    )
    lowered = (ADAPTER_SCALING * of_everyone(latent_part, "mp")).astype(jnp.bfloat16)

    grad_up, back_part, loss_part = trainer_step(
        got_gap.reshape(rows, part), lowered, up_map, facts
    )
    loss_sum = lax.psum(loss_part[0, :NB], DP_MP)
    lowered_gradient = (ADAPTER_SCALING * of_everyone(back_part, "mp")).astype(jnp.bfloat16)
    grad_down = jnp.dot(lowered_gradient, normed, preferred_element_type=jnp.float32)
    bucket_loss = loss_sum / (floor_counts * width)
    progress = jnp.sum(weights * bucket_loss) / jnp.sum(bucket_loss)
    competence_next = competence + 0.5 * (1.0 - competence) * progress
    return (grad_down[None], grad_up[None], bucket_loss, competence_next)


def solution(mesh):
    split = Mesh(mesh.devices.reshape(4, 8, 2, mesh.shape["mp"]), DP_MP)
    placed = (
        P(DP, None, "mp"),
        P(DP, None, "mp"),
        P(None, "mp"),
        P("mp"),
        P(DP, None, "mp"),
        P(DP, None, "mp"),
        P(DP),
        P(DP),
        P(DP),
        P(DP, None),
        P(),
    )
    return jax.shard_map(
        on_device,
        mesh=split,
        in_specs=placed,
        out_specs=(P(DP, None, "mp"), P(DP, None, "mp"), P(), P()),
        check_vma=False,
    )
```

```python
import jax
import jax.numpy as jnp
from jax import lax
from jax.experimental import pallas as pl
from jax.experimental.pallas import tpu as pltpu
from jax.sharding import Mesh
from jax.sharding import PartitionSpec as P

NB = 16
DP = ("dp_0", "dp_1", "dp_2")
DP_MP = ("dp_0", "dp_1", "dp_2", "mp")

RMS_EPSILON = 1e-05
SHARPNESS = 12.0
ADAPTER_SCALING = 2.0
PER_PAIR = 2
VMEM_BYTES = 48 * 1024 * 1024
CONTRACT_LAST = (((1,), (1,)), ((), ()))
CONTRACT_FIRST = (((0,), (0,)), ((), ()))


def of_everyone(value, axis):
    peers = lax.axis_size(axis)
    everything = lax.all_to_all(
        jnp.broadcast_to(value[None], (peers, *value.shape)), axis, 0, 0, tiled=True
    )
    return jnp.sum(everything, axis=0)


def route_kernel(
    ids, dest, buckets, lengths, pool, gain, send, own, info, counts, slot_of, arrived
):
    sampled = ids.shape[0]
    slots = send.shape[0]

    def clear(k, carry):
        arrived[k] = 0
        for s in range(PER_PAIR):
            info[k, s] = 0
            info[k, PER_PAIR + s] = 0
        return carry

    def clear_counts(b, carry):
        counts[b] = 0
        return carry

    lax.fori_loop(0, slots // PER_PAIR, clear, 0)
    lax.fori_loop(0, NB, clear_counts, 0)

    def place(j, carry):
        block = ids[j]
        trainer = dest[j]
        values = pool[block]
        own[j] = values
        order = arrived[trainer]
        arrived[trainer] = order + 1
        slot = trainer * PER_PAIR + order
        send[slot] = values
        slot_of[j] = slot
        bucket = buckets[block]
        length = lengths[block]
        info[trainer, order] = bucket
        info[trainer, PER_PAIR + order] = length
        counts[bucket] = counts[bucket] + length
        return carry

    lax.fori_loop(0, sampled, place, 0)

    def list_free(k, found):
        for s in range(PER_PAIR):
            free = arrived[k] <= s

            @pl.when(free)
            def _():
                slot = k * PER_PAIR + s
                slot_of[sampled + found] = slot
                send[slot] = jnp.zeros(send.shape[1:], send.dtype)

            found = found + jnp.where(free, 1, 0)
        return found

    lax.fori_loop(0, slots // PER_PAIR, list_free, 0)
    whole = gain[...]
    high = whole.astype(jnp.bfloat16).astype(jnp.float32)
    middle = (whole - high).astype(jnp.bfloat16).astype(jnp.float32)
    low = whole - high - middle
    zeros = jnp.zeros((own.shape[1] - 3, whole.shape[1]), jnp.float32)
    own[sampled] = jnp.concatenate([high, middle, low, zeros], axis=0).astype(jnp.bfloat16)
    own[sampled + 1] = jnp.zeros(own.shape[1:], own.dtype)


def route(ids, dest, buckets, lengths, pool, gain, trainers):
    sampled = ids.shape[0]
    slots = trainers * PER_PAIR
    block = pool.shape[1:]
    smem = pl.BlockSpec(memory_space=pltpu.SMEM)
    vmem = pl.BlockSpec(memory_space=pltpu.VMEM)
    return pl.pallas_call(
        route_kernel,
        out_shape=(
            jax.ShapeDtypeStruct((slots, *block), pool.dtype),
            jax.ShapeDtypeStruct((sampled + 2, *block), pool.dtype),
            jax.ShapeDtypeStruct((trainers, 2 * PER_PAIR), jnp.int32),
            jax.ShapeDtypeStruct((NB,), jnp.int32),
            jax.ShapeDtypeStruct((slots,), jnp.int32),
        ),
        in_specs=[smem, smem, smem, smem, vmem, vmem],
        out_specs=(vmem, vmem, smem, smem, smem),
        scratch_shapes=[pltpu.SMEM((trainers,), jnp.int32)],
        compiler_params=pltpu.CompilerParams(vmem_limit_bytes=VMEM_BYTES),
        cost_estimate=pl.CostEstimate(flops=0, bytes_accessed=5 << 20, transcendentals=0),
        name="route",
    )(ids, dest, buckets, lengths, pool, gain[None, :])


def gap_kernel(ids, slot_of, gathered, own, frozen, targets, send, done, normed, gap):
    step = pl.program_id(0)
    parts, _, part = gathered.shape
    sampled, block_len, columns = gap.shape
    rows = sampled * block_len
    width = frozen.shape[1]
    slots = send.shape[0]

    @pl.when(step == 0)
    def _():
        done[0] = 0
        chunk = 128

        def normalize(i, carry):
            at = pl.ds(pl.multiple_of(i * chunk, chunk), chunk)
            total = jnp.zeros((chunk, 1), jnp.float32)
            for p in range(parts):
                x = gathered[p, at, :].astype(jnp.float32)
                total = total + jnp.sum(x * x, axis=1, keepdims=True)
            inverse = lax.rsqrt(total / (parts * part) + RMS_EPSILON)
            for p in range(parts):
                x = gathered[p, at, :].astype(jnp.float32)
                pieces = gathered[p, rows : rows + 16, :].astype(jnp.float32)
                gain = pieces[0:1] + pieces[1:2] + pieces[2:3]
                normed[at, p * part : (p + 1) * part] = (x * inverse * gain).astype(jnp.bfloat16)
            return carry

        lax.fori_loop(0, rows // chunk, normalize, 0)

    projected = jnp.dot(normed[...], frozen[...], preferred_element_type=jnp.float32)
    projected = projected.reshape(sampled, block_len, width)
    at = pl.ds(pl.multiple_of(step * width, width), width)
    gap[:, :, at] = own[:sampled, :, at].astype(jnp.float32) + projected

    @pl.when(step == pl.num_programs(0) - 1)
    def _():
        def place(j, carry):
            target = targets[ids[j]].astype(jnp.float32)
            send[slot_of[j]] = (gap[j] - target).astype(jnp.bfloat16)
            return carry

        lax.fori_loop(0, sampled, place, 0)

        def fill(s, carry):
            send[slot_of[sampled + s]] = jnp.zeros((block_len, columns), jnp.bfloat16)
            return carry

        lax.fori_loop(0, slots - sampled, fill, 0)


def base_gap_slots(ids, slot_of, gathered, own, frozen, targets):
    parts, _, part = gathered.shape
    width, columns = frozen.shape
    slots = slot_of.shape[0]
    sampled = ids.shape[0]
    block_len = own.shape[1]
    rows = sampled * block_len
    tile = 256
    smem = pl.BlockSpec(memory_space=pltpu.SMEM)
    return pl.pallas_call(
        gap_kernel,
        grid=(columns // tile,),
        out_shape=(
            jax.ShapeDtypeStruct((slots, *own.shape[1:]), jnp.bfloat16),
            jax.ShapeDtypeStruct((1,), jnp.int32),
        ),
        in_specs=[
            smem,
            smem,
            pl.BlockSpec(gathered.shape, lambda n: (0, 0, 0)),
            pl.BlockSpec(own.shape, lambda n: (0, 0, 0)),
            pl.BlockSpec((width, tile), lambda n: (0, n)),
            pl.BlockSpec(targets.shape, lambda n: (0, 0, 0)),
        ],
        out_specs=(pl.BlockSpec((slots, *own.shape[1:]), lambda n: (0, 0, 0)), smem),
        scratch_shapes=[
            pltpu.VMEM((rows, width), jnp.bfloat16),
            pltpu.VMEM((sampled, block_len, columns), jnp.float32),
        ],
        compiler_params=pltpu.CompilerParams(vmem_limit_bytes=VMEM_BYTES),
        cost_estimate=pl.CostEstimate(
            flops=2 * rows * width * columns, bytes_accessed=18 << 20, transcendentals=rows
        ),
        name="base_gap",
    )(ids, slot_of, gathered, own, frozen, targets)


def trainer_kernel(gap, lowered, up, facts, grad_up, back, loss):
    step = pl.program_id(0)
    low = lowered[...]
    up_map = up[...]
    facts_now = facts[...]
    distance = gap[...].astype(jnp.float32) + lax.dot_general(
        low, up_map, CONTRACT_FIRST, preferred_element_type=jnp.float32
    )
    output_grad = (facts_now[:, NB : NB + 1] * distance).astype(jnp.bfloat16)
    squares = jnp.sum(distance * distance, axis=1, keepdims=True)
    part = jnp.sum(facts_now * squares, axis=0, keepdims=True)
    back[...] = lax.dot_general(
        up_map, output_grad, CONTRACT_LAST, preferred_element_type=jnp.float32
    )
    own = jnp.dot(low, output_grad, preferred_element_type=jnp.float32)

    @pl.when(step == 0)
    def _():
        grad_up[...] = own
        loss[...] = part

    @pl.when(step > 0)
    def _():
        grad_up[...] += own
        loss[...] += part


def trainer_step(gap, lowered, up, facts):
    rows, columns = gap.shape
    rank = up.shape[0]
    lanes = facts.shape[1]
    chunk = 256
    return pl.pallas_call(
        trainer_kernel,
        grid=(rows // chunk,),
        out_shape=(
            jax.ShapeDtypeStruct((rank, columns), jnp.float32),
            jax.ShapeDtypeStruct((rank, rows), jnp.float32),
            jax.ShapeDtypeStruct((1, lanes), jnp.float32),
        ),
        in_specs=[
            pl.BlockSpec((chunk, columns), lambda i: (i, 0)),
            pl.BlockSpec((rank, chunk), lambda i: (0, i)),
            pl.BlockSpec((rank, columns), lambda i: (0, 0)),
            pl.BlockSpec((chunk, lanes), lambda i: (i, 0)),
        ],
        out_specs=(
            pl.BlockSpec((rank, columns), lambda i: (0, 0)),
            pl.BlockSpec((rank, chunk), lambda i: (0, i)),
            pl.BlockSpec((1, lanes), lambda i: (0, 0)),
        ),
        compiler_params=pltpu.CompilerParams(vmem_limit_bytes=VMEM_BYTES),
        cost_estimate=pl.CostEstimate(
            flops=6 * rows * rank * columns, bytes_accessed=4 << 20, transcendentals=0
        ),
        name="trainer_step",
    )(gap, lowered, up, facts)


def on_device(
    pool_inputs,
    pool_targets,
    frozen,
    gain,
    adapter_down,
    adapter_up,
    sample_ids,
    buckets,
    lengths,
    destinations,
    competence,
):
    trainers = lax.axis_size(DP)
    parts = lax.axis_size("mp")
    sampled = sample_ids.shape[0]
    _, block_len, part = pool_inputs.shape
    width = frozen.shape[0]
    slots = trainers * PER_PAIR
    rows = slots * block_len
    per_peer = PER_PAIR * block_len
    down_map = adapter_down[0]
    up_map = adapter_up[0]
    bucket_range = jnp.arange(NB, dtype=jnp.int32)

    send_x, own_x, info, counts, slot_of = route(
        sample_ids, destinations[:, 0], buckets, lengths, pool_inputs, gain, trainers
    )
    got_x = lax.all_to_all(
        send_x.reshape(trainers, per_peer, part), DP, 0, 0, tiled=True
    )
    gathered = lax.all_gather(own_x.reshape(-1, part), "mp")
    message = jnp.concatenate(
        [info, jnp.broadcast_to(counts[None, :], (trainers, NB))], axis=1
    )
    got_info = lax.all_to_all(message[:, None, :], DP, 0, 0, tiled=True)[:, 0, :]

    send_gap, done = base_gap_slots(sample_ids, slot_of, gathered, own_x, frozen, pool_targets)
    got_gap = lax.all_to_all(
        send_gap.reshape(trainers, per_peer, part), DP, 0, 0, tiled=True
    )

    floor_counts = jnp.maximum(
        jnp.sum(got_info[:, 2 * PER_PAIR :], axis=0).astype(jnp.float32), 1.0
    )
    weights = jax.nn.sigmoid(
        SHARPNESS * (competence[0] - (bucket_range.astype(jnp.float32) + 0.5) / NB)
    )
    row_bucket = jnp.repeat(got_info[:, :PER_PAIR].reshape(slots), block_len)
    row_length = jnp.repeat(got_info[:, PER_PAIR : 2 * PER_PAIR].reshape(slots), block_len)
    live = (jnp.arange(rows, dtype=jnp.int32) % block_len < row_length).astype(jnp.float32)
    onehot = (row_bucket[:, None] == bucket_range[None, :]).astype(jnp.float32) * live[:, None]
    coefficient = 2.0 * jnp.sum(onehot * (weights / floor_counts)[None, :], axis=1)
    facts = jnp.concatenate(
        [onehot, coefficient[:, None], jnp.zeros((rows, 128 - NB - 1), jnp.float32)], axis=1
    )

    got_x, done = lax.optimization_barrier((got_x, done))
    values = got_x.reshape(rows, part).astype(jnp.float32)
    square_total = of_everyone(jnp.sum(values * values, axis=1), "mp")
    inverse_rms = lax.rsqrt(square_total / width + RMS_EPSILON)
    normed = (values * inverse_rms[:, None] * gain[None, :]).astype(jnp.bfloat16)
    latent_part = lax.dot_general(
        down_map, normed, CONTRACT_LAST, preferred_element_type=jnp.float32
    )
    lowered = (ADAPTER_SCALING * of_everyone(latent_part, "mp")).astype(jnp.bfloat16)

    grad_up, back_part, loss_part = trainer_step(
        got_gap.reshape(rows, part), lowered, up_map, facts
    )
    loss_sum = of_everyone(loss_part[:, :NB], DP_MP)[0]
    lowered_gradient = (ADAPTER_SCALING * of_everyone(back_part, "mp")).astype(jnp.bfloat16)
    grad_down = jnp.dot(lowered_gradient, normed, preferred_element_type=jnp.float32)
    bucket_loss = loss_sum / (floor_counts * width)
    progress = jnp.sum(weights * bucket_loss) / jnp.sum(bucket_loss)
    competence_next = competence + 0.5 * (1.0 - competence) * progress
    return (grad_down[None], grad_up[None], bucket_loss, competence_next)


def solution(mesh):
    split = Mesh(mesh.devices.reshape(4, 8, 2, mesh.shape["mp"]), DP_MP)
    placed = (
        P(DP, None, "mp"),
        P(DP, None, "mp"),
        P(None, "mp"),
        P("mp"),
        P(DP, None, "mp"),
        P(DP, None, "mp"),
        P(DP),
        P(DP),
        P(DP),
        P(DP, None),
        P(),
    )
    return jax.shard_map(
        on_device,
        mesh=split,
        in_specs=placed,
        out_specs=(P(DP, None, "mp"), P(DP, None, "mp"), P(), P()),
        check_vma=False,
    )
```

```python
import jax
import jax.numpy as jnp
from jax import lax
from jax.experimental import pallas as pl
from jax.experimental.pallas import tpu as pltpu
from jax.sharding import Mesh
from jax.sharding import PartitionSpec as P

NB = 16
DP = ("dp_0", "dp_1", "dp_2")
DP_MP = ("dp_0", "dp_1", "dp_2", "mp")

RMS_EPSILON = 1e-05
SHARPNESS = 12.0
ADAPTER_SCALING = 2.0
PER_PAIR = 2
VMEM_BYTES = 48 * 1024 * 1024
CONTRACT_LAST = (((1,), (1,)), ((), ()))
CONTRACT_FIRST = (((0,), (0,)), ((), ()))


def of_everyone(value, axis):
    peers = lax.axis_size(axis)
    everything = lax.all_to_all(
        jnp.broadcast_to(value[None], (peers, *value.shape)), axis, 0, 0, tiled=True
    )
    return jnp.sum(everything, axis=0)


def route_kernel(
    ids_in, dest_in, buckets_in, lengths_in, pool_in, gain_in,
    send_out, own_out, info, counts, slot_of,
    ids, dest, buckets, lengths, pool, gain, send, own, arrived, sem,
):
    pairs = (
        (pool_in, pool),
        (ids_in, ids),
        (dest_in, dest),
        (buckets_in, buckets),
        (lengths_in, lengths),
        (gain_in, gain),
    )
    copies = [
        pltpu.make_async_copy(source, target, sem.at[i])
        for i, (source, target) in enumerate(pairs)
    ]
    for copy in copies:
        copy.start()
    sampled = ids.shape[0]
    slots = send.shape[0]

    def clear(k, carry):
        arrived[k] = 0
        for s in range(PER_PAIR):
            info[k, s] = 0
            info[k, PER_PAIR + s] = 0
        return carry

    def clear_counts(b, carry):
        counts[b] = 0
        return carry

    lax.fori_loop(0, slots // PER_PAIR, clear, 0)
    lax.fori_loop(0, NB, clear_counts, 0)
    for copy in copies:
        copy.wait()

    def place(j, carry):
        block = ids[j]
        trainer = dest[j]
        values = pool[block]
        own[j] = values
        order = arrived[trainer]
        arrived[trainer] = order + 1
        slot = trainer * PER_PAIR + order
        send[slot] = values
        slot_of[j] = slot
        bucket = buckets[block]
        length = lengths[block]
        info[trainer, order] = bucket
        info[trainer, PER_PAIR + order] = length
        counts[bucket] = counts[bucket] + length
        return carry

    lax.fori_loop(0, sampled, place, 0)

    def list_free(k, found):
        for s in range(PER_PAIR):
            free = arrived[k] <= s

            @pl.when(free)
            def _():
                slot = k * PER_PAIR + s
                slot_of[sampled + found] = slot
                send[slot] = jnp.zeros(send.shape[1:], send.dtype)

            found = found + jnp.where(free, 1, 0)
        return found

    lax.fori_loop(0, slots // PER_PAIR, list_free, 0)
    send_copy = pltpu.make_async_copy(send, send_out, sem.at[0])
    send_copy.start()
    whole = gain[...]
    high = whole.astype(jnp.bfloat16).astype(jnp.float32)
    middle = (whole - high).astype(jnp.bfloat16).astype(jnp.float32)
    low = whole - high - middle
    zeros = jnp.zeros((own.shape[1] - 3, whole.shape[1]), jnp.float32)
    own[sampled] = jnp.concatenate([high, middle, low, zeros], axis=0).astype(jnp.bfloat16)
    own[sampled + 1] = jnp.zeros(own.shape[1:], own.dtype)
    own_copy = pltpu.make_async_copy(own, own_out, sem.at[1])
    own_copy.start()
    own_copy.wait()
    send_copy.wait()


def route(ids, dest, buckets, lengths, pool, gain, trainers):
    sampled = ids.shape[0]
    slots = trainers * PER_PAIR
    block = pool.shape[1:]
    smem = pl.BlockSpec(memory_space=pltpu.SMEM)
    hbm = pl.BlockSpec(memory_space=pltpu.HBM)
    return pl.pallas_call(
        route_kernel,
        out_shape=(
            jax.ShapeDtypeStruct((slots, *block), pool.dtype),
            jax.ShapeDtypeStruct((sampled + 2, *block), pool.dtype),
            jax.ShapeDtypeStruct((trainers, 2 * PER_PAIR), jnp.int32),
            jax.ShapeDtypeStruct((NB,), jnp.int32),
            jax.ShapeDtypeStruct((slots,), jnp.int32),
        ),
        in_specs=[hbm] * 6,
        out_specs=(hbm, hbm, smem, smem, smem),
        scratch_shapes=[
            pltpu.SMEM(ids.shape, jnp.int32),
            pltpu.SMEM(dest.shape, jnp.int32),
            pltpu.SMEM(buckets.shape, jnp.int32),
            pltpu.SMEM(lengths.shape, jnp.int32),
            pltpu.VMEM(pool.shape, pool.dtype),
            pltpu.VMEM((1, gain.shape[0]), jnp.float32),
            pltpu.VMEM((slots, *block), pool.dtype),
            pltpu.VMEM((sampled + 2, *block), pool.dtype),
            pltpu.SMEM((trainers,), jnp.int32),
            pltpu.SemaphoreType.DMA((6,)),
        ],
        compiler_params=pltpu.CompilerParams(vmem_limit_bytes=VMEM_BYTES),
        cost_estimate=pl.CostEstimate(flops=0, bytes_accessed=5 << 20, transcendentals=0),
        name="route",
    )(ids, dest, buckets, lengths, pool, gain[None, :])


def gap_kernel(ids, slot_of, gathered, own, frozen, targets, send_out, done, send, normed, gap, sem):
    step = pl.program_id(0)
    parts, _, part = gathered.shape
    sampled, block_len, columns = gap.shape
    rows = sampled * block_len
    width = frozen.shape[1]
    slots = send.shape[0]

    @pl.when(step == 0)
    def _():
        done[0] = 0.0
        chunk = 128

        def normalize(i, carry):
            at = pl.ds(pl.multiple_of(i * chunk, chunk), chunk)
            total = jnp.zeros((chunk, 1), jnp.float32)
            for p in range(parts):
                x = gathered[p, at, :].astype(jnp.float32)
                total = total + jnp.sum(x * x, axis=1, keepdims=True)
            inverse = lax.rsqrt(total / (parts * part) + RMS_EPSILON)
            for p in range(parts):
                x = gathered[p, at, :].astype(jnp.float32)
                pieces = gathered[p, rows : rows + 16, :].astype(jnp.float32)
                gain = pieces[0:1] + pieces[1:2] + pieces[2:3]
                normed[at, p * part : (p + 1) * part] = (x * inverse * gain).astype(jnp.bfloat16)
            return carry

        lax.fori_loop(0, rows // chunk, normalize, 0)

    projected = jnp.dot(normed[...], frozen[...], preferred_element_type=jnp.float32)
    projected = projected.reshape(sampled, block_len, width)
    at = pl.ds(pl.multiple_of(step * width, width), width)
    gap[:, :, at] = own[:sampled, :, at].astype(jnp.float32) + projected

    @pl.when(step == pl.num_programs(0) - 1)
    def _():
        def place(j, carry):
            target = targets[ids[j]].astype(jnp.float32)
            send[slot_of[j]] = (gap[j] - target).astype(jnp.bfloat16)
            return carry

        lax.fori_loop(0, sampled, place, 0)

        def fill(s, carry):
            send[slot_of[sampled + s]] = jnp.zeros((block_len, columns), jnp.bfloat16)
            return carry

        lax.fori_loop(0, slots - sampled, fill, 0)
        copy = pltpu.make_async_copy(send, send_out, sem.at[0])
        copy.start()
        copy.wait()


def base_gap_slots(ids, slot_of, gathered, own, frozen, targets):
    parts, _, part = gathered.shape
    width, columns = frozen.shape
    slots = slot_of.shape[0]
    sampled = ids.shape[0]
    block_len = own.shape[1]
    rows = sampled * block_len
    tile = 256
    smem = pl.BlockSpec(memory_space=pltpu.SMEM)
    return pl.pallas_call(
        gap_kernel,
        grid=(columns // tile,),
        out_shape=(
            jax.ShapeDtypeStruct((slots, *own.shape[1:]), jnp.bfloat16),
            jax.ShapeDtypeStruct((1,), jnp.float32),
        ),
        in_specs=[
            smem,
            smem,
            pl.BlockSpec(gathered.shape, lambda n: (0, 0, 0)),
            pl.BlockSpec(own.shape, lambda n: (0, 0, 0)),
            pl.BlockSpec((width, tile), lambda n: (0, n)),
            pl.BlockSpec(targets.shape, lambda n: (0, 0, 0)),
        ],
        out_specs=(pl.BlockSpec(memory_space=pltpu.HBM), smem),
        scratch_shapes=[
            pltpu.VMEM((slots, *own.shape[1:]), jnp.bfloat16),
            pltpu.VMEM((rows, width), jnp.bfloat16),
            pltpu.VMEM((sampled, block_len, columns), jnp.float32),
            pltpu.SemaphoreType.DMA((1,)),
        ],
        compiler_params=pltpu.CompilerParams(vmem_limit_bytes=VMEM_BYTES),
        cost_estimate=pl.CostEstimate(
            flops=2 * rows * width * columns, bytes_accessed=18 << 20, transcendentals=rows
        ),
        name="base_gap",
    )(ids, slot_of, gathered, own, frozen, targets)


def trainer_kernel(gap, lowered, up, facts, grad_up, back_out, loss_out, back, loss, sem):
    step = pl.program_id(0)
    chunk = gap.shape[0]
    low = lowered[...]
    up_map = up[...]
    facts_now = facts[...]
    distance = gap[...].astype(jnp.float32) + lax.dot_general(
        low, up_map, CONTRACT_FIRST, preferred_element_type=jnp.float32
    )
    output_grad = (facts_now[:, NB : NB + 1] * distance).astype(jnp.bfloat16)
    squares = jnp.sum(distance * distance, axis=1, keepdims=True)
    part = jnp.sum(facts_now * squares, axis=0, keepdims=True)
    back_now = lax.dot_general(
        up_map, output_grad, CONTRACT_LAST, preferred_element_type=jnp.float32
    )
    at = pl.ds(pl.multiple_of(step * chunk, chunk), chunk)
    for p in range(back.shape[0]):
        back[p, :, at] = back_now
    own = jnp.dot(low, output_grad, preferred_element_type=jnp.float32)

    @pl.when(step == 0)
    def _():
        grad_up[...] = own
        loss[...] = jnp.broadcast_to(part[None], loss.shape)

    @pl.when(step > 0)
    def _():
        grad_up[...] += own
        loss[...] += part[None]

    @pl.when(step == pl.num_programs(0) - 1)
    def _():
        copies = (
            pltpu.make_async_copy(loss, loss_out, sem.at[0]),
            pltpu.make_async_copy(back, back_out, sem.at[1]),
        )
        for copy in copies:
            copy.start()
        for copy in copies:
            copy.wait()


def trainer_step(gap, lowered, up, facts, trainers, parts):
    rows, columns = gap.shape
    rank = up.shape[0]
    lanes = facts.shape[1]
    chunk = 256
    hbm = pl.BlockSpec(memory_space=pltpu.HBM)
    return pl.pallas_call(
        trainer_kernel,
        grid=(rows // chunk,),
        out_shape=(
            jax.ShapeDtypeStruct((rank, columns), jnp.float32),
            jax.ShapeDtypeStruct((parts, rank, rows), jnp.float32),
            jax.ShapeDtypeStruct((trainers, 1, lanes), jnp.float32),
        ),
        in_specs=[
            pl.BlockSpec((chunk, columns), lambda i: (i, 0)),
            pl.BlockSpec((rank, chunk), lambda i: (0, i)),
            pl.BlockSpec((rank, columns), lambda i: (0, 0)),
            pl.BlockSpec((chunk, lanes), lambda i: (i, 0)),
        ],
        out_specs=(pl.BlockSpec((rank, columns), lambda i: (0, 0)), hbm, hbm),
        scratch_shapes=[
            pltpu.VMEM((parts, rank, rows), jnp.float32),
            pltpu.VMEM((trainers, 1, lanes), jnp.float32),
            pltpu.SemaphoreType.DMA((2,)),
        ],
        compiler_params=pltpu.CompilerParams(vmem_limit_bytes=VMEM_BYTES),
        cost_estimate=pl.CostEstimate(
            flops=6 * rows * rank * columns, bytes_accessed=4 << 20, transcendentals=0
        ),
        name="trainer_step",
    )(gap, lowered, up, facts)


def on_device(
    pool_inputs,
    pool_targets,
    frozen,
    gain,
    adapter_down,
    adapter_up,
    sample_ids,
    buckets,
    lengths,
    destinations,
    competence,
):
    trainers = lax.axis_size(DP)
    parts = lax.axis_size("mp")
    sampled = sample_ids.shape[0]
    _, block_len, part = pool_inputs.shape
    width = frozen.shape[0]
    slots = trainers * PER_PAIR
    rows = slots * block_len
    per_peer = PER_PAIR * block_len
    down_map = adapter_down[0]
    up_map = adapter_up[0]
    bucket_range = jnp.arange(NB, dtype=jnp.int32)

    send_x, own_x, info, counts, slot_of = route(
        sample_ids, destinations[:, 0], buckets, lengths, pool_inputs, gain, trainers
    )
    got_x = lax.all_to_all(
        send_x.reshape(trainers, per_peer, part), DP, 0, 0, tiled=True
    )
    gathered = lax.all_gather(own_x.reshape(-1, part), "mp")
    message = jnp.concatenate(
        [info, jnp.broadcast_to(counts[None, :], (trainers, NB))], axis=1
    )
    got_info = lax.all_to_all(message[:, None, :], DP, 0, 0, tiled=True)[:, 0, :]

    send_gap, done = base_gap_slots(sample_ids, slot_of, gathered, own_x, frozen, pool_targets)
    got_gap = lax.all_to_all(
        send_gap.reshape(trainers, per_peer, part), DP, 0, 0, tiled=True
    )

    floor_counts = jnp.maximum(
        jnp.sum(got_info[:, 2 * PER_PAIR :], axis=0).astype(jnp.float32), 1.0
    )
    weights = jax.nn.sigmoid(
        SHARPNESS * (competence[0] - (bucket_range.astype(jnp.float32) + 0.5) / NB)
    )
    row_bucket = jnp.repeat(got_info[:, :PER_PAIR].reshape(slots), block_len)
    row_length = jnp.repeat(got_info[:, PER_PAIR : 2 * PER_PAIR].reshape(slots), block_len)
    live = (jnp.arange(rows, dtype=jnp.int32) % block_len < row_length).astype(jnp.float32)
    onehot = (row_bucket[:, None] == bucket_range[None, :]).astype(jnp.float32) * live[:, None]
    coefficient = 2.0 * jnp.sum(onehot * (weights / floor_counts)[None, :], axis=1)
    facts = jnp.concatenate(
        [onehot, coefficient[:, None], jnp.zeros((rows, 128 - NB - 1), jnp.float32)], axis=1
    )

    values = got_x.reshape(rows, part).astype(jnp.float32)
    square_total = of_everyone(jnp.sum(values * values, axis=1) + done, "mp")
    inverse_rms = lax.rsqrt(square_total / width + RMS_EPSILON)
    normed = (values * inverse_rms[:, None] * gain[None, :]).astype(jnp.bfloat16)
    latent_part = lax.dot_general(
        down_map, normed, CONTRACT_LAST, preferred_element_type=jnp.float32
    )
    lowered = (ADAPTER_SCALING * of_everyone(latent_part, "mp")).astype(jnp.bfloat16)

    grad_up, back_part, loss_part = trainer_step(
        got_gap.reshape(rows, part), lowered, up_map, facts, trainers, parts
    )
    loss_over_dp = jnp.sum(lax.all_to_all(loss_part, DP, 0, 0, tiled=True), axis=0)
    back = jnp.sum(lax.all_to_all(back_part, "mp", 0, 0, tiled=True), axis=0)
    loss_sum = of_everyone(loss_over_dp, "mp")[0, :NB]
    lowered_gradient = (ADAPTER_SCALING * back).astype(jnp.bfloat16)
    grad_down = jnp.dot(lowered_gradient, normed, preferred_element_type=jnp.float32)
    bucket_loss = loss_sum / (floor_counts * width)
    progress = jnp.sum(weights * bucket_loss) / jnp.sum(bucket_loss)
    competence_next = competence + 0.5 * (1.0 - competence) * progress
    return (grad_down[None], grad_up[None], bucket_loss, competence_next)


def solution(mesh):
    split = Mesh(mesh.devices.reshape(4, 8, 2, mesh.shape["mp"]), DP_MP)
    placed = (
        P(DP, None, "mp"),
        P(DP, None, "mp"),
        P(None, "mp"),
        P("mp"),
        P(DP, None, "mp"),
        P(DP, None, "mp"),
        P(DP),
        P(DP),
        P(DP),
        P(DP, None),
        P(),
    )
    return jax.shard_map(
        on_device,
        mesh=split,
        in_specs=placed,
        out_specs=(P(DP, None, "mp"), P(DP, None, "mp"), P(), P()),
        check_vma=False,
    )
```

```python
import jax
import jax.numpy as jnp
from jax import lax
from jax.experimental import pallas as pl
from jax.experimental.pallas import tpu as pltpu
from jax.sharding import Mesh
from jax.sharding import PartitionSpec as P

NB = 16
DP = ("dp_0", "dp_1", "dp_2")
DP_MP = ("dp_0", "dp_1", "dp_2", "mp")

RMS_EPSILON = 1e-05
SHARPNESS = 12.0
ADAPTER_SCALING = 2.0
PER_PAIR = 2
VMEM_BYTES = 62 * 1024 * 1024
CONTRACT_LAST = (((1,), (1,)), ((), ()))
CONTRACT_FIRST = (((0,), (0,)), ((), ()))


def over_parts(value, axis):
    peers = lax.axis_size(axis)
    others = [
        lax.ppermute(value, axis, [(i, i ^ distance) for i in range(peers)])
        for distance in range(1, peers)
    ]
    return (value + others[0]) + (others[1] + others[2])


def square_kernel(values, done, total):
    lanes = 128
    sums = jnp.zeros((values.shape[0], lanes), jnp.float32)
    for g in range(values.shape[1] // lanes):
        x = values[:, g * lanes : (g + 1) * lanes].astype(jnp.float32)
        sums = sums + x * x
    total[...] = jnp.sum(sums.T, axis=0, keepdims=True) + done[0]


def row_squares(values, done):
    rows, columns = values.shape
    chunk = 256
    return pl.pallas_call(
        square_kernel,
        grid=(rows // chunk,),
        out_shape=jax.ShapeDtypeStruct((1, rows), jnp.float32),
        in_specs=[
            pl.BlockSpec((chunk, columns), lambda i: (i, 0)),
            pl.BlockSpec(memory_space=pltpu.SMEM),
        ],
        out_specs=pl.BlockSpec((1, chunk), lambda i: (0, i)),
        compiler_params=pltpu.CompilerParams(vmem_limit_bytes=VMEM_BYTES),
        cost_estimate=pl.CostEstimate(
            flops=2 * rows * columns, bytes_accessed=2 << 20, transcendentals=0
        ),
        name="row_squares",
    )(values, done)


def route_kernel(
    ids_in, dest_in, buckets_in, lengths_in, pool_in, gain_in,
    send_out, own_out, info, counts, slot_of,
    ids, dest, buckets, lengths, pool, gain, send, own, arrived, sem,
):
    pairs = (
        (pool_in, pool),
        (ids_in, ids),
        (dest_in, dest),
        (buckets_in, buckets),
        (lengths_in, lengths),
        (gain_in, gain),
    )
    copies = [
        pltpu.make_async_copy(source, target, sem.at[i])
        for i, (source, target) in enumerate(pairs)
    ]
    for copy in copies:
        copy.start()
    sampled = ids.shape[0]
    slots = send.shape[0]

    def clear(k, carry):
        arrived[k] = 0
        for s in range(PER_PAIR):
            info[k, s] = 0
            info[k, PER_PAIR + s] = 0
        return carry

    def clear_counts(b, carry):
        counts[b] = 0
        return carry

    lax.fori_loop(0, slots // PER_PAIR, clear, 0)
    lax.fori_loop(0, NB, clear_counts, 0)
    for copy in copies:
        copy.wait()

    def place(j, carry):
        block = ids[j]
        trainer = dest[j]
        values = pool[block]
        own[j] = values
        order = arrived[trainer]
        arrived[trainer] = order + 1
        slot = trainer * PER_PAIR + order
        send[slot] = values
        slot_of[j] = slot
        bucket = buckets[block]
        length = lengths[block]
        info[trainer, order] = bucket
        info[trainer, PER_PAIR + order] = length
        counts[bucket] = counts[bucket] + length
        return carry

    lax.fori_loop(0, sampled, place, 0)

    def list_free(k, found):
        for s in range(PER_PAIR):
            free = arrived[k] <= s

            @pl.when(free)
            def _():
                slot = k * PER_PAIR + s
                slot_of[sampled + found] = slot
                send[slot] = jnp.zeros(send.shape[1:], send.dtype)

            found = found + jnp.where(free, 1, 0)
        return found

    lax.fori_loop(0, slots // PER_PAIR, list_free, 0)
    send_copy = pltpu.make_async_copy(send, send_out, sem.at[0])
    send_copy.start()
    whole = gain[...]
    high = whole.astype(jnp.bfloat16).astype(jnp.float32)
    middle = (whole - high).astype(jnp.bfloat16).astype(jnp.float32)
    low = whole - high - middle
    zeros = jnp.zeros((own.shape[1] - 3, whole.shape[1]), jnp.float32)
    own[sampled] = jnp.concatenate([high, middle, low, zeros], axis=0).astype(jnp.bfloat16)
    own[sampled + 1] = jnp.zeros(own.shape[1:], own.dtype)
    own_copy = pltpu.make_async_copy(own, own_out, sem.at[1])
    own_copy.start()
    own_copy.wait()
    send_copy.wait()


def route(ids, dest, buckets, lengths, pool, gain, trainers):
    sampled = ids.shape[0]
    slots = trainers * PER_PAIR
    block = pool.shape[1:]
    smem = pl.BlockSpec(memory_space=pltpu.SMEM)
    hbm = pl.BlockSpec(memory_space=pltpu.HBM)
    return pl.pallas_call(
        route_kernel,
        out_shape=(
            jax.ShapeDtypeStruct((slots, *block), pool.dtype),
            jax.ShapeDtypeStruct((sampled + 2, *block), pool.dtype),
            jax.ShapeDtypeStruct((trainers, 2 * PER_PAIR), jnp.int32),
            jax.ShapeDtypeStruct((NB,), jnp.int32),
            jax.ShapeDtypeStruct((slots,), jnp.int32),
        ),
        in_specs=[hbm] * 6,
        out_specs=(hbm, hbm, smem, smem, smem),
        scratch_shapes=[
            pltpu.SMEM(ids.shape, jnp.int32),
            pltpu.SMEM(dest.shape, jnp.int32),
            pltpu.SMEM(buckets.shape, jnp.int32),
            pltpu.SMEM(lengths.shape, jnp.int32),
            pltpu.VMEM(pool.shape, pool.dtype),
            pltpu.VMEM((1, gain.shape[0]), jnp.float32),
            pltpu.VMEM((slots, *block), pool.dtype),
            pltpu.VMEM((sampled + 2, *block), pool.dtype),
            pltpu.SMEM((trainers,), jnp.int32),
            pltpu.SemaphoreType.DMA((6,)),
        ],
        compiler_params=pltpu.CompilerParams(vmem_limit_bytes=VMEM_BYTES),
        cost_estimate=pl.CostEstimate(flops=0, bytes_accessed=5 << 20, transcendentals=0),
        name="route",
    )(ids, dest, buckets, lengths, pool, gain[None, :])


def gap_kernel(ids, slot_of, gathered, own, frozen, targets, send_out, done, send, normed, gap, sem):
    step = pl.program_id(0)
    parts, _, part = gathered.shape
    sampled, block_len, columns = gap.shape
    rows = sampled * block_len
    width = frozen.shape[1]
    slots = send.shape[0]

    @pl.when(step == 0)
    def _():
        done[0] = 0.0
        chunk = 128

        def normalize(i, carry):
            at = pl.ds(pl.multiple_of(i * chunk, chunk), chunk)
            total = jnp.zeros((chunk, 1), jnp.float32)
            for p in range(parts):
                x = gathered[p, at, :].astype(jnp.float32)
                total = total + jnp.sum(x * x, axis=1, keepdims=True)
            inverse = lax.rsqrt(total / (parts * part) + RMS_EPSILON)
            for p in range(parts):
                x = gathered[p, at, :].astype(jnp.float32)
                pieces = gathered[p, rows : rows + 16, :].astype(jnp.float32)
                gain = pieces[0:1] + pieces[1:2] + pieces[2:3]
                normed[at, p * part : (p + 1) * part] = (x * inverse * gain).astype(jnp.bfloat16)
            return carry

        lax.fori_loop(0, rows // chunk, normalize, 0)

    projected = jnp.dot(normed[...], frozen[...], preferred_element_type=jnp.float32)
    projected = projected.reshape(sampled, block_len, width)
    at = pl.ds(pl.multiple_of(step * width, width), width)
    gap[:, :, at] = own[:sampled, :, at].astype(jnp.float32) + projected

    @pl.when(step == pl.num_programs(0) - 1)
    def _():
        def place(j, carry):
            target = targets[ids[j]].astype(jnp.float32)
            send[slot_of[j]] = (gap[j] - target).astype(jnp.bfloat16)
            return carry

        lax.fori_loop(0, sampled, place, 0)

        def fill(s, carry):
            send[slot_of[sampled + s]] = jnp.zeros((block_len, columns), jnp.bfloat16)
            return carry

        lax.fori_loop(0, slots - sampled, fill, 0)
        copy = pltpu.make_async_copy(send, send_out, sem.at[0])
        copy.start()
        copy.wait()


def base_gap_slots(ids, slot_of, gathered, own, frozen, targets):
    parts, _, part = gathered.shape
    width, columns = frozen.shape
    slots = slot_of.shape[0]
    sampled = ids.shape[0]
    block_len = own.shape[1]
    rows = sampled * block_len
    tile = 256
    smem = pl.BlockSpec(memory_space=pltpu.SMEM)
    return pl.pallas_call(
        gap_kernel,
        grid=(columns // tile,),
        out_shape=(
            jax.ShapeDtypeStruct((slots, *own.shape[1:]), jnp.bfloat16),
            jax.ShapeDtypeStruct((1,), jnp.float32),
        ),
        in_specs=[
            smem,
            smem,
            pl.BlockSpec(gathered.shape, lambda n: (0, 0, 0)),
            pl.BlockSpec(own.shape, lambda n: (0, 0, 0)),
            pl.BlockSpec((width, tile), lambda n: (0, n)),
            pl.BlockSpec(targets.shape, lambda n: (0, 0, 0)),
        ],
        out_specs=(pl.BlockSpec(memory_space=pltpu.HBM), smem),
        scratch_shapes=[
            pltpu.VMEM((slots, *own.shape[1:]), jnp.bfloat16),
            pltpu.VMEM((rows, width), jnp.bfloat16),
            pltpu.VMEM((sampled, block_len, columns), jnp.float32),
            pltpu.SemaphoreType.DMA((1,)),
        ],
        compiler_params=pltpu.CompilerParams(vmem_limit_bytes=VMEM_BYTES),
        cost_estimate=pl.CostEstimate(
            flops=2 * rows * width * columns, bytes_accessed=18 << 20, transcendentals=rows
        ),
        name="base_gap",
    )(ids, slot_of, gathered, own, frozen, targets)


def trainer_kernel(gap, lowered, up, facts, grad_up, back, loss_out, loss, sem):
    step = pl.program_id(0)
    low = lowered[...]
    up_map = up[...]
    facts_now = facts[...]
    distance = gap[...].astype(jnp.float32) + lax.dot_general(
        low, up_map, CONTRACT_FIRST, preferred_element_type=jnp.float32
    )
    output_grad = (facts_now[:, NB : NB + 1] * distance).astype(jnp.bfloat16)
    squares = jnp.sum(distance * distance, axis=1, keepdims=True)
    part = jnp.sum(facts_now * squares, axis=0, keepdims=True)
    back[...] = lax.dot_general(
        up_map, output_grad, CONTRACT_LAST, preferred_element_type=jnp.float32
    )
    own = jnp.dot(low, output_grad, preferred_element_type=jnp.float32)

    @pl.when(step == 0)
    def _():
        grad_up[...] = own
        loss[...] = jnp.broadcast_to(part[None], loss.shape)

    @pl.when(step > 0)
    def _():
        grad_up[...] += own
        loss[...] += part[None]

    @pl.when(step == pl.num_programs(0) - 1)
    def _():
        copy = pltpu.make_async_copy(loss, loss_out, sem.at[0])
        copy.start()
        copy.wait()


def trainer_step(gap, lowered, up, facts, trainers):
    rows, columns = gap.shape
    rank = up.shape[0]
    lanes = facts.shape[1]
    chunk = 256
    return pl.pallas_call(
        trainer_kernel,
        grid=(rows // chunk,),
        out_shape=(
            jax.ShapeDtypeStruct((rank, columns), jnp.float32),
            jax.ShapeDtypeStruct((rank, rows), jnp.float32),
            jax.ShapeDtypeStruct((trainers, 1, lanes), jnp.float32),
        ),
        in_specs=[
            pl.BlockSpec((chunk, columns), lambda i: (i, 0)),
            pl.BlockSpec((rank, chunk), lambda i: (0, i)),
            pl.BlockSpec((rank, columns), lambda i: (0, 0)),
            pl.BlockSpec((chunk, lanes), lambda i: (i, 0)),
        ],
        out_specs=(
            pl.BlockSpec((rank, columns), lambda i: (0, 0)),
            pl.BlockSpec((rank, chunk), lambda i: (0, i)),
            pl.BlockSpec(memory_space=pltpu.HBM),
        ),
        scratch_shapes=[
            pltpu.VMEM((trainers, 1, lanes), jnp.float32),
            pltpu.SemaphoreType.DMA((1,)),
        ],
        compiler_params=pltpu.CompilerParams(vmem_limit_bytes=VMEM_BYTES),
        cost_estimate=pl.CostEstimate(
            flops=6 * rows * rank * columns, bytes_accessed=4 << 20, transcendentals=0
        ),
        name="trainer_step",
    )(gap, lowered, up, facts)


def on_device(
    pool_inputs,
    pool_targets,
    frozen,
    gain,
    adapter_down,
    adapter_up,
    sample_ids,
    buckets,
    lengths,
    destinations,
    competence,
):
    trainers = lax.axis_size(DP)
    parts = lax.axis_size("mp")
    sampled = sample_ids.shape[0]
    _, block_len, part = pool_inputs.shape
    width = frozen.shape[0]
    slots = trainers * PER_PAIR
    rows = slots * block_len
    per_peer = PER_PAIR * block_len
    down_map = adapter_down[0]
    up_map = adapter_up[0]
    bucket_range = jnp.arange(NB, dtype=jnp.int32)

    send_x, own_x, info, counts, slot_of = route(
        sample_ids, destinations[:, 0], buckets, lengths, pool_inputs, gain, trainers
    )
    got_x = lax.all_to_all(
        send_x.reshape(trainers, per_peer, part), DP, 0, 0, tiled=True
    )
    gathered = lax.all_gather(own_x.reshape(-1, part), "mp")
    message = jnp.concatenate(
        [info, jnp.broadcast_to(counts[None, :], (trainers, NB))], axis=1
    )
    got_info = lax.all_to_all(message[:, None, :], DP, 0, 0, tiled=True)[:, 0, :]

    send_gap, done = base_gap_slots(sample_ids, slot_of, gathered, own_x, frozen, pool_targets)
    got_gap = lax.all_to_all(
        send_gap.reshape(trainers, per_peer, part), DP, 0, 0, tiled=True
    )

    floor_counts = jnp.maximum(
        jnp.sum(got_info[:, 2 * PER_PAIR :], axis=0).astype(jnp.float32), 1.0
    )
    weights = jax.nn.sigmoid(
        SHARPNESS * (competence[0] - (bucket_range.astype(jnp.float32) + 0.5) / NB)
    )
    row_bucket = jnp.repeat(got_info[:, :PER_PAIR].reshape(slots), block_len)
    row_length = jnp.repeat(got_info[:, PER_PAIR : 2 * PER_PAIR].reshape(slots), block_len)
    live = (jnp.arange(rows, dtype=jnp.int32) % block_len < row_length).astype(jnp.float32)
    onehot = (row_bucket[:, None] == bucket_range[None, :]).astype(jnp.float32) * live[:, None]
    coefficient = 2.0 * jnp.sum(onehot * (weights / floor_counts)[None, :], axis=1)
    facts = jnp.concatenate(
        [onehot, coefficient[:, None], jnp.zeros((rows, 128 - NB - 1), jnp.float32)], axis=1
    )

    rows_x = got_x.reshape(rows, part)
    values = rows_x.astype(jnp.float32)
    square_total = over_parts(row_squares(rows_x, done), "mp")[0]
    inverse_rms = lax.rsqrt(square_total / width + RMS_EPSILON)
    normed = (values * inverse_rms[:, None] * gain[None, :]).astype(jnp.bfloat16)
    latent_part = lax.dot_general(
        down_map, normed, CONTRACT_LAST, preferred_element_type=jnp.float32
    )
    lowered = (ADAPTER_SCALING * over_parts(latent_part, "mp")).astype(jnp.bfloat16)

    grad_up, back_part, loss_part = trainer_step(
        got_gap.reshape(rows, part), lowered, up_map, facts, trainers
    )
    loss_over_dp = jnp.sum(lax.all_to_all(loss_part, DP, 0, 0, tiled=True), axis=0)
    back = over_parts(back_part, "mp")
    loss_sum = over_parts(loss_over_dp, "mp")[0, :NB]
    lowered_gradient = (ADAPTER_SCALING * back).astype(jnp.bfloat16)
    grad_down = jnp.dot(lowered_gradient, normed, preferred_element_type=jnp.float32)
    bucket_loss = loss_sum / (floor_counts * width)
    progress = jnp.sum(weights * bucket_loss) / jnp.sum(bucket_loss)
    competence_next = competence + 0.5 * (1.0 - competence) * progress
    return (grad_down[None], grad_up[None], bucket_loss, competence_next)


def solution(mesh):
    split = Mesh(mesh.devices.reshape(4, 8, 2, mesh.shape["mp"]), DP_MP)
    placed = (
        P(DP, None, "mp"),
        P(DP, None, "mp"),
        P(None, "mp"),
        P("mp"),
        P(DP, None, "mp"),
        P(DP, None, "mp"),
        P(DP),
        P(DP),
        P(DP),
        P(DP, None),
        P(),
    )
    return jax.shard_map(
        on_device,
        mesh=split,
        in_specs=placed,
        out_specs=(P(DP, None, "mp"), P(DP, None, "mp"), P(), P()),
        check_vma=False,
    )
```

```python
import jax
import jax.numpy as jnp
from jax import lax
from jax.experimental import pallas as pl
from jax.experimental.pallas import tpu as pltpu
from jax.sharding import Mesh
from jax.sharding import PartitionSpec as P

NB = 16
DP = ("dp_0", "dp_1", "dp_2")
DP_MP = ("dp_0", "dp_1", "dp_2", "mp")

RMS_EPSILON = 1e-05
SHARPNESS = 12.0
ADAPTER_SCALING = 2.0
PER_PAIR = 2
VMEM_BYTES = 62 * 1024 * 1024
CONTRACT_LAST = (((1,), (1,)), ((), ()))
CONTRACT_FIRST = (((0,), (0,)), ((), ()))


def over_parts(value, axis):
    peers = lax.axis_size(axis)
    others = [
        lax.ppermute(value, axis, [(i, i ^ distance) for i in range(peers)])
        for distance in range(1, peers)
    ]
    return (value + others[0]) + (others[1] + others[2])


def lane_group(packed, group, groups):
    slots = [packed[:, s * groups + group][:, None] for s in range(PER_PAIR)]
    whole = jnp.concatenate(slots, axis=1).astype(jnp.float32)
    return whole.reshape(-1, packed.shape[-1])


def square_kernel(packed, done, total):
    groups = (packed.shape[1] - 1) // PER_PAIR
    sums = None
    for g in range(groups):
        x = lane_group(packed, g, groups)
        sums = x * x if sums is None else sums + x * x
    total[...] = jnp.sum(sums.T, axis=0, keepdims=True) + done[0]


def row_squares(packed, done):
    peers, pieces, block_len, lanes = packed.shape
    rows = peers * PER_PAIR * block_len
    chunk = 16
    return pl.pallas_call(
        square_kernel,
        grid=(peers // chunk,),
        out_shape=jax.ShapeDtypeStruct((1, rows), jnp.float32),
        in_specs=[
            pl.BlockSpec((chunk, pieces, block_len, lanes), lambda i: (i, 0, 0, 0)),
            pl.BlockSpec(memory_space=pltpu.SMEM),
        ],
        out_specs=pl.BlockSpec((1, rows * chunk // peers), lambda i: (0, i)),
        compiler_params=pltpu.CompilerParams(vmem_limit_bytes=VMEM_BYTES),
        cost_estimate=pl.CostEstimate(flops=4 << 20, bytes_accessed=2 << 20, transcendentals=0),
        name="row_squares",
    )(packed, done)


def latent_kernel(packed, squares, gain, down, normed, latent):
    lanes = packed.shape[-1]
    groups = (packed.shape[1] - 1) // PER_PAIR
    inverse = lax.rsqrt(squares[...] + RMS_EPSILON)
    inverse = jnp.broadcast_to(inverse, (lanes, inverse.shape[1])).T
    for g in range(groups):
        at = slice(g * lanes, (g + 1) * lanes)
        x = lane_group(packed, g, groups)
        normed[:, at] = (x * inverse * gain[:, at]).astype(jnp.bfloat16)
    latent[...] = lax.dot_general(
        down[...], normed[...], CONTRACT_LAST, preferred_element_type=jnp.float32
    )


def latents(packed, mean_squares, gain, down):
    peers, pieces, block_len, lanes = packed.shape
    rows = peers * PER_PAIR * block_len
    rank, columns = down.shape
    chunk = 16
    part = rows * chunk // peers
    return pl.pallas_call(
        latent_kernel,
        grid=(peers // chunk,),
        out_shape=(
            jax.ShapeDtypeStruct((rows, columns), jnp.bfloat16),
            jax.ShapeDtypeStruct((rank, rows), jnp.float32),
        ),
        in_specs=[
            pl.BlockSpec((chunk, pieces, block_len, lanes), lambda i: (i, 0, 0, 0)),
            pl.BlockSpec((1, part), lambda i: (0, i)),
            pl.BlockSpec((1, columns), lambda i: (0, 0)),
            pl.BlockSpec((rank, columns), lambda i: (0, 0)),
        ],
        out_specs=(
            pl.BlockSpec((part, columns), lambda i: (i, 0)),
            pl.BlockSpec((rank, part), lambda i: (0, i)),
        ),
        compiler_params=pltpu.CompilerParams(vmem_limit_bytes=VMEM_BYTES),
        cost_estimate=pl.CostEstimate(
            flops=2 * rows * rank * columns, bytes_accessed=4 << 20, transcendentals=rows
        ),
        name="latents",
    )(packed, mean_squares, gain[None, :], down)


def route_kernel(
    ids_in, dest_in, buckets_in, lengths_in, pool_in, gain_in,
    send_out, own_out, slot_of,
    ids, dest, buckets, lengths, pool, gain, send, own, arrived, info, counts, sem,
):
    pairs = (
        (pool_in, pool),
        (ids_in, ids),
        (dest_in, dest),
        (buckets_in, buckets),
        (lengths_in, lengths),
        (gain_in, gain),
    )
    copies = [
        pltpu.make_async_copy(source, target, sem.at[i])
        for i, (source, target) in enumerate(pairs)
    ]
    for copy in copies:
        copy.start()
    sampled = ids.shape[0]
    trainers, pieces, block_len, lanes = send.shape
    groups = (pieces - 1) // PER_PAIR

    def clear(k, carry):
        arrived[k] = 0
        for s in range(PER_PAIR):
            info[s, k] = 0
            info[PER_PAIR + s, k] = 0
        return carry

    def clear_counts(b, carry):
        counts[b] = 0
        return carry

    lax.fori_loop(0, trainers, clear, 0)
    lax.fori_loop(0, NB, clear_counts, 0)
    for copy in copies:
        copy.wait()

    def place(j, carry):
        block = ids[j]
        trainer = dest[j]
        values = pool[block]
        own[j] = values
        order = arrived[trainer]
        arrived[trainer] = order + 1
        slot = trainer * PER_PAIR + order
        for g in range(groups):
            send[trainer, order * groups + g] = values[:, g * lanes : (g + 1) * lanes]
        slot_of[j] = slot
        bucket = buckets[block]
        length = lengths[block]
        info[order, trainer] = bucket
        info[PER_PAIR + order, trainer] = length
        counts[bucket] = counts[bucket] + length
        return carry

    lax.fori_loop(0, sampled, place, 0)

    row = lax.broadcasted_iota(jnp.int32, (block_len, lanes), 0)
    lane = lax.broadcasted_iota(jnp.int32, (block_len, lanes), 1)
    holder = jnp.zeros((block_len, lanes), jnp.int32)
    for b in range(NB):
        count = counts[b]
        holder = jnp.where((row == 1) & (lane == b), count // 16, holder)
        holder = jnp.where((row == 2) & (lane == b), count % 16, holder)

    def finish(k, found):
        for s in range(PER_PAIR):
            free = arrived[k] <= s

            @pl.when(free)
            def _():
                slot_of[sampled + found] = k * PER_PAIR + s
                for g in range(groups):
                    send[k, s * groups + g] = jnp.zeros((block_len, lanes), send.dtype)

            found = found + jnp.where(free, 1, 0)
        facts = holder
        for i in range(2 * PER_PAIR):
            facts = jnp.where((row == 0) & (lane == i), info[i, k], facts)
        send[k, pieces - 1] = facts.astype(jnp.float32).astype(send.dtype)
        return found

    lax.fori_loop(0, trainers, finish, 0)
    send_copy = pltpu.make_async_copy(send, send_out, sem.at[0])
    send_copy.start()
    whole = gain[...]
    high = whole.astype(jnp.bfloat16).astype(jnp.float32)
    middle = (whole - high).astype(jnp.bfloat16).astype(jnp.float32)
    low = whole - high - middle
    zeros = jnp.zeros((own.shape[1] - 3, whole.shape[1]), jnp.float32)
    own[sampled] = jnp.concatenate([high, middle, low, zeros], axis=0).astype(jnp.bfloat16)
    own[sampled + 1] = jnp.zeros(own.shape[1:], own.dtype)
    own_copy = pltpu.make_async_copy(own, own_out, sem.at[1])
    own_copy.start()
    own_copy.wait()
    send_copy.wait()


def route(ids, dest, buckets, lengths, pool, gain, trainers):
    sampled = ids.shape[0]
    slots = trainers * PER_PAIR
    block = pool.shape[1:]
    lanes = 128
    message = (trainers, PER_PAIR * (block[1] // lanes) + 1, block[0], lanes)
    smem = pl.BlockSpec(memory_space=pltpu.SMEM)
    hbm = pl.BlockSpec(memory_space=pltpu.HBM)
    return pl.pallas_call(
        route_kernel,
        out_shape=(
            jax.ShapeDtypeStruct(message, pool.dtype),
            jax.ShapeDtypeStruct((sampled + 2, *block), pool.dtype),
            jax.ShapeDtypeStruct((slots,), jnp.int32),
        ),
        in_specs=[hbm] * 6,
        out_specs=(hbm, hbm, smem),
        scratch_shapes=[
            pltpu.SMEM(ids.shape, jnp.int32),
            pltpu.SMEM(dest.shape, jnp.int32),
            pltpu.SMEM(buckets.shape, jnp.int32),
            pltpu.SMEM(lengths.shape, jnp.int32),
            pltpu.VMEM(pool.shape, pool.dtype),
            pltpu.VMEM((1, gain.shape[0]), jnp.float32),
            pltpu.VMEM(message, pool.dtype),
            pltpu.VMEM((sampled + 2, *block), pool.dtype),
            pltpu.SMEM((trainers,), jnp.int32),
            pltpu.SMEM((2 * PER_PAIR, trainers), jnp.int32),
            pltpu.SMEM((NB,), jnp.int32),
            pltpu.SemaphoreType.DMA((6,)),
        ],
        compiler_params=pltpu.CompilerParams(vmem_limit_bytes=VMEM_BYTES),
        cost_estimate=pl.CostEstimate(flops=0, bytes_accessed=5 << 20, transcendentals=0),
        name="route",
    )(ids, dest, buckets, lengths, pool, gain[None, :])


def gap_kernel(
    ids, slot_of, gathered, pieces, frozen, own_in, targets_in,
    send_out, done, own, targets, send, normed, gap, sem,
):
    step = pl.program_id(0)
    parts, chunk, part = gathered.shape
    sampled, block_len, columns = gap.shape
    chunks = sampled * block_len // chunk
    width = frozen.shape[1]
    slots = send.shape[0]
    own_copy = pltpu.make_async_copy(own_in.at[pl.ds(0, sampled)], own, sem.at[0])
    target_copy = pltpu.make_async_copy(targets_in, targets, sem.at[1])

    @pl.when(step == 0)
    def _():
        own_copy.start()
        target_copy.start()
        done[0] = 0.0

        def fill(s, carry):
            send[slot_of[sampled + s]] = jnp.zeros((block_len, columns), jnp.bfloat16)
            return carry

        lax.fori_loop(0, slots - sampled, fill, 0)

    @pl.when(step < chunks)
    def _():
        total = jnp.zeros((chunk, 1), jnp.float32)
        for p in range(parts):
            x = gathered[p].astype(jnp.float32)
            total = total + jnp.sum(x * x, axis=1, keepdims=True)
        inverse = lax.rsqrt(total / (parts * part) + RMS_EPSILON)
        at = pl.ds(pl.multiple_of(step * chunk, chunk), chunk)
        for p in range(parts):
            three = pieces[p].astype(jnp.float32)
            gain = three[0:1] + three[1:2] + three[2:3]
            x = gathered[p].astype(jnp.float32)
            normed[at, p * part : (p + 1) * part] = (x * inverse * gain).astype(jnp.bfloat16)

    @pl.when(step == chunks)
    def _():
        own_copy.wait()
        target_copy.wait()

    @pl.when(step >= chunks)
    def _():
        projected = jnp.dot(normed[...], frozen[...], preferred_element_type=jnp.float32)
        at = pl.ds(pl.multiple_of((step - chunks) * width, width), width)
        x = own[:, :, at].astype(jnp.float32)
        gap[:, :, at] = x + projected.reshape(sampled, block_len, width)

    @pl.when(step == pl.num_programs(0) - 1)
    def _():
        def place(j, carry):
            target = targets[ids[j]].astype(jnp.float32)
            send[slot_of[j]] = (gap[j] - target).astype(jnp.bfloat16)
            return carry

        lax.fori_loop(0, sampled, place, 0, unroll=4)
        copy = pltpu.make_async_copy(send, send_out, sem.at[0])
        copy.start()
        copy.wait()


def base_gap_slots(ids, slot_of, gathered, own, frozen, targets):
    parts, _, part = gathered.shape
    width, columns = frozen.shape
    slots = slot_of.shape[0]
    sampled = ids.shape[0]
    block = own.shape[1:]
    rows = sampled * block[0]
    tile = 256
    chunk = 128
    chunks = rows // chunk
    smem = pl.BlockSpec(memory_space=pltpu.SMEM)
    hbm = pl.BlockSpec(memory_space=pltpu.HBM)
    return pl.pallas_call(
        gap_kernel,
        grid=(chunks + columns // tile,),
        out_shape=(
            jax.ShapeDtypeStruct((slots, *block), jnp.bfloat16),
            jax.ShapeDtypeStruct((1,), jnp.float32),
        ),
        in_specs=[
            smem,
            smem,
            pl.BlockSpec((parts, chunk, part), lambda n: (0, jnp.minimum(n, chunks - 1), 0)),
            pl.BlockSpec((parts, 16, part), lambda n: (0, rows // 16, 0)),
            pl.BlockSpec((width, tile), lambda n: (0, jnp.maximum(n - chunks, 0))),
            hbm,
            hbm,
        ],
        out_specs=(hbm, smem),
        scratch_shapes=[
            pltpu.VMEM((sampled, *block), jnp.bfloat16),
            pltpu.VMEM(targets.shape, jnp.bfloat16),
            pltpu.VMEM((slots, *block), jnp.bfloat16),
            pltpu.VMEM((rows, width), jnp.bfloat16),
            pltpu.VMEM((sampled, *block), jnp.float32),
            pltpu.SemaphoreType.DMA((2,)),
        ],
        compiler_params=pltpu.CompilerParams(vmem_limit_bytes=VMEM_BYTES),
        cost_estimate=pl.CostEstimate(
            flops=2 * rows * width * columns, bytes_accessed=18 << 20, transcendentals=rows
        ),
        name="base_gap",
    )(ids, slot_of, gathered, gathered, frozen, own, targets)


def trainer_kernel(gap, lowered, up, facts, grad_up, back, loss):
    step = pl.program_id(0)
    rank, columns = up.shape
    lanes = facts.shape[1]
    low = lowered[...]
    up_map = up[...]
    facts_now = facts[...]
    distance = gap[...].astype(jnp.float32) + lax.dot_general(
        low, up_map, CONTRACT_FIRST, preferred_element_type=jnp.float32
    )
    output_grad = (facts_now[:, NB : NB + 1] * distance).astype(jnp.bfloat16)
    squares = jnp.sum(distance * distance, axis=1, keepdims=True)
    loss[...] = jnp.zeros(loss.shape, jnp.float32)
    loss[0:1, 0:lanes] = jnp.sum(facts_now * squares, axis=0, keepdims=True)
    back[0:rank] = lax.dot_general(
        up_map, output_grad, CONTRACT_LAST, preferred_element_type=jnp.float32
    )
    back[rank:] = loss[...]
    own = jnp.dot(low, output_grad, preferred_element_type=jnp.float32)

    @pl.when(step == 0)
    def _():
        grad_up[...] = own

    @pl.when(step > 0)
    def _():
        grad_up[...] += own


def trainer_step(gap, lowered, up, facts):
    rows, columns = gap.shape
    rank = up.shape[0]
    lanes = facts.shape[1]
    chunk = 256
    return pl.pallas_call(
        trainer_kernel,
        grid=(rows // chunk,),
        out_shape=(
            jax.ShapeDtypeStruct((rank, columns), jnp.float32),
            jax.ShapeDtypeStruct((rank + 8, rows), jnp.float32),
        ),
        in_specs=[
            pl.BlockSpec((chunk, columns), lambda i: (i, 0)),
            pl.BlockSpec((rank, chunk), lambda i: (0, i)),
            pl.BlockSpec((rank, columns), lambda i: (0, 0)),
            pl.BlockSpec((chunk, lanes), lambda i: (i, 0)),
        ],
        out_specs=(
            pl.BlockSpec((rank, columns), lambda i: (0, 0)),
            pl.BlockSpec((rank + 8, chunk), lambda i: (0, i)),
        ),
        scratch_shapes=[pltpu.VMEM((8, chunk), jnp.float32)],
        compiler_params=pltpu.CompilerParams(vmem_limit_bytes=VMEM_BYTES),
        cost_estimate=pl.CostEstimate(
            flops=6 * rows * rank * columns, bytes_accessed=4 << 20, transcendentals=0
        ),
        name="trainer_step",
    )(gap, lowered, up, facts)


def on_device(
    pool_inputs,
    pool_targets,
    frozen,
    gain,
    adapter_down,
    adapter_up,
    sample_ids,
    buckets,
    lengths,
    destinations,
    competence,
):
    trainers = lax.axis_size(DP)
    parts = lax.axis_size("mp")
    sampled = sample_ids.shape[0]
    _, block_len, part = pool_inputs.shape
    width = frozen.shape[0]
    slots = trainers * PER_PAIR
    rows = slots * block_len
    per_peer = PER_PAIR * block_len
    down_map = adapter_down[0]
    up_map = adapter_up[0]
    bucket_range = jnp.arange(NB, dtype=jnp.int32)

    send_x, own_x, slot_of = route(
        sample_ids, destinations[:, 0], buckets, lengths, pool_inputs, gain, trainers
    )
    got_x = lax.all_to_all(send_x, DP, 0, 0, tiled=True)
    gathered = lax.all_gather(own_x.reshape(-1, part), "mp")
    send_gap, done = base_gap_slots(sample_ids, slot_of, gathered, own_x, frozen, pool_targets)
    got_gap = lax.all_to_all(
        send_gap.reshape(trainers, per_peer, part), DP, 0, 0, tiled=True
    )

    got_info = got_x[:, -1, 0, : 2 * PER_PAIR].astype(jnp.float32).astype(jnp.int32)
    got_counts = got_x[:, -1, 1:3, :NB].astype(jnp.float32)
    counts = jnp.sum(16.0 * got_counts[:, 0] + got_counts[:, 1], axis=0)
    floor_counts = jnp.maximum(counts, 1.0)
    weights = jax.nn.sigmoid(
        SHARPNESS * (competence[0] - (bucket_range.astype(jnp.float32) + 0.5) / NB)
    )
    row_bucket = jnp.repeat(got_info[:, :PER_PAIR].reshape(slots), block_len)
    row_length = jnp.repeat(got_info[:, PER_PAIR:].reshape(slots), block_len)
    live = (jnp.arange(rows, dtype=jnp.int32) % block_len < row_length).astype(jnp.float32)
    onehot = (row_bucket[:, None] == bucket_range[None, :]).astype(jnp.float32) * live[:, None]
    coefficient = 2.0 * jnp.sum(onehot * (weights / floor_counts)[None, :], axis=1)
    facts = jnp.concatenate(
        [onehot, coefficient[:, None], jnp.zeros((rows, 128 - NB - 1), jnp.float32)], axis=1
    )

    mean_squares = over_parts(row_squares(got_x, done), "mp") / width
    normed, latent_part = latents(got_x, mean_squares, gain, down_map)
    lowered = (ADAPTER_SCALING * over_parts(latent_part, "mp")).astype(jnp.bfloat16)

    grad_up, back_part = trainer_step(got_gap.reshape(rows, part), lowered, up_map, facts)
    back = over_parts(back_part, "mp")
    rank = up_map.shape[0]
    own_loss = jnp.sum(back[rank].reshape(-1, 256)[:, :NB], axis=0)
    loss_sum = jnp.sum(
        lax.all_to_all(jnp.broadcast_to(own_loss, (trainers, 1, NB)), DP, 0, 0, tiled=True),
        axis=(0, 1),
    )
    lowered_gradient = (ADAPTER_SCALING * back[:rank]).astype(jnp.bfloat16)
    grad_down = jnp.dot(lowered_gradient, normed, preferred_element_type=jnp.float32)
    bucket_loss = loss_sum / (floor_counts * width)
    progress = jnp.sum(weights * bucket_loss) / jnp.sum(bucket_loss)
    competence_next = competence + 0.5 * (1.0 - competence) * progress
    return (grad_down[None], grad_up[None], bucket_loss, competence_next)


def solution(mesh):
    split = Mesh(mesh.devices.reshape(4, 8, 2, mesh.shape["mp"]), DP_MP)
    placed = (
        P(DP, None, "mp"),
        P(DP, None, "mp"),
        P(None, "mp"),
        P("mp"),
        P(DP, None, "mp"),
        P(DP, None, "mp"),
        P(DP),
        P(DP),
        P(DP),
        P(DP, None),
        P(),
    )
    return jax.shard_map(
        on_device,
        mesh=split,
        in_specs=placed,
        out_specs=(P(DP, None, "mp"), P(DP, None, "mp"), P(), P()),
        check_vma=False,
    )
```

```python
import jax
import jax.numpy as jnp
from jax import lax
from jax.experimental import pallas as pl
from jax.experimental.pallas import tpu as pltpu
from jax.sharding import Mesh
from jax.sharding import PartitionSpec as P

NB = 16
DP = ("dp_0", "dp_1", "dp_2")
DP_MP = ("dp_0", "dp_1", "dp_2", "mp")

RMS_EPSILON = 1e-05
SHARPNESS = 12.0
ADAPTER_SCALING = 2.0
PER_PAIR = 2
VMEM_BYTES = 62 * 1024 * 1024
CONTRACT_LAST = (((1,), (1,)), ((), ()))
CONTRACT_FIRST = (((0,), (0,)), ((), ()))


def swap(value, axis, distance):
    peers = lax.axis_size(axis)
    return lax.ppermute(value, axis, [(i, i ^ distance) for i in range(peers)])


def over_parts(value, axis):
    pair = value + swap(value, axis, 1)
    return pair + swap(pair, axis, 3)


def from_parts(value, axis, cut):
    near = swap(value, axis, 1)
    other = swap(value, axis, 3)
    return near, other, swap(other[:cut], axis, 1), swap(near[cut:], axis, 3)


def lane_group(packed, group, groups):
    slots = [packed[:, s * groups + group][:, None] for s in range(PER_PAIR)]
    whole = jnp.concatenate(slots, axis=1).astype(jnp.float32)
    return whole.reshape(-1, packed.shape[-1])


def square_kernel(packed, done, total):
    groups = (packed.shape[1] - 1) // PER_PAIR
    sums = None
    for g in range(groups):
        x = lane_group(packed, g, groups)
        sums = x * x if sums is None else sums + x * x
    total[...] = jnp.sum(sums.T, axis=0, keepdims=True) + done[0]


def row_squares(packed, done):
    peers, pieces, block_len, lanes = packed.shape
    rows = peers * PER_PAIR * block_len
    chunk = 16
    return pl.pallas_call(
        square_kernel,
        grid=(peers // chunk,),
        out_shape=jax.ShapeDtypeStruct((1, rows), jnp.float32),
        in_specs=[
            pl.BlockSpec((chunk, pieces, block_len, lanes), lambda i: (i, 0, 0, 0)),
            pl.BlockSpec(memory_space=pltpu.SMEM),
        ],
        out_specs=pl.BlockSpec((1, rows * chunk // peers), lambda i: (0, i)),
        compiler_params=pltpu.CompilerParams(vmem_limit_bytes=VMEM_BYTES),
        cost_estimate=pl.CostEstimate(flops=4 << 20, bytes_accessed=2 << 20, transcendentals=0),
        name="row_squares",
    )(packed, done)


def latent_kernel(packed, squares, gain, down, normed, latent):
    lanes = packed.shape[-1]
    groups = (packed.shape[1] - 1) // PER_PAIR
    inverse = lax.rsqrt(squares[...] + RMS_EPSILON)
    inverse = jnp.broadcast_to(inverse, (lanes, inverse.shape[1])).T
    for g in range(groups):
        at = slice(g * lanes, (g + 1) * lanes)
        x = lane_group(packed, g, groups)
        normed[:, at] = (x * inverse * gain[:, at]).astype(jnp.bfloat16)
    latent[...] = lax.dot_general(
        down[...], normed[...], CONTRACT_LAST, preferred_element_type=jnp.float32
    )


def latents(packed, mean_squares, gain, down):
    peers, pieces, block_len, lanes = packed.shape
    rows = peers * PER_PAIR * block_len
    rank, columns = down.shape
    chunk = 16
    part = rows * chunk // peers
    return pl.pallas_call(
        latent_kernel,
        grid=(peers // chunk,),
        out_shape=(
            jax.ShapeDtypeStruct((rows, columns), jnp.bfloat16),
            jax.ShapeDtypeStruct((rank, rows), jnp.float32),
        ),
        in_specs=[
            pl.BlockSpec((chunk, pieces, block_len, lanes), lambda i: (i, 0, 0, 0)),
            pl.BlockSpec((1, part), lambda i: (0, i)),
            pl.BlockSpec((1, columns), lambda i: (0, 0)),
            pl.BlockSpec((rank, columns), lambda i: (0, 0)),
        ],
        out_specs=(
            pl.BlockSpec((part, columns), lambda i: (i, 0)),
            pl.BlockSpec((rank, part), lambda i: (0, i)),
        ),
        compiler_params=pltpu.CompilerParams(vmem_limit_bytes=VMEM_BYTES),
        cost_estimate=pl.CostEstimate(
            flops=2 * rows * rank * columns, bytes_accessed=4 << 20, transcendentals=rows
        ),
        name="latents",
    )(packed, mean_squares, gain[None, :], down)


def route_kernel(
    ids_in, dest_in, buckets_in, lengths_in, pool_in, gain_in,
    send_out, own_out, slot_of,
    ids, dest, buckets, lengths, pool, gain, send, own, arrived, info, counts, sem,
):
    pairs = (
        (pool_in, pool),
        (ids_in, ids),
        (dest_in, dest),
        (buckets_in, buckets),
        (lengths_in, lengths),
        (gain_in, gain),
    )
    copies = [
        pltpu.make_async_copy(source, target, sem.at[i])
        for i, (source, target) in enumerate(pairs)
    ]
    for copy in copies:
        copy.start()
    sampled = ids.shape[0]
    trainers, pieces, block_len, lanes = send.shape
    groups = (pieces - 1) // PER_PAIR

    def clear(k, carry):
        arrived[k] = 0
        for s in range(PER_PAIR):
            info[s, k] = 0
            info[PER_PAIR + s, k] = 0
        return carry

    def clear_counts(b, carry):
        counts[b] = 0
        return carry

    lax.fori_loop(0, trainers, clear, 0)
    lax.fori_loop(0, NB, clear_counts, 0)
    for copy in copies:
        copy.wait()

    def place(j, carry):
        block = ids[j]
        trainer = dest[j]
        values = pool[block]
        own[j] = values
        order = arrived[trainer]
        arrived[trainer] = order + 1
        slot = trainer * PER_PAIR + order
        for g in range(groups):
            send[trainer, order * groups + g] = values[:, g * lanes : (g + 1) * lanes]
        slot_of[j] = slot
        bucket = buckets[block]
        length = lengths[block]
        info[order, trainer] = bucket
        info[PER_PAIR + order, trainer] = length
        counts[bucket] = counts[bucket] + length
        return carry

    lax.fori_loop(0, sampled, place, 0)

    row = lax.broadcasted_iota(jnp.int32, (block_len, lanes), 0)
    lane = lax.broadcasted_iota(jnp.int32, (block_len, lanes), 1)
    holder = jnp.zeros((block_len, lanes), jnp.int32)
    for b in range(NB):
        count = counts[b]
        holder = jnp.where((row == 1) & (lane == b), count // 16, holder)
        holder = jnp.where((row == 2) & (lane == b), count % 16, holder)

    def finish(k, found):
        for s in range(PER_PAIR):
            free = arrived[k] <= s

            @pl.when(free)
            def _():
                slot_of[sampled + found] = k * PER_PAIR + s
                for g in range(groups):
                    send[k, s * groups + g] = jnp.zeros((block_len, lanes), send.dtype)

            found = found + jnp.where(free, 1, 0)
        facts = holder
        for i in range(2 * PER_PAIR):
            facts = jnp.where((row == 0) & (lane == i), info[i, k], facts)
        send[k, pieces - 1] = facts.astype(jnp.float32).astype(send.dtype)
        return found

    lax.fori_loop(0, trainers, finish, 0)
    send_copy = pltpu.make_async_copy(send, send_out, sem.at[0])
    send_copy.start()
    whole = gain[...]
    high = whole.astype(jnp.bfloat16).astype(jnp.float32)
    middle = (whole - high).astype(jnp.bfloat16).astype(jnp.float32)
    low = whole - high - middle
    zeros = jnp.zeros((own.shape[1] - 3, whole.shape[1]), jnp.float32)
    own[sampled] = jnp.concatenate([high, middle, low, zeros], axis=0).astype(jnp.bfloat16)
    own[sampled + 1] = jnp.zeros(own.shape[1:], own.dtype)
    own_copy = pltpu.make_async_copy(own, own_out, sem.at[1])
    own_copy.start()
    own_copy.wait()
    send_copy.wait()


def route(ids, dest, buckets, lengths, pool, gain, trainers):
    sampled = ids.shape[0]
    slots = trainers * PER_PAIR
    block = pool.shape[1:]
    lanes = 128
    message = (trainers, PER_PAIR * (block[1] // lanes) + 1, block[0], lanes)
    smem = pl.BlockSpec(memory_space=pltpu.SMEM)
    hbm = pl.BlockSpec(memory_space=pltpu.HBM)
    return pl.pallas_call(
        route_kernel,
        out_shape=(
            jax.ShapeDtypeStruct(message, pool.dtype),
            jax.ShapeDtypeStruct((sampled + 2, *block), pool.dtype),
            jax.ShapeDtypeStruct((slots,), jnp.int32),
        ),
        in_specs=[hbm] * 6,
        out_specs=(hbm, hbm, smem),
        scratch_shapes=[
            pltpu.SMEM(ids.shape, jnp.int32),
            pltpu.SMEM(dest.shape, jnp.int32),
            pltpu.SMEM(buckets.shape, jnp.int32),
            pltpu.SMEM(lengths.shape, jnp.int32),
            pltpu.VMEM(pool.shape, pool.dtype),
            pltpu.VMEM((1, gain.shape[0]), jnp.float32),
            pltpu.VMEM(message, pool.dtype),
            pltpu.VMEM((sampled + 2, *block), pool.dtype),
            pltpu.SMEM((trainers,), jnp.int32),
            pltpu.SMEM((2 * PER_PAIR, trainers), jnp.int32),
            pltpu.SMEM((NB,), jnp.int32),
            pltpu.SemaphoreType.DMA((6,)),
        ],
        compiler_params=pltpu.CompilerParams(vmem_limit_bytes=VMEM_BYTES),
        cost_estimate=pl.CostEstimate(flops=0, bytes_accessed=5 << 20, transcendentals=0),
        name="route",
    )(ids, dest, buckets, lengths, pool, gain[None, :])


def gap_kernel(
    ids, slot_of, order, mine, near, other, far_first, far_last,
    mine_gain, near_gain, other_gain, far_gain, frozen, own_in, targets_in,
    send_out, done, own, targets, send, normed, gap, sem,
):
    step = pl.program_id(0)
    chunk, part = mine.shape
    sampled, block_len, columns = gap.shape
    chunks = sampled * block_len // chunk
    width, tile = frozen.shape
    far_first_chunks = chunks // 2
    slots = send.shape[0]
    own_copy = pltpu.make_async_copy(own_in.at[pl.ds(0, sampled)], own, sem.at[0])
    target_copy = pltpu.make_async_copy(targets_in, targets, sem.at[1])

    @pl.when(step == 0)
    def _():
        own_copy.start()
        target_copy.start()
        done[0] = 0.0

        def fill(s, carry):
            send[slot_of[sampled + s]] = jnp.zeros((block_len, columns), jnp.bfloat16)
            return carry

        lax.fori_loop(0, slots - sampled, fill, 0)

    @pl.when(step < chunks)
    def _():
        first = step < far_first_chunks
        rows_of = (
            lambda: mine[...].astype(jnp.float32),
            lambda: near[...].astype(jnp.float32),
            lambda: jnp.where(first, far_first[...], far_last[...]).astype(jnp.float32),
            lambda: other[...].astype(jnp.float32),
        )
        gains = (mine_gain, near_gain, far_gain, other_gain)
        squares = jnp.zeros((chunk, part), jnp.float32)
        for get in rows_of:
            x = get()
            squares = squares + x * x
        total = jnp.sum(squares, axis=1, keepdims=True)
        inverse = lax.rsqrt(total / width + RMS_EPSILON)
        at = pl.ds(pl.multiple_of(step * chunk, chunk), chunk)
        for p, (get, pieces) in enumerate(zip(rows_of, gains)):
            three = pieces[...].astype(jnp.float32)
            gain = three[0:1] + three[1:2] + three[2:3]
            to = pl.ds(pl.multiple_of(order[p] * part, part), part)
            normed[at, to] = (get() * inverse * gain).astype(jnp.bfloat16)

    @pl.when(step == chunks)
    def _():
        own_copy.wait()
        target_copy.wait()

    @pl.when(step >= chunks)
    def _():
        projected = jnp.dot(normed[...], frozen[...], preferred_element_type=jnp.float32)
        at = pl.ds(pl.multiple_of((step - chunks) * tile, tile), tile)
        x = own[:, :, at].astype(jnp.float32)
        gap[:, :, at] = x + projected.reshape(sampled, block_len, tile)

    @pl.when(step == pl.num_programs(0) - 1)
    def _():
        def place(j, carry):
            target = targets[ids[j]].astype(jnp.float32)
            send[slot_of[j]] = (gap[j] - target).astype(jnp.bfloat16)
            return carry

        lax.fori_loop(0, sampled, place, 0, unroll=4)
        copy = pltpu.make_async_copy(send, send_out, sem.at[0])
        copy.start()
        copy.wait()


def base_gap_slots(ids, slot_of, order, own, received, frozen, targets):
    near, other, far_first, far_last = received
    part = near.shape[1]
    width, columns = frozen.shape
    slots = slot_of.shape[0]
    sampled = ids.shape[0]
    block = own.shape[1:]
    rows = sampled * block[0]
    tile = 256
    chunk = 128
    chunks = rows // chunk
    half = chunks // 2
    all_rows = pl.BlockSpec((chunk, part), lambda n: (jnp.minimum(n, chunks - 1), 0))
    all_gain = pl.BlockSpec((16, part), lambda n: (rows // 16, 0))
    mine = own.reshape(-1, part)
    smem = pl.BlockSpec(memory_space=pltpu.SMEM)
    hbm = pl.BlockSpec(memory_space=pltpu.HBM)
    return pl.pallas_call(
        gap_kernel,
        grid=(chunks + columns // tile,),
        out_shape=(
            jax.ShapeDtypeStruct((slots, *block), jnp.bfloat16),
            jax.ShapeDtypeStruct((1,), jnp.float32),
        ),
        in_specs=[
            smem,
            smem,
            smem,
            all_rows,
            all_rows,
            all_rows,
            pl.BlockSpec((chunk, part), lambda n: (jnp.minimum(n, half - 1), 0)),
            pl.BlockSpec((chunk, part), lambda n: (jnp.clip(n - half, 0, half - 1), 0)),
            all_gain,
            all_gain,
            all_gain,
            pl.BlockSpec((16, part), lambda n: (rows // 32, 0)),
            pl.BlockSpec((width, tile), lambda n: (0, jnp.maximum(n - chunks, 0))),
            hbm,
            hbm,
        ],
        out_specs=(hbm, smem),
        scratch_shapes=[
            pltpu.VMEM((sampled, *block), jnp.bfloat16),
            pltpu.VMEM(targets.shape, jnp.bfloat16),
            pltpu.VMEM((slots, *block), jnp.bfloat16),
            pltpu.VMEM((rows, width), jnp.bfloat16),
            pltpu.VMEM((sampled, *block), jnp.float32),
            pltpu.SemaphoreType.DMA((2,)),
        ],
        compiler_params=pltpu.CompilerParams(vmem_limit_bytes=VMEM_BYTES),
        cost_estimate=pl.CostEstimate(
            flops=2 * rows * width * columns, bytes_accessed=18 << 20, transcendentals=rows
        ),
        name="base_gap",
    )(
        ids, slot_of, order, mine, near, other, far_first, far_last,
        mine, near, other, far_last, frozen, own, targets,
    )


def trainer_kernel(gap, lowered, up, facts, grad_up, back, loss):
    step = pl.program_id(0)
    low = lowered[...]
    up_map = up[...]
    facts_now = facts[...]
    distance = gap[...].astype(jnp.float32) + lax.dot_general(
        low, up_map, CONTRACT_FIRST, preferred_element_type=jnp.float32
    )
    output_grad = (facts_now[:, NB : NB + 1] * distance).astype(jnp.bfloat16)
    squares = jnp.sum(distance * distance, axis=1, keepdims=True)
    part = jnp.sum(facts_now * squares, axis=0, keepdims=True)
    back[...] = lax.dot_general(
        up_map, output_grad, CONTRACT_LAST, preferred_element_type=jnp.float32
    )
    own = jnp.dot(low, output_grad, preferred_element_type=jnp.float32)

    @pl.when(step == 0)
    def _():
        grad_up[...] = own
        loss[...] = part

    @pl.when(step > 0)
    def _():
        grad_up[...] += own
        loss[...] += part


def trainer_step(gap, lowered, up, facts):
    rows, columns = gap.shape
    rank = up.shape[0]
    lanes = facts.shape[1]
    chunk = 256
    return pl.pallas_call(
        trainer_kernel,
        grid=(rows // chunk,),
        out_shape=(
            jax.ShapeDtypeStruct((rank, columns), jnp.float32),
            jax.ShapeDtypeStruct((rank, rows), jnp.float32),
            jax.ShapeDtypeStruct((1, lanes), jnp.float32),
        ),
        in_specs=[
            pl.BlockSpec((chunk, columns), lambda i: (i, 0)),
            pl.BlockSpec((rank, chunk), lambda i: (0, i)),
            pl.BlockSpec((rank, columns), lambda i: (0, 0)),
            pl.BlockSpec((chunk, lanes), lambda i: (i, 0)),
        ],
        out_specs=(
            pl.BlockSpec((rank, columns), lambda i: (0, 0)),
            pl.BlockSpec((rank, chunk), lambda i: (0, i)),
            pl.BlockSpec((1, lanes), lambda i: (0, 0)),
        ),
        compiler_params=pltpu.CompilerParams(vmem_limit_bytes=VMEM_BYTES),
        cost_estimate=pl.CostEstimate(
            flops=6 * rows * rank * columns, bytes_accessed=4 << 20, transcendentals=0
        ),
        name="trainer_step",
    )(gap, lowered, up, facts)


def on_device(
    pool_inputs,
    pool_targets,
    frozen,
    gain,
    adapter_down,
    adapter_up,
    sample_ids,
    buckets,
    lengths,
    destinations,
    competence,
):
    trainers = lax.axis_size(DP)
    sampled = sample_ids.shape[0]
    _, block_len, part = pool_inputs.shape
    width = frozen.shape[0]
    slots = trainers * PER_PAIR
    rows = slots * block_len
    per_peer = PER_PAIR * block_len
    down_map = adapter_down[0]
    up_map = adapter_up[0]
    bucket_range = jnp.arange(NB, dtype=jnp.int32)

    send_x, own_x, slot_of = route(
        sample_ids, destinations[:, 0], buckets, lengths, pool_inputs, gain, trainers
    )
    got_x = lax.all_to_all(send_x, DP, 0, 0, tiled=True)
    cut = sampled * block_len // 2
    received = from_parts(own_x.reshape(-1, part), "mp", cut)
    order = lax.axis_index("mp") ^ jnp.arange(lax.axis_size("mp"), dtype=jnp.int32)
    send_gap, done = base_gap_slots(
        sample_ids, slot_of, order, own_x, received, frozen, pool_targets
    )
    got_gap = lax.all_to_all(
        send_gap.reshape(trainers, per_peer, part), DP, 0, 0, tiled=True
    )

    got_info = got_x[:, -1, 0, : 2 * PER_PAIR].astype(jnp.float32).astype(jnp.int32)
    got_counts = got_x[:, -1, 1:3, :NB].astype(jnp.float32)
    counts = jnp.sum(16.0 * got_counts[:, 0] + got_counts[:, 1], axis=0)
    floor_counts = jnp.maximum(counts, 1.0)
    weights = jax.nn.sigmoid(
        SHARPNESS * (competence[0] - (bucket_range.astype(jnp.float32) + 0.5) / NB)
    )
    row_bucket = jnp.repeat(got_info[:, :PER_PAIR].reshape(slots), block_len)
    row_length = jnp.repeat(got_info[:, PER_PAIR:].reshape(slots), block_len)
    live = (jnp.arange(rows, dtype=jnp.int32) % block_len < row_length).astype(jnp.float32)
    onehot = (row_bucket[:, None] == bucket_range[None, :]).astype(jnp.float32) * live[:, None]
    coefficient = 2.0 * jnp.sum(onehot * (weights / floor_counts)[None, :], axis=1)
    facts = jnp.concatenate(
        [onehot, coefficient[:, None], jnp.zeros((rows, 128 - NB - 1), jnp.float32)], axis=1
    )

    mean_squares = over_parts(row_squares(got_x, done), "mp") / width
    normed, latent_part = latents(got_x, mean_squares, gain, down_map)
    lowered = (ADAPTER_SCALING * over_parts(latent_part, "mp")).astype(jnp.bfloat16)

    grad_up, back_part, loss_part = trainer_step(
        got_gap.reshape(rows, part), lowered, up_map, facts
    )
    own_loss = over_parts(loss_part, "mp")[:, :NB]
    loss_sum = jnp.sum(
        lax.all_to_all(jnp.broadcast_to(own_loss, (trainers, 1, NB)), DP, 0, 0, tiled=True),
        axis=(0, 1),
    )
    back = over_parts(back_part, "mp")
    lowered_gradient = (ADAPTER_SCALING * back).astype(jnp.bfloat16)
    grad_down = jnp.dot(lowered_gradient, normed, preferred_element_type=jnp.float32)
    bucket_loss = loss_sum / (floor_counts * width)
    progress = jnp.sum(weights * bucket_loss) / jnp.sum(bucket_loss)
    competence_next = competence + 0.5 * (1.0 - competence) * progress
    return (grad_down[None], grad_up[None], bucket_loss, competence_next)


def solution(mesh):
    split = Mesh(mesh.devices.reshape(4, 8, 2, mesh.shape["mp"]), DP_MP)
    placed = (
        P(DP, None, "mp"),
        P(DP, None, "mp"),
        P(None, "mp"),
        P("mp"),
        P(DP, None, "mp"),
        P(DP, None, "mp"),
        P(DP),
        P(DP),
        P(DP),
        P(DP, None),
        P(),
    )
    return jax.shard_map(
        on_device,
        mesh=split,
        in_specs=placed,
        out_specs=(P(DP, None, "mp"), P(DP, None, "mp"), P(), P()),
        check_vma=False,
    )
```

```python
import jax
import jax.numpy as jnp
from jax import lax
from jax.experimental import pallas as pl
from jax.experimental.pallas import tpu as pltpu
from jax.sharding import Mesh
from jax.sharding import PartitionSpec as P

NB = 16
DP = ("dp_0", "dp_1", "dp_2")
DP_MP = ("dp_0", "dp_1", "dp_2", "mp")

RMS_EPSILON = 1e-05
SHARPNESS = 12.0
ADAPTER_SCALING = 2.0
PER_PAIR = 2
VMEM_BYTES = 62 * 1024 * 1024
CONTRACT_LAST = (((1,), (1,)), ((), ()))
CONTRACT_FIRST = (((0,), (0,)), ((), ()))


def swap(value, axis, distance):
    peers = lax.axis_size(axis)
    return lax.ppermute(value, axis, [(i, i ^ distance) for i in range(peers)])


def over_parts(value, axis):
    pair = value + swap(value, axis, 1)
    return pair + swap(pair, axis, 3)


def from_parts(value, axis, cut):
    near = swap(value, axis, 1)
    other = swap(value, axis, 3)
    return near, other, swap(other[:cut], axis, 1), swap(near[cut:], axis, 3)


def lane_group(packed, group, groups):
    slots = [packed[:, s * groups + group][:, None] for s in range(PER_PAIR)]
    whole = jnp.concatenate(slots, axis=1).astype(jnp.float32)
    return whole.reshape(-1, packed.shape[-1])


def square_kernel(packed, done, total):
    groups = (packed.shape[1] - 1) // PER_PAIR
    sums = None
    for g in range(groups):
        x = lane_group(packed, g, groups)
        sums = x * x if sums is None else sums + x * x
    total[...] = jnp.sum(sums.T, axis=0, keepdims=True) + done[0]


def row_squares(packed, done):
    peers, pieces, block_len, lanes = packed.shape
    rows = peers * PER_PAIR * block_len
    chunk = 16
    return pl.pallas_call(
        square_kernel,
        grid=(peers // chunk,),
        out_shape=jax.ShapeDtypeStruct((1, rows), jnp.float32),
        in_specs=[
            pl.BlockSpec((chunk, pieces, block_len, lanes), lambda i: (i, 0, 0, 0)),
            pl.BlockSpec(memory_space=pltpu.SMEM),
        ],
        out_specs=pl.BlockSpec((1, rows * chunk // peers), lambda i: (0, i)),
        compiler_params=pltpu.CompilerParams(vmem_limit_bytes=VMEM_BYTES),
        cost_estimate=pl.CostEstimate(flops=4 << 20, bytes_accessed=2 << 20, transcendentals=0),
        name="row_squares",
    )(packed, done)


def latent_kernel(packed, squares, gain, down, normed, latent):
    lanes = packed.shape[-1]
    groups = (packed.shape[1] - 1) // PER_PAIR
    inverse = lax.rsqrt(squares[...] + RMS_EPSILON)
    inverse = jnp.broadcast_to(inverse, (lanes, inverse.shape[1])).T
    for g in range(groups):
        at = slice(g * lanes, (g + 1) * lanes)
        x = lane_group(packed, g, groups)
        normed[:, at] = (x * inverse * gain[:, at]).astype(jnp.bfloat16)
    latent[...] = lax.dot_general(
        down[...], normed[...], CONTRACT_LAST, preferred_element_type=jnp.float32
    )


def latents(packed, mean_squares, gain, down):
    peers, pieces, block_len, lanes = packed.shape
    rows = peers * PER_PAIR * block_len
    rank, columns = down.shape
    chunk = 16
    part = rows * chunk // peers
    return pl.pallas_call(
        latent_kernel,
        grid=(peers // chunk,),
        out_shape=(
            jax.ShapeDtypeStruct((rows, columns), jnp.bfloat16),
            jax.ShapeDtypeStruct((rank, rows), jnp.float32),
        ),
        in_specs=[
            pl.BlockSpec((chunk, pieces, block_len, lanes), lambda i: (i, 0, 0, 0)),
            pl.BlockSpec((1, part), lambda i: (0, i)),
            pl.BlockSpec((1, columns), lambda i: (0, 0)),
            pl.BlockSpec((rank, columns), lambda i: (0, 0)),
        ],
        out_specs=(
            pl.BlockSpec((part, columns), lambda i: (i, 0)),
            pl.BlockSpec((rank, part), lambda i: (0, i)),
        ),
        compiler_params=pltpu.CompilerParams(vmem_limit_bytes=VMEM_BYTES),
        cost_estimate=pl.CostEstimate(
            flops=2 * rows * rank * columns, bytes_accessed=4 << 20, transcendentals=rows
        ),
        name="latents",
    )(packed, mean_squares, gain[None, :], down)


def route_kernel(
    ids_in, dest_in, buckets_in, lengths_in, pool_in, gain_in,
    send_out, own_out, slot_of,
    ids, dest, buckets, lengths, pool, gain, send, own, arrived, info, counts, sem,
):
    pairs = (
        (pool_in, pool),
        (ids_in, ids),
        (dest_in, dest),
        (buckets_in, buckets),
        (lengths_in, lengths),
        (gain_in, gain),
    )
    copies = [
        pltpu.make_async_copy(source, target, sem.at[i])
        for i, (source, target) in enumerate(pairs)
    ]
    for copy in copies:
        copy.start()
    sampled = ids.shape[0]
    trainers, pieces, block_len, lanes = send.shape
    groups = (pieces - 1) // PER_PAIR

    def clear(k, carry):
        arrived[k] = 0
        for s in range(PER_PAIR):
            info[s, k] = 0
            info[PER_PAIR + s, k] = 0
        return carry

    def clear_counts(b, carry):
        counts[b] = 0
        return carry

    lax.fori_loop(0, trainers, clear, 0)
    lax.fori_loop(0, NB, clear_counts, 0)
    for copy in copies:
        copy.wait()

    def place(j, carry):
        block = ids[j]
        trainer = dest[j]
        values = pool[block]
        own[j] = values
        order = arrived[trainer]
        arrived[trainer] = order + 1
        slot = trainer * PER_PAIR + order
        for g in range(groups):
            send[trainer, order * groups + g] = values[:, g * lanes : (g + 1) * lanes]
        slot_of[j] = slot
        bucket = buckets[block]
        length = lengths[block]
        info[order, trainer] = bucket
        info[PER_PAIR + order, trainer] = length
        counts[bucket] = counts[bucket] + length
        return carry

    lax.fori_loop(0, sampled, place, 0)

    row = lax.broadcasted_iota(jnp.int32, (block_len, lanes), 0)
    lane = lax.broadcasted_iota(jnp.int32, (block_len, lanes), 1)
    holder = jnp.zeros((block_len, lanes), jnp.int32)
    for b in range(NB):
        count = counts[b]
        holder = jnp.where((row == 1) & (lane == b), count // 16, holder)
        holder = jnp.where((row == 2) & (lane == b), count % 16, holder)

    def finish(k, found):
        for s in range(PER_PAIR):
            free = arrived[k] <= s

            @pl.when(free)
            def _():
                slot_of[sampled + found] = k * PER_PAIR + s
                for g in range(groups):
                    send[k, s * groups + g] = jnp.zeros((block_len, lanes), send.dtype)

            found = found + jnp.where(free, 1, 0)
        facts = holder
        for i in range(2 * PER_PAIR):
            facts = jnp.where((row == 0) & (lane == i), info[i, k], facts)
        send[k, pieces - 1] = facts.astype(jnp.float32).astype(send.dtype)
        return found

    lax.fori_loop(0, trainers, finish, 0)
    send_copy = pltpu.make_async_copy(send, send_out, sem.at[0])
    send_copy.start()
    whole = gain[...]
    high = whole.astype(jnp.bfloat16).astype(jnp.float32)
    middle = (whole - high).astype(jnp.bfloat16).astype(jnp.float32)
    low = whole - high - middle
    zeros = jnp.zeros((own.shape[1] - 3, whole.shape[1]), jnp.float32)
    own[sampled] = jnp.concatenate([high, middle, low, zeros], axis=0).astype(jnp.bfloat16)
    own[sampled + 1] = jnp.zeros(own.shape[1:], own.dtype)
    own_copy = pltpu.make_async_copy(own, own_out, sem.at[1])
    own_copy.start()
    own_copy.wait()
    send_copy.wait()


def route(ids, dest, buckets, lengths, pool, gain, trainers):
    sampled = ids.shape[0]
    slots = trainers * PER_PAIR
    block = pool.shape[1:]
    lanes = 128
    message = (trainers, PER_PAIR * (block[1] // lanes) + 1, block[0], lanes)
    smem = pl.BlockSpec(memory_space=pltpu.SMEM)
    hbm = pl.BlockSpec(memory_space=pltpu.HBM)
    return pl.pallas_call(
        route_kernel,
        out_shape=(
            jax.ShapeDtypeStruct(message, pool.dtype),
            jax.ShapeDtypeStruct((sampled + 2, *block), pool.dtype),
            jax.ShapeDtypeStruct((slots,), jnp.int32),
        ),
        in_specs=[hbm] * 6,
        out_specs=(hbm, hbm, smem),
        scratch_shapes=[
            pltpu.SMEM(ids.shape, jnp.int32),
            pltpu.SMEM(dest.shape, jnp.int32),
            pltpu.SMEM(buckets.shape, jnp.int32),
            pltpu.SMEM(lengths.shape, jnp.int32),
            pltpu.VMEM(pool.shape, pool.dtype),
            pltpu.VMEM((1, gain.shape[0]), jnp.float32),
            pltpu.VMEM(message, pool.dtype),
            pltpu.VMEM((sampled + 2, *block), pool.dtype),
            pltpu.SMEM((trainers,), jnp.int32),
            pltpu.SMEM((2 * PER_PAIR, trainers), jnp.int32),
            pltpu.SMEM((NB,), jnp.int32),
            pltpu.SemaphoreType.DMA((6,)),
        ],
        compiler_params=pltpu.CompilerParams(vmem_limit_bytes=VMEM_BYTES),
        cost_estimate=pl.CostEstimate(flops=0, bytes_accessed=5 << 20, transcendentals=0),
        name="route",
    )(ids, dest, buckets, lengths, pool, gain[None, :])


def early_kernel(ids, own, near, other, targets, apart, squares):
    step = pl.program_id(0)
    chunk, part = near.shape
    lanes = squares.shape[1]
    blocks, block_len, _ = own.shape
    sums = jnp.zeros(squares.shape, jnp.float32)
    for g in range(part // lanes):
        at = slice(g * lanes, (g + 1) * lanes)
        for piece in (own[:, :, at].reshape(chunk, lanes), near[:, at], other[:, at]):
            x = piece.astype(jnp.float32)
            sums = sums + x * x
    squares[...] = sums

    def subtract(j, carry):
        target = targets[ids[step * blocks + j]].astype(jnp.float32)
        apart[j] = own[j].astype(jnp.float32) - target
        return carry

    lax.fori_loop(0, blocks, subtract, 0)


def early_part(ids, own, near, other, targets):
    part = near.shape[1]
    block = own.shape[1:]
    sampled = ids.shape[0]
    rows = sampled * block[0]
    chunk = 128
    blocks = chunk // block[0]
    lanes = 128
    return pl.pallas_call(
        early_kernel,
        grid=(rows // chunk,),
        out_shape=(
            jax.ShapeDtypeStruct((sampled, *block), jnp.float32),
            jax.ShapeDtypeStruct((rows, lanes), jnp.float32),
        ),
        in_specs=[
            pl.BlockSpec(memory_space=pltpu.SMEM),
            pl.BlockSpec((blocks, *block), lambda n: (n, 0, 0)),
            pl.BlockSpec((chunk, part), lambda n: (n, 0)),
            pl.BlockSpec((chunk, part), lambda n: (n, 0)),
            pl.BlockSpec(targets.shape, lambda n: (0, 0, 0)),
        ],
        out_specs=(
            pl.BlockSpec((blocks, *block), lambda n: (n, 0, 0)),
            pl.BlockSpec((chunk, lanes), lambda n: (n, 0)),
        ),
        compiler_params=pltpu.CompilerParams(vmem_limit_bytes=VMEM_BYTES),
        cost_estimate=pl.CostEstimate(flops=6 << 20, bytes_accessed=8 << 20, transcendentals=0),
        name="early_part",
    )(ids, own, near, other, targets)


def gap_kernel(
    slot_of, order, mine, near, other, far_first, far_last,
    mine_gain, near_gain, other_gain, far_gain, squares, apart_in, frozen_in,
    send_out, done, apart, frozen, send, normed, gap, sem,
):
    step = pl.program_id(0)
    chunk, part = mine.shape
    sampled, block_len, columns = gap.shape
    chunks = sampled * block_len // chunk
    tiles, width, tile = frozen.shape
    slots = send.shape[0]
    apart_copy = pltpu.make_async_copy(apart_in, apart, sem.at[0])
    frozen_copies = [
        pltpu.make_async_copy(
            frozen_in.at[:, pl.ds(t * tile, tile)], frozen.at[t], sem.at[1 + t]
        )
        for t in range(tiles)
    ]

    @pl.when(step == 0)
    def _():
        frozen_copies[0].start()
        apart_copy.start()
        for copy in frozen_copies[1:]:
            copy.start()
        done[0] = 0.0

        def fill(s, carry):
            send[slot_of[sampled + s]] = jnp.zeros((block_len, columns), jnp.bfloat16)
            return carry

        lax.fori_loop(0, slots - sampled, fill, 0, unroll=4)

    def normalize(far):
        x = far[...].astype(jnp.float32)
        total = jnp.sum(squares[...], axis=1, keepdims=True)
        total = total + jnp.sum(x * x, axis=1, keepdims=True)
        inverse = lax.rsqrt(total / width + RMS_EPSILON)
        at = pl.ds(pl.multiple_of(step * chunk, chunk), chunk)
        pieces = ((mine, mine_gain), (near, near_gain), (far, far_gain), (other, other_gain))
        for p, (piece, gains) in enumerate(pieces):
            three = gains[...].astype(jnp.float32)
            gain = three[0:1] + three[1:2] + three[2:3]
            to = pl.ds(pl.multiple_of(order[p] * part, part), part)
            x = piece[...].astype(jnp.float32)
            normed[at, to] = (x * inverse * gain).astype(jnp.bfloat16)

    @pl.when(step < chunks // 2)
    def _():
        normalize(far_first)

    @pl.when(step >= chunks // 2)
    def _():
        normalize(far_last)

    @pl.when(step == chunks - 1)
    def _():
        apart_copy.wait()
        for t in range(tiles):
            frozen_copies[t].wait()
            projected = jnp.dot(normed[...], frozen[t], preferred_element_type=jnp.float32)
            at = slice(t * tile, (t + 1) * tile)
            whole = apart[:, :, at] + projected.reshape(sampled, block_len, tile)
            gap[:, :, at] = whole.astype(jnp.bfloat16)

        def place(j, carry):
            send[slot_of[j]] = gap[j]
            return carry

        lax.fori_loop(0, sampled, place, 0, unroll=8)
        copy = pltpu.make_async_copy(send, send_out, sem.at[0])
        copy.start()
        copy.wait()


def base_gap_slots(slot_of, order, own, received, apart, squares, frozen):
    near, other, far_first, far_last = received
    part = near.shape[1]
    width, columns = frozen.shape
    slots = slot_of.shape[0]
    sampled, *block = apart.shape
    rows = sampled * block[0]
    tile = 256
    tiles = columns // tile
    chunk = 128
    chunks = rows // chunk
    half = chunks // 2
    all_rows = pl.BlockSpec((chunk, part), lambda n: (n, 0))
    all_gain = pl.BlockSpec((16, part), lambda n: (rows // 16, 0))
    mine = own.reshape(-1, part)
    smem = pl.BlockSpec(memory_space=pltpu.SMEM)
    hbm = pl.BlockSpec(memory_space=pltpu.HBM)
    return pl.pallas_call(
        gap_kernel,
        grid=(chunks,),
        out_shape=(
            jax.ShapeDtypeStruct((slots, *block), jnp.bfloat16),
            jax.ShapeDtypeStruct((1,), jnp.float32),
        ),
        in_specs=[
            smem,
            smem,
            all_rows,
            all_rows,
            all_rows,
            pl.BlockSpec((chunk, part), lambda n: (jnp.minimum(n, half - 1), 0)),
            pl.BlockSpec((chunk, part), lambda n: (jnp.maximum(n - half, 0), 0)),
            all_gain,
            all_gain,
            all_gain,
            pl.BlockSpec((16, part), lambda n: (rows // 32, 0)),
            pl.BlockSpec((chunk, squares.shape[1]), lambda n: (n, 0)),
            hbm,
            hbm,
        ],
        out_specs=(hbm, smem),
        scratch_shapes=[
            pltpu.VMEM((sampled, *block), jnp.float32),
            pltpu.VMEM((tiles, width, tile), jnp.bfloat16),
            pltpu.VMEM((slots, *block), jnp.bfloat16),
            pltpu.VMEM((rows, width), jnp.bfloat16),
            pltpu.VMEM((sampled, *block), jnp.bfloat16),
            pltpu.SemaphoreType.DMA((1 + tiles,)),
        ],
        compiler_params=pltpu.CompilerParams(vmem_limit_bytes=VMEM_BYTES),
        cost_estimate=pl.CostEstimate(
            flops=2 * rows * width * columns, bytes_accessed=18 << 20, transcendentals=rows
        ),
        name="base_gap",
    )(
        slot_of, order, mine, near, other, far_first, far_last,
        mine, near, other, far_last, squares, apart, frozen,
    )


def trainer_kernel(gap, lowered, up, facts, grad_up, back, loss):
    step = pl.program_id(0)
    low = lowered[...]
    up_map = up[...]
    facts_now = facts[...]
    distance = gap[...].astype(jnp.float32) + lax.dot_general(
        low, up_map, CONTRACT_FIRST, preferred_element_type=jnp.float32
    )
    output_grad = (facts_now[:, NB : NB + 1] * distance).astype(jnp.bfloat16)
    squares = jnp.sum(distance * distance, axis=1, keepdims=True)
    part = jnp.sum(facts_now * squares, axis=0, keepdims=True)
    back[...] = lax.dot_general(
        up_map, output_grad, CONTRACT_LAST, preferred_element_type=jnp.float32
    )
    own = jnp.dot(low, output_grad, preferred_element_type=jnp.float32)

    @pl.when(step == 0)
    def _():
        grad_up[...] = own
        loss[...] = part

    @pl.when(step > 0)
    def _():
        grad_up[...] += own
        loss[...] += part


def trainer_step(gap, lowered, up, facts):
    rows, columns = gap.shape
    rank = up.shape[0]
    lanes = facts.shape[1]
    chunk = 256
    return pl.pallas_call(
        trainer_kernel,
        grid=(rows // chunk,),
        out_shape=(
            jax.ShapeDtypeStruct((rank, columns), jnp.float32),
            jax.ShapeDtypeStruct((rank, rows), jnp.float32),
            jax.ShapeDtypeStruct((1, lanes), jnp.float32),
        ),
        in_specs=[
            pl.BlockSpec((chunk, columns), lambda i: (i, 0)),
            pl.BlockSpec((rank, chunk), lambda i: (0, i)),
            pl.BlockSpec((rank, columns), lambda i: (0, 0)),
            pl.BlockSpec((chunk, lanes), lambda i: (i, 0)),
        ],
        out_specs=(
            pl.BlockSpec((rank, columns), lambda i: (0, 0)),
            pl.BlockSpec((rank, chunk), lambda i: (0, i)),
            pl.BlockSpec((1, lanes), lambda i: (0, 0)),
        ),
        compiler_params=pltpu.CompilerParams(vmem_limit_bytes=VMEM_BYTES),
        cost_estimate=pl.CostEstimate(
            flops=6 * rows * rank * columns, bytes_accessed=4 << 20, transcendentals=0
        ),
        name="trainer_step",
    )(gap, lowered, up, facts)


def on_device(
    pool_inputs,
    pool_targets,
    frozen,
    gain,
    adapter_down,
    adapter_up,
    sample_ids,
    buckets,
    lengths,
    destinations,
    competence,
):
    trainers = lax.axis_size(DP)
    sampled = sample_ids.shape[0]
    _, block_len, part = pool_inputs.shape
    width = frozen.shape[0]
    slots = trainers * PER_PAIR
    rows = slots * block_len
    per_peer = PER_PAIR * block_len
    down_map = adapter_down[0]
    up_map = adapter_up[0]
    bucket_range = jnp.arange(NB, dtype=jnp.int32)

    send_x, own_x, slot_of = route(
        sample_ids, destinations[:, 0], buckets, lengths, pool_inputs, gain, trainers
    )
    got_x = lax.all_to_all(send_x, DP, 0, 0, tiled=True)
    cut = sampled * block_len // 2
    received = from_parts(own_x.reshape(-1, part), "mp", cut)
    order = lax.axis_index("mp") ^ jnp.arange(lax.axis_size("mp"), dtype=jnp.int32)
    apart, near_squares = early_part(
        sample_ids, own_x, received[0], received[1], pool_targets
    )
    send_gap, done = base_gap_slots(
        slot_of, order, own_x, received, apart, near_squares, frozen
    )
    got_gap = lax.all_to_all(
        send_gap.reshape(trainers, per_peer, part), DP, 0, 0, tiled=True
    )

    got_info = got_x[:, -1, 0, : 2 * PER_PAIR].astype(jnp.float32).astype(jnp.int32)
    got_counts = got_x[:, -1, 1:3, :NB].astype(jnp.float32)
    counts = jnp.sum(16.0 * got_counts[:, 0] + got_counts[:, 1], axis=0)
    floor_counts = jnp.maximum(counts, 1.0)
    weights = jax.nn.sigmoid(
        SHARPNESS * (competence[0] - (bucket_range.astype(jnp.float32) + 0.5) / NB)
    )
    row_bucket = jnp.repeat(got_info[:, :PER_PAIR].reshape(slots), block_len)
    row_length = jnp.repeat(got_info[:, PER_PAIR:].reshape(slots), block_len)
    live = (jnp.arange(rows, dtype=jnp.int32) % block_len < row_length).astype(jnp.float32)
    onehot = (row_bucket[:, None] == bucket_range[None, :]).astype(jnp.float32) * live[:, None]
    coefficient = 2.0 * jnp.sum(onehot * (weights / floor_counts)[None, :], axis=1)
    facts = jnp.concatenate(
        [onehot, coefficient[:, None], jnp.zeros((rows, 128 - NB - 1), jnp.float32)], axis=1
    )

    mean_squares = over_parts(row_squares(got_x, done), "mp") / width
    normed, latent_part = latents(got_x, mean_squares, gain, down_map)
    lowered = (ADAPTER_SCALING * over_parts(latent_part, "mp")).astype(jnp.bfloat16)

    grad_up, back_part, loss_part = trainer_step(
        got_gap.reshape(rows, part), lowered, up_map, facts
    )
    everyone = trainers * lax.axis_size("mp")
    loss_sum = jnp.sum(
        lax.all_to_all(
            jnp.broadcast_to(loss_part[:, :NB], (everyone, 1, NB)), DP_MP, 0, 0, tiled=True
        ),
        axis=(0, 1),
    )
    back = over_parts(back_part, "mp")
    lowered_gradient = (ADAPTER_SCALING * back).astype(jnp.bfloat16)
    grad_down = jnp.dot(lowered_gradient, normed, preferred_element_type=jnp.float32)
    bucket_loss = loss_sum / (floor_counts * width)
    progress = jnp.sum(weights * bucket_loss) / jnp.sum(bucket_loss)
    competence_next = competence + 0.5 * (1.0 - competence) * progress
    return (grad_down[None], grad_up[None], bucket_loss, competence_next)


def solution(mesh):
    split = Mesh(mesh.devices.reshape(4, 8, 2, mesh.shape["mp"]), DP_MP)
    placed = (
        P(DP, None, "mp"),
        P(DP, None, "mp"),
        P(None, "mp"),
        P("mp"),
        P(DP, None, "mp"),
        P(DP, None, "mp"),
        P(DP),
        P(DP),
        P(DP),
        P(DP, None),
        P(),
    )
    return jax.shard_map(
        on_device,
        mesh=split,
        in_specs=placed,
        out_specs=(P(DP, None, "mp"), P(DP, None, "mp"), P(), P()),
        check_vma=False,
    )
```

```python
import jax
import jax.numpy as jnp
from jax import lax
from jax.experimental import pallas as pl
from jax.experimental.pallas import tpu as pltpu
from jax.sharding import Mesh
from jax.sharding import PartitionSpec as P

NB = 16
DP = ("dp_0", "dp_1", "dp_2")
DP_MP = ("dp_0", "dp_1", "dp_2", "mp")

RMS_EPSILON = 1e-05
SHARPNESS = 12.0
ADAPTER_SCALING = 2.0
PER_PAIR = 2
TILES = 1
VMEM_BYTES = 62 * 1024 * 1024
CONTRACT_LAST = (((1,), (1,)), ((), ()))
CONTRACT_FIRST = (((0,), (0,)), ((), ()))


def swap(value, axis, distance):
    peers = lax.axis_size(axis)
    return lax.ppermute(value, axis, [(i, i ^ distance) for i in range(peers)])


def over_parts(value, axis):
    pair = value + swap(value, axis, 1)
    return pair + swap(pair, axis, 3)


def from_parts(value, axis, cut):
    near = swap(value, axis, 1)
    other = swap(value, axis, 3)
    return near, other, swap(other[:cut], axis, 1), swap(near[cut:], axis, 3)


def lane_group(packed, group, groups):
    slots = [packed[:, s * groups + group][:, None] for s in range(PER_PAIR)]
    whole = jnp.concatenate(slots, axis=1).astype(jnp.float32)
    return whole.reshape(-1, packed.shape[-1])


def square_kernel(packed, done, total):
    groups = (packed.shape[1] - 1) // PER_PAIR
    sums = None
    for g in range(groups):
        x = lane_group(packed, g, groups)
        sums = x * x if sums is None else sums + x * x
    total[...] = jnp.sum(sums.T, axis=0, keepdims=True) + done[0]


def row_squares(packed, done):
    peers, pieces, block_len, lanes = packed.shape
    rows = peers * PER_PAIR * block_len
    chunk = 16
    return pl.pallas_call(
        square_kernel,
        grid=(peers // chunk,),
        out_shape=jax.ShapeDtypeStruct((1, rows), jnp.float32),
        in_specs=[
            pl.BlockSpec((chunk, pieces, block_len, lanes), lambda i: (i, 0, 0, 0)),
            pl.BlockSpec(memory_space=pltpu.SMEM),
        ],
        out_specs=pl.BlockSpec((1, rows * chunk // peers), lambda i: (0, i)),
        compiler_params=pltpu.CompilerParams(vmem_limit_bytes=VMEM_BYTES),
        cost_estimate=pl.CostEstimate(flops=4 << 20, bytes_accessed=2 << 20, transcendentals=0),
        name="row_squares",
    )(packed, done)


def latent_kernel(packed, squares, gain, down, normed, latent):
    lanes = packed.shape[-1]
    groups = (packed.shape[1] - 1) // PER_PAIR
    inverse = lax.rsqrt(squares[...] + RMS_EPSILON)
    inverse = jnp.broadcast_to(inverse, (lanes, inverse.shape[1])).T
    for g in range(groups):
        at = slice(g * lanes, (g + 1) * lanes)
        x = lane_group(packed, g, groups)
        normed[:, at] = (x * inverse * gain[:, at]).astype(jnp.bfloat16)
    latent[...] = lax.dot_general(
        down[...], normed[...], CONTRACT_LAST, preferred_element_type=jnp.float32
    )


def latents(packed, mean_squares, gain, down):
    peers, pieces, block_len, lanes = packed.shape
    rows = peers * PER_PAIR * block_len
    rank, columns = down.shape
    chunk = 16
    part = rows * chunk // peers
    return pl.pallas_call(
        latent_kernel,
        grid=(peers // chunk,),
        out_shape=(
            jax.ShapeDtypeStruct((rows, columns), jnp.bfloat16),
            jax.ShapeDtypeStruct((rank, rows), jnp.float32),
        ),
        in_specs=[
            pl.BlockSpec((chunk, pieces, block_len, lanes), lambda i: (i, 0, 0, 0)),
            pl.BlockSpec((1, part), lambda i: (0, i)),
            pl.BlockSpec((1, columns), lambda i: (0, 0)),
            pl.BlockSpec((rank, columns), lambda i: (0, 0)),
        ],
        out_specs=(
            pl.BlockSpec((part, columns), lambda i: (i, 0)),
            pl.BlockSpec((rank, part), lambda i: (0, i)),
        ),
        compiler_params=pltpu.CompilerParams(vmem_limit_bytes=VMEM_BYTES),
        cost_estimate=pl.CostEstimate(
            flops=2 * rows * rank * columns, bytes_accessed=4 << 20, transcendentals=rows
        ),
        name="latents",
    )(packed, mean_squares, gain[None, :], down)


def route_kernel(
    ids_in, dest_in, buckets_in, lengths_in, pool_in, gain_in,
    send_out, own_out, slot_of,
    ids, dest, buckets, lengths, pool, gain, send, own, arrived, info, counts, sem,
):
    pairs = (
        (pool_in, pool),
        (ids_in, ids),
        (dest_in, dest),
        (buckets_in, buckets),
        (lengths_in, lengths),
        (gain_in, gain),
    )
    copies = [
        pltpu.make_async_copy(source, target, sem.at[i])
        for i, (source, target) in enumerate(pairs)
    ]
    for copy in copies:
        copy.start()
    sampled = ids.shape[0]
    trainers, pieces, block_len, lanes = send.shape
    groups = (pieces - 1) // PER_PAIR

    def clear(k, carry):
        arrived[k] = 0
        for s in range(PER_PAIR):
            info[s, k] = 0
            info[PER_PAIR + s, k] = 0
        return carry

    def clear_counts(b, carry):
        counts[b] = 0
        return carry

    lax.fori_loop(0, trainers, clear, 0)
    lax.fori_loop(0, NB, clear_counts, 0)
    for copy in copies:
        copy.wait()

    def place(j, carry):
        block = ids[j]
        trainer = dest[j]
        values = pool[block]
        own[j] = values
        order = arrived[trainer]
        arrived[trainer] = order + 1
        slot = trainer * PER_PAIR + order
        for g in range(groups):
            send[trainer, order * groups + g] = values[:, g * lanes : (g + 1) * lanes]
        slot_of[j] = slot
        bucket = buckets[block]
        length = lengths[block]
        info[order, trainer] = bucket
        info[PER_PAIR + order, trainer] = length
        counts[bucket] = counts[bucket] + length
        return carry

    lax.fori_loop(0, sampled, place, 0)

    row = lax.broadcasted_iota(jnp.int32, (block_len, lanes), 0)
    lane = lax.broadcasted_iota(jnp.int32, (block_len, lanes), 1)
    holder = jnp.zeros((block_len, lanes), jnp.int32)
    for b in range(NB):
        count = counts[b]
        holder = jnp.where((row == 1) & (lane == b), count // 16, holder)
        holder = jnp.where((row == 2) & (lane == b), count % 16, holder)

    def finish(k, found):
        for s in range(PER_PAIR):
            free = arrived[k] <= s

            @pl.when(free)
            def _():
                slot_of[sampled + found] = k * PER_PAIR + s
                for g in range(groups):
                    send[k, s * groups + g] = jnp.zeros((block_len, lanes), send.dtype)

            found = found + jnp.where(free, 1, 0)
        facts = holder
        for i in range(2 * PER_PAIR):
            facts = jnp.where((row == 0) & (lane == i), info[i, k], facts)
        send[k, pieces - 1] = facts.astype(jnp.float32).astype(send.dtype)
        return found

    lax.fori_loop(0, trainers, finish, 0)
    send_copy = pltpu.make_async_copy(send, send_out, sem.at[0])
    send_copy.start()
    whole = gain[...]
    high = whole.astype(jnp.bfloat16).astype(jnp.float32)
    middle = (whole - high).astype(jnp.bfloat16).astype(jnp.float32)
    low = whole - high - middle
    zeros = jnp.zeros((own.shape[1] - 3, whole.shape[1]), jnp.float32)
    own[sampled] = jnp.concatenate([high, middle, low, zeros], axis=0).astype(jnp.bfloat16)
    own[sampled + 1] = jnp.zeros(own.shape[1:], own.dtype)
    own_copy = pltpu.make_async_copy(own, own_out, sem.at[1])
    own_copy.start()
    own_copy.wait()
    send_copy.wait()


def route(ids, dest, buckets, lengths, pool, gain, trainers):
    sampled = ids.shape[0]
    slots = trainers * PER_PAIR
    block = pool.shape[1:]
    lanes = 128
    message = (trainers, PER_PAIR * (block[1] // lanes) + 1, block[0], lanes)
    smem = pl.BlockSpec(memory_space=pltpu.SMEM)
    hbm = pl.BlockSpec(memory_space=pltpu.HBM)
    return pl.pallas_call(
        route_kernel,
        out_shape=(
            jax.ShapeDtypeStruct(message, pool.dtype),
            jax.ShapeDtypeStruct((sampled + 2, *block), pool.dtype),
            jax.ShapeDtypeStruct((slots,), jnp.int32),
        ),
        in_specs=[hbm] * 6,
        out_specs=(hbm, hbm, smem),
        scratch_shapes=[
            pltpu.SMEM(ids.shape, jnp.int32),
            pltpu.SMEM(dest.shape, jnp.int32),
            pltpu.SMEM(buckets.shape, jnp.int32),
            pltpu.SMEM(lengths.shape, jnp.int32),
            pltpu.VMEM(pool.shape, pool.dtype),
            pltpu.VMEM((1, gain.shape[0]), jnp.float32),
            pltpu.VMEM(message, pool.dtype),
            pltpu.VMEM((sampled + 2, *block), pool.dtype),
            pltpu.SMEM((trainers,), jnp.int32),
            pltpu.SMEM((2 * PER_PAIR, trainers), jnp.int32),
            pltpu.SMEM((NB,), jnp.int32),
            pltpu.SemaphoreType.DMA((6,)),
        ],
        compiler_params=pltpu.CompilerParams(vmem_limit_bytes=VMEM_BYTES),
        cost_estimate=pl.CostEstimate(flops=0, bytes_accessed=5 << 20, transcendentals=0),
        name="route",
    )(ids, dest, buckets, lengths, pool, gain[None, :])


def early_kernel(ids, own, near, other, targets, taken, squares):
    step = pl.program_id(0)
    chunk, part = near.shape
    lanes = squares.shape[1]
    blocks = own.shape[0]
    sums = jnp.zeros(squares.shape, jnp.float32)
    for g in range(part // lanes):
        at = slice(g * lanes, (g + 1) * lanes)
        for piece in (own[:, :, at].reshape(chunk, lanes), near[:, at], other[:, at]):
            x = piece.astype(jnp.float32)
            sums = sums + x * x
    squares[...] = sums

    def take(j, carry):
        taken[j] = targets[ids[step * blocks + j]]
        return carry

    lax.fori_loop(0, blocks, take, 0, unroll=4)


def early_part(ids, own, near, other, targets):
    part = near.shape[1]
    block = own.shape[1:]
    sampled = ids.shape[0]
    rows = sampled * block[0]
    chunk = 128
    blocks = chunk // block[0]
    lanes = 128
    return pl.pallas_call(
        early_kernel,
        grid=(rows // chunk,),
        out_shape=(
            jax.ShapeDtypeStruct((sampled, *block), jnp.bfloat16),
            jax.ShapeDtypeStruct((rows, lanes), jnp.float32),
        ),
        in_specs=[
            pl.BlockSpec(memory_space=pltpu.SMEM),
            pl.BlockSpec((blocks, *block), lambda n: (n, 0, 0)),
            pl.BlockSpec((chunk, part), lambda n: (n, 0)),
            pl.BlockSpec((chunk, part), lambda n: (n, 0)),
            pl.BlockSpec(targets.shape, lambda n: (0, 0, 0)),
        ],
        out_specs=(
            pl.BlockSpec((blocks, *block), lambda n: (n, 0, 0)),
            pl.BlockSpec((chunk, lanes), lambda n: (n, 0)),
        ),
        compiler_params=pltpu.CompilerParams(vmem_limit_bytes=VMEM_BYTES),
        cost_estimate=pl.CostEstimate(flops=6 << 20, bytes_accessed=7 << 20, transcendentals=0),
        name="early_part",
    )(ids, own, near, other, targets)


def gap_kernel(
    slot_of, order, far_first_in, far_last_in, mine_in, near_in, other_in, squares_in,
    frozen_in, taken_in,
    send_out, done, pieces, squares, frozen, taken, send, normed, total, gap, sem,
):
    parts, _, part = pieces.shape
    sampled, block_len, columns = gap.shape
    rows = sampled * block_len
    cut = far_first_in.shape[0]
    slots = send.shape[0]
    places = (2, 0, 1, 3)
    copies = [
        pltpu.make_async_copy(
            far_first_in, pieces.at[0, pl.ds(0, cut)], sem.at[0]
        ),
        pltpu.make_async_copy(
            far_last_in, pieces.at[0, pl.ds(cut, far_last_in.shape[0])], sem.at[1]
        ),
        pltpu.make_async_copy(squares_in, squares, sem.at[2]),
        pltpu.make_async_copy(mine_in, pieces.at[1], sem.at[3]),
        pltpu.make_async_copy(near_in, pieces.at[2], sem.at[4]),
        pltpu.make_async_copy(other_in, pieces.at[3], sem.at[5]),
        pltpu.make_async_copy(taken_in, taken, sem.at[6]),
    ]
    weights = [
        pltpu.make_async_copy(
            frozen_in.at[pl.ds(pl.multiple_of(order[places[i]] * part, part), part)],
            frozen.at[i],
            sem.at[7 + i],
        )
        for i in range(parts)
    ]
    started = copies[:3] + weights[:1]
    for i in range(1, parts):
        started += [copies[2 + i], weights[i]]
    for copy in started + copies[6:]:
        copy.start()
    done[0] = 0.0

    def fill(s, carry):
        send[slot_of[sampled + s]] = jnp.zeros((block_len, columns), jnp.bfloat16)
        return carry

    lax.fori_loop(0, slots - sampled, fill, 0, unroll=8)
    for copy in copies[:3]:
        copy.wait()
    chunk = 128

    def invert(r):
        at = slice(r * chunk, (r + 1) * chunk)
        x = pieces[0, at].astype(jnp.float32)
        sums = squares[at]
        lanes = sums.shape[1]
        for g in range(part // lanes):
            sums = sums + x[:, g * lanes : (g + 1) * lanes] * x[:, g * lanes : (g + 1) * lanes]
        mean = jnp.sum(sums, axis=1, keepdims=True) / (parts * part)
        squares[at] = jnp.broadcast_to(lax.rsqrt(mean + RMS_EPSILON), sums.shape)

    def normalize(i, r):
        at = slice(r * chunk, (r + 1) * chunk)
        three = pieces[i, rows : rows + 16].astype(jnp.float32)
        gain = three[0:1] + three[1:2] + three[2:3]
        x = pieces[i, at].astype(jnp.float32)
        normed[i, at] = (x * squares[at, 0:1] * gain).astype(jnp.bfloat16)

    chunks = rows // chunk
    for r in range(chunks):
        invert(r)
        normalize(0, r)
    tile = columns // TILES
    for i in range(parts):
        weights[i].wait()
        if i + 1 < parts:
            copies[3 + i].wait()
        else:
            copies[6].wait()
        for n in range(TILES):
            at = slice(n * tile, (n + 1) * tile)
            product = jnp.dot(
                normed[i], frozen[i, :, at], preferred_element_type=jnp.float32
            )
            if i > 0:
                product = total[:, at] + product
            if i + 1 < parts:
                total[:, at] = product
                for r in range(n * chunks // TILES, (n + 1) * chunks // TILES):
                    normalize(i + 1, r)
            else:
                x = pieces[1, :rows, at].astype(jnp.float32)
                whole = (x + product).reshape(sampled, block_len, tile)
                gap[:, :, at] = (whole - taken[:, :, at].astype(jnp.float32)).astype(jnp.bfloat16)

    def place(j, carry):
        send[slot_of[j]] = gap[j]
        return carry

    lax.fori_loop(0, sampled, place, 0, unroll=8)
    copy = pltpu.make_async_copy(send, send_out, sem.at[0])
    copy.start()
    copy.wait()


def base_gap_slots(slot_of, order, own, received, taken, squares, frozen):
    near, other, far_first, far_last = received
    height, part = near.shape
    width, columns = frozen.shape
    slots = slot_of.shape[0]
    sampled, *block = taken.shape
    rows = sampled * block[0]
    parts = width // part
    smem = pl.BlockSpec(memory_space=pltpu.SMEM)
    hbm = pl.BlockSpec(memory_space=pltpu.HBM)
    return pl.pallas_call(
        gap_kernel,
        out_shape=(
            jax.ShapeDtypeStruct((slots, *block), jnp.bfloat16),
            jax.ShapeDtypeStruct((1,), jnp.float32),
        ),
        in_specs=[smem, smem] + [hbm] * 8,
        out_specs=(hbm, smem),
        scratch_shapes=[
            pltpu.VMEM((parts, height, part), jnp.bfloat16),
            pltpu.VMEM(squares.shape, jnp.float32),
            pltpu.VMEM((parts, part, columns), jnp.bfloat16),
            pltpu.VMEM((sampled, *block), jnp.bfloat16),
            pltpu.VMEM((slots, *block), jnp.bfloat16),
            pltpu.VMEM((parts, rows, part), jnp.bfloat16),
            pltpu.VMEM((rows, columns), jnp.float32),
            pltpu.VMEM((sampled, *block), jnp.bfloat16),
            pltpu.SemaphoreType.DMA((7 + parts,)),
        ],
        compiler_params=pltpu.CompilerParams(vmem_limit_bytes=VMEM_BYTES),
        cost_estimate=pl.CostEstimate(
            flops=2 * rows * width * columns, bytes_accessed=18 << 20, transcendentals=rows
        ),
        name="base_gap",
    )(
        slot_of, order, far_first, far_last, own.reshape(-1, part), near, other, squares,
        frozen, taken,
    )


def trainer_kernel(gap, lowered, up, facts, grad_up, back, loss):
    step = pl.program_id(0)
    rank, columns = up.shape
    lanes = facts.shape[1]
    low = lowered[...]
    up_map = up[...]
    facts_now = facts[...]
    distance = gap[...].astype(jnp.float32) + lax.dot_general(
        low, up_map, CONTRACT_FIRST, preferred_element_type=jnp.float32
    )
    output_grad = (facts_now[:, NB : NB + 1] * distance).astype(jnp.bfloat16)
    squares = jnp.sum(distance * distance, axis=1, keepdims=True)
    loss[...] = jnp.zeros(loss.shape, jnp.float32)
    loss[0:1, 0:lanes] = jnp.sum(facts_now * squares, axis=0, keepdims=True)
    back[0:rank] = lax.dot_general(
        up_map, output_grad, CONTRACT_LAST, preferred_element_type=jnp.float32
    )
    back[rank:] = loss[...]
    own = jnp.dot(low, output_grad, preferred_element_type=jnp.float32)

    @pl.when(step == 0)
    def _():
        grad_up[...] = own

    @pl.when(step > 0)
    def _():
        grad_up[...] += own


def trainer_step(gap, lowered, up, facts):
    rows, columns = gap.shape
    rank = up.shape[0]
    lanes = facts.shape[1]
    chunk = 256
    return pl.pallas_call(
        trainer_kernel,
        grid=(rows // chunk,),
        out_shape=(
            jax.ShapeDtypeStruct((rank, columns), jnp.float32),
            jax.ShapeDtypeStruct((rank + 8, rows), jnp.float32),
        ),
        in_specs=[
            pl.BlockSpec((chunk, columns), lambda i: (i, 0)),
            pl.BlockSpec((rank, chunk), lambda i: (0, i)),
            pl.BlockSpec((rank, columns), lambda i: (0, 0)),
            pl.BlockSpec((chunk, lanes), lambda i: (i, 0)),
        ],
        out_specs=(
            pl.BlockSpec((rank, columns), lambda i: (0, 0)),
            pl.BlockSpec((rank + 8, chunk), lambda i: (0, i)),
        ),
        scratch_shapes=[pltpu.VMEM((8, chunk), jnp.float32)],
        compiler_params=pltpu.CompilerParams(vmem_limit_bytes=VMEM_BYTES),
        cost_estimate=pl.CostEstimate(
            flops=6 * rows * rank * columns, bytes_accessed=4 << 20, transcendentals=0
        ),
        name="trainer_step",
    )(gap, lowered, up, facts)


def on_device(
    pool_inputs,
    pool_targets,
    frozen,
    gain,
    adapter_down,
    adapter_up,
    sample_ids,
    buckets,
    lengths,
    destinations,
    competence,
):
    trainers = lax.axis_size(DP)
    sampled = sample_ids.shape[0]
    _, block_len, part = pool_inputs.shape
    width = frozen.shape[0]
    slots = trainers * PER_PAIR
    rows = slots * block_len
    per_peer = PER_PAIR * block_len
    down_map = adapter_down[0]
    up_map = adapter_up[0]
    bucket_range = jnp.arange(NB, dtype=jnp.int32)

    send_x, own_x, slot_of = route(
        sample_ids, destinations[:, 0], buckets, lengths, pool_inputs, gain, trainers
    )
    got_x = lax.all_to_all(send_x, DP, 0, 0, tiled=True)
    cut = sampled * block_len // 2
    received = from_parts(own_x.reshape(-1, part), "mp", cut)
    order = lax.axis_index("mp") ^ jnp.arange(lax.axis_size("mp"), dtype=jnp.int32)
    taken, near_squares = early_part(
        sample_ids, own_x, received[0], received[1], pool_targets
    )
    send_gap, done = base_gap_slots(
        slot_of, order, own_x, received, taken, near_squares, frozen
    )
    got_gap = lax.all_to_all(
        send_gap.reshape(trainers, per_peer, part), DP, 0, 0, tiled=True
    )

    got_info = got_x[:, -1, 0, : 2 * PER_PAIR].astype(jnp.float32).astype(jnp.int32)
    got_counts = got_x[:, -1, 1:3, :NB].astype(jnp.float32)
    counts = jnp.sum(16.0 * got_counts[:, 0] + got_counts[:, 1], axis=0)
    floor_counts = jnp.maximum(counts, 1.0)
    weights = jax.nn.sigmoid(
        SHARPNESS * (competence[0] - (bucket_range.astype(jnp.float32) + 0.5) / NB)
    )
    row_bucket = jnp.repeat(got_info[:, :PER_PAIR].reshape(slots), block_len)
    row_length = jnp.repeat(got_info[:, PER_PAIR:].reshape(slots), block_len)
    live = (jnp.arange(rows, dtype=jnp.int32) % block_len < row_length).astype(jnp.float32)
    onehot = (row_bucket[:, None] == bucket_range[None, :]).astype(jnp.float32) * live[:, None]
    coefficient = 2.0 * jnp.sum(onehot * (weights / floor_counts)[None, :], axis=1)
    facts = jnp.concatenate(
        [onehot, coefficient[:, None], jnp.zeros((rows, 128 - NB - 1), jnp.float32)], axis=1
    )

    mean_squares = over_parts(row_squares(got_x, done), "mp") / width
    normed, latent_part = latents(got_x, mean_squares, gain, down_map)
    lowered = (ADAPTER_SCALING * over_parts(latent_part, "mp")).astype(jnp.bfloat16)

    grad_up, back_part = trainer_step(got_gap.reshape(rows, part), lowered, up_map, facts)
    back = over_parts(back_part, "mp")
    rank = up_map.shape[0]
    own_loss = jnp.sum(back[rank].reshape(-1, 256)[:, :NB], axis=0)
    loss_sum = jnp.sum(
        lax.all_to_all(jnp.broadcast_to(own_loss, (trainers, 1, NB)), DP, 0, 0, tiled=True),
        axis=(0, 1),
    )
    lowered_gradient = (ADAPTER_SCALING * back[:rank]).astype(jnp.bfloat16)
    grad_down = jnp.dot(lowered_gradient, normed, preferred_element_type=jnp.float32)
    bucket_loss = loss_sum / (floor_counts * width)
    progress = jnp.sum(weights * bucket_loss) / jnp.sum(bucket_loss)
    competence_next = competence + 0.5 * (1.0 - competence) * progress
    return (grad_down[None], grad_up[None], bucket_loss, competence_next)


def solution(mesh):
    split = Mesh(mesh.devices.reshape(4, 8, 2, mesh.shape["mp"]), DP_MP)
    placed = (
        P(DP, None, "mp"),
        P(DP, None, "mp"),
        P(None, "mp"),
        P("mp"),
        P(DP, None, "mp"),
        P(DP, None, "mp"),
        P(DP),
        P(DP),
        P(DP),
        P(DP, None),
        P(),
    )
    return jax.shard_map(
        on_device,
        mesh=split,
        in_specs=placed,
        out_specs=(P(DP, None, "mp"), P(DP, None, "mp"), P(), P()),
        check_vma=False,
    )
```

```python
import jax
import jax.numpy as jnp
from jax import lax
from jax.experimental import pallas as pl
from jax.experimental.pallas import tpu as pltpu
from jax.sharding import Mesh
from jax.sharding import PartitionSpec as P

NB = 16
DP = ("dp_0", "dp_1", "dp_2")
DP_MP = ("dp_0", "dp_1", "dp_2", "mp")

RMS_EPSILON = 1e-05
SHARPNESS = 12.0
ADAPTER_SCALING = 2.0
PER_PAIR = 2
TILES = 1
MODEL_PARTS = 4
VMEM_BYTES = 62 * 1024 * 1024
CONTRACT_LAST = (((1,), (1,)), ((), ()))
CONTRACT_FIRST = (((0,), (0,)), ((), ()))


def swap(value, axis, distance):
    peers = lax.axis_size(axis)
    return lax.ppermute(value, axis, [(i, i ^ distance) for i in range(peers)])


def over_parts(value, axis):
    pair = value + swap(value, axis, 1)
    return pair + swap(pair, axis, 3)


def rounded_over_parts(value, sent, axis):
    pair = value + swap(sent, axis, 1).astype(jnp.float32)
    return pair + swap(pair.astype(sent.dtype), axis, 3).astype(jnp.float32)


def from_parts(first, last, axis):
    other_first = swap(first, axis, 3)
    near_last = swap(last, axis, 1)
    near_first = swap(first, axis, 1)
    other_last = swap(last, axis, 3)
    far = (swap(other_first, axis, 1), swap(near_last, axis, 3))
    return (near_first, near_last), (other_first, other_last), far


def lane_group(packed, group, groups):
    slots = [packed[:, s * groups + group][:, None] for s in range(PER_PAIR)]
    whole = jnp.concatenate(slots, axis=1).astype(jnp.float32)
    return whole.reshape(-1, packed.shape[-1])


def square_kernel(packed, done, total):
    groups = (packed.shape[1] - 1) // PER_PAIR
    sums = None
    for g in range(groups):
        x = lane_group(packed, g, groups)
        sums = x * x if sums is None else sums + x * x
    total[...] = jnp.sum(sums.T, axis=0, keepdims=True) + done[0]


def row_squares(packed, done):
    peers, pieces, block_len, lanes = packed.shape
    rows = peers * PER_PAIR * block_len
    chunk = 16
    return pl.pallas_call(
        square_kernel,
        grid=(peers // chunk,),
        out_shape=jax.ShapeDtypeStruct((1, rows), jnp.float32),
        in_specs=[
            pl.BlockSpec((chunk, pieces, block_len, lanes), lambda i: (i, 0, 0, 0)),
            pl.BlockSpec(memory_space=pltpu.SMEM),
        ],
        out_specs=pl.BlockSpec((1, rows * chunk // peers), lambda i: (0, i)),
        compiler_params=pltpu.CompilerParams(vmem_limit_bytes=VMEM_BYTES),
        cost_estimate=pl.CostEstimate(flops=4 << 20, bytes_accessed=2 << 20, transcendentals=0),
        name="row_squares",
    )(packed, done)


def latent_kernel(packed, squares, gain, down, normed, latent):
    lanes = packed.shape[-1]
    groups = (packed.shape[1] - 1) // PER_PAIR
    inverse = lax.rsqrt(squares[...] + RMS_EPSILON)
    inverse = jnp.broadcast_to(inverse, (lanes, inverse.shape[1])).T
    for g in range(groups):
        at = slice(g * lanes, (g + 1) * lanes)
        x = lane_group(packed, g, groups)
        normed[:, at] = (x * inverse * gain[:, at]).astype(jnp.bfloat16)
    latent[...] = lax.dot_general(
        down[...], normed[...], CONTRACT_LAST, preferred_element_type=jnp.float32
    )


def latents(packed, mean_squares, gain, down):
    peers, pieces, block_len, lanes = packed.shape
    rows = peers * PER_PAIR * block_len
    rank, columns = down.shape
    chunk = 16
    part = rows * chunk // peers
    return pl.pallas_call(
        latent_kernel,
        grid=(peers // chunk,),
        out_shape=(
            jax.ShapeDtypeStruct((rows, columns), jnp.bfloat16),
            jax.ShapeDtypeStruct((rank, rows), jnp.float32),
        ),
        in_specs=[
            pl.BlockSpec((chunk, pieces, block_len, lanes), lambda i: (i, 0, 0, 0)),
            pl.BlockSpec((1, part), lambda i: (0, i)),
            pl.BlockSpec((1, columns), lambda i: (0, 0)),
            pl.BlockSpec((rank, columns), lambda i: (0, 0)),
        ],
        out_specs=(
            pl.BlockSpec((part, columns), lambda i: (i, 0)),
            pl.BlockSpec((rank, part), lambda i: (0, i)),
        ),
        compiler_params=pltpu.CompilerParams(vmem_limit_bytes=VMEM_BYTES),
        cost_estimate=pl.CostEstimate(
            flops=2 * rows * rank * columns, bytes_accessed=4 << 20, transcendentals=rows
        ),
        name="latents",
    )(packed, mean_squares, gain[None, :], down)


def route_kernel(
    ids_in, dest_in, buckets_in, lengths_in, pool_in, gain_in,
    send_out, first_out, last_out, slot_of,
    ids, dest, buckets, lengths, pool, gain, send, own, arrived, info, counts, sem,
):
    pairs = (
        (pool_in, pool),
        (ids_in, ids),
        (dest_in, dest),
        (buckets_in, buckets),
        (lengths_in, lengths),
        (gain_in, gain),
    )
    copies = [
        pltpu.make_async_copy(source, target, sem.at[i])
        for i, (source, target) in enumerate(pairs)
    ]
    for copy in copies:
        copy.start()
    sampled = ids.shape[0]
    trainers, pieces, block_len, lanes = send.shape
    groups = (pieces - 1) // PER_PAIR

    def clear(k, carry):
        arrived[k] = 0
        for s in range(PER_PAIR):
            info[s, k] = 0
            info[PER_PAIR + s, k] = 0
        return carry

    def clear_counts(b, carry):
        counts[b] = 0
        return carry

    lax.fori_loop(0, trainers, clear, 0)
    lax.fori_loop(0, NB, clear_counts, 0)
    for copy in copies:
        copy.wait()

    def place(j, carry):
        block = ids[j]
        trainer = dest[j]
        values = pool[block]
        own[j] = values
        order = arrived[trainer]
        arrived[trainer] = order + 1
        slot = trainer * PER_PAIR + order
        for g in range(groups):
            send[trainer, order * groups + g] = values[:, g * lanes : (g + 1) * lanes]
        slot_of[j] = slot
        bucket = buckets[block]
        length = lengths[block]
        info[order, trainer] = bucket
        info[PER_PAIR + order, trainer] = length
        counts[bucket] = counts[bucket] + length
        return carry

    lax.fori_loop(0, sampled, place, 0)

    row = lax.broadcasted_iota(jnp.int32, (block_len, lanes), 0)
    lane = lax.broadcasted_iota(jnp.int32, (block_len, lanes), 1)
    holder = jnp.zeros((block_len, lanes), jnp.int32)
    for b in range(NB):
        count = counts[b]
        holder = jnp.where((row == 1) & (lane == b), count // 16, holder)
        holder = jnp.where((row == 2) & (lane == b), count % 16, holder)

    def finish(k, found):
        for s in range(PER_PAIR):
            free = arrived[k] <= s

            @pl.when(free)
            def _():
                slot_of[sampled + found] = k * PER_PAIR + s
                for g in range(groups):
                    send[k, s * groups + g] = jnp.zeros((block_len, lanes), send.dtype)

            found = found + jnp.where(free, 1, 0)
        facts = holder
        for i in range(2 * PER_PAIR):
            facts = jnp.where((row == 0) & (lane == i), info[i, k], facts)
        send[k, pieces - 1] = facts.astype(jnp.float32).astype(send.dtype)
        return found

    lax.fori_loop(0, trainers, finish, 0)
    send_copy = pltpu.make_async_copy(send, send_out, sem.at[0])
    send_copy.start()
    whole = gain[...]
    high = whole.astype(jnp.bfloat16).astype(jnp.float32)
    middle = (whole - high).astype(jnp.bfloat16).astype(jnp.float32)
    low = whole - high - middle
    zeros = jnp.zeros((own.shape[1] - 3, whole.shape[1]), jnp.float32)
    own[sampled] = jnp.concatenate([high, middle, low, zeros], axis=0).astype(jnp.bfloat16)
    own[sampled + 1] = jnp.zeros(own.shape[1:], own.dtype)
    cut = first_out.shape[0]
    own_copies = (
        pltpu.make_async_copy(own.at[pl.ds(0, cut)], first_out, sem.at[1]),
        pltpu.make_async_copy(own.at[pl.ds(cut, last_out.shape[0])], last_out, sem.at[2]),
    )
    for copy in own_copies:
        copy.start()
    for copy in own_copies:
        copy.wait()
    send_copy.wait()


def route(ids, dest, buckets, lengths, pool, gain, trainers):
    sampled = ids.shape[0]
    slots = trainers * PER_PAIR
    block = pool.shape[1:]
    lanes = 128
    message = (trainers, PER_PAIR * (block[1] // lanes) + 1, block[0], lanes)
    smem = pl.BlockSpec(memory_space=pltpu.SMEM)
    hbm = pl.BlockSpec(memory_space=pltpu.HBM)
    return pl.pallas_call(
        route_kernel,
        out_shape=(
            jax.ShapeDtypeStruct(message, pool.dtype),
            jax.ShapeDtypeStruct((sampled // 2, *block), pool.dtype),
            jax.ShapeDtypeStruct((sampled - sampled // 2 + 2, *block), pool.dtype),
            jax.ShapeDtypeStruct((slots,), jnp.int32),
        ),
        in_specs=[hbm] * 6,
        out_specs=(hbm, hbm, hbm, smem),
        scratch_shapes=[
            pltpu.SMEM(ids.shape, jnp.int32),
            pltpu.SMEM(dest.shape, jnp.int32),
            pltpu.SMEM(buckets.shape, jnp.int32),
            pltpu.SMEM(lengths.shape, jnp.int32),
            pltpu.VMEM(pool.shape, pool.dtype),
            pltpu.VMEM((1, gain.shape[0]), jnp.float32),
            pltpu.VMEM(message, pool.dtype),
            pltpu.VMEM((sampled + 2, *block), pool.dtype),
            pltpu.SMEM((trainers,), jnp.int32),
            pltpu.SMEM((2 * PER_PAIR, trainers), jnp.int32),
            pltpu.SMEM((NB,), jnp.int32),
            pltpu.SemaphoreType.DMA((6,)),
        ],
        compiler_params=pltpu.CompilerParams(vmem_limit_bytes=VMEM_BYTES),
        cost_estimate=pl.CostEstimate(flops=0, bytes_accessed=5 << 20, transcendentals=0),
        name="route",
    )(ids, dest, buckets, lengths, pool, gain[None, :])


def early_kernel(
    ids, mine_first, mine_last, near_first, near_last, other_first, other_last, targets,
    taken, squares,
):
    step = pl.program_id(0)
    half = pl.num_programs(0) // 2
    part = near_first.shape[1]
    lanes = squares.shape[1]
    blocks = taken.shape[0]

    def add_squares(pieces):
        sums = jnp.zeros(squares.shape, jnp.float32)
        for g in range(part // lanes):
            at = slice(g * lanes, (g + 1) * lanes)
            for piece in pieces:
                x = piece[:, at].astype(jnp.float32)
                sums = sums + x * x
        squares[...] = sums

    @pl.when(step < half)
    def _():
        add_squares((mine_first, near_first, other_first))

    @pl.when(step >= half)
    def _():
        add_squares((mine_last, near_last, other_last))

    def take(j, carry):
        taken[j] = targets[ids[step * blocks + j]]
        return carry

    lax.fori_loop(0, blocks, take, 0, unroll=4)


def early_part(ids, mine, near, other, targets):
    part = near[0].shape[1]
    block = targets.shape[1:]
    sampled = ids.shape[0]
    rows = sampled * block[0]
    chunk = 128
    blocks = chunk // block[0]
    half = rows // chunk // 2
    lanes = 128
    first = pl.BlockSpec((chunk, part), lambda n: (jnp.minimum(n, half - 1), 0))
    last = pl.BlockSpec((chunk, part), lambda n: (jnp.maximum(n - half, 0), 0))
    return pl.pallas_call(
        early_kernel,
        grid=(rows // chunk,),
        out_shape=(
            jax.ShapeDtypeStruct((sampled, *block), jnp.bfloat16),
            jax.ShapeDtypeStruct((rows, lanes), jnp.float32),
        ),
        in_specs=[pl.BlockSpec(memory_space=pltpu.SMEM)]
        + [first, last] * 3
        + [pl.BlockSpec(targets.shape, lambda n: (0, 0, 0))],
        out_specs=(
            pl.BlockSpec((blocks, *block), lambda n: (n, 0, 0)),
            pl.BlockSpec((chunk, lanes), lambda n: (n, 0)),
        ),
        compiler_params=pltpu.CompilerParams(vmem_limit_bytes=VMEM_BYTES),
        cost_estimate=pl.CostEstimate(flops=6 << 20, bytes_accessed=7 << 20, transcendentals=0),
        name="early_part",
    )(ids, *mine, *near, *other, targets)


def gap_kernel(
    slot_of, order, far_first, far_last, mine_first, mine_last, near_first, near_last,
    other_first, other_last, squares_in, frozen_in, taken_in,
    send_out, done, pieces, squares, frozen, taken, send, normed, total, gap, sem,
):
    parts, _, part = pieces.shape
    sampled, block_len, columns = gap.shape
    rows = sampled * block_len
    cut = far_first.shape[0]
    slots = send.shape[0]
    places = (2, 0, 1, 3)
    halves = (
        (far_first, far_last),
        (mine_first, mine_last),
        (near_first, near_last),
        (other_first, other_last),
    )
    copies = [
        (
            pltpu.make_async_copy(first, pieces.at[i, pl.ds(0, cut)], sem.at[2 * i]),
            pltpu.make_async_copy(
                last, pieces.at[i, pl.ds(cut, last.shape[0])], sem.at[2 * i + 1]
            ),
        )
        for i, (first, last) in enumerate(halves)
    ]
    squares_copy = pltpu.make_async_copy(squares_in, squares, sem.at[2 * parts])
    taken_copy = pltpu.make_async_copy(taken_in, taken, sem.at[2 * parts + 1])
    weights = [
        pltpu.make_async_copy(
            frozen_in.at[pl.ds(pl.multiple_of(order[places[i]] * part, part), part)],
            frozen.at[i],
            sem.at[2 * parts + 2 + i],
        )
        for i in range(parts)
    ]
    squares_copy.start()
    for i in range(parts):
        for copy in copies[i]:
            copy.start()
        weights[i].start()
    taken_copy.start()
    done[0] = 0.0

    def fill(s, carry):
        send[slot_of[sampled + s]] = jnp.zeros((block_len, columns), jnp.bfloat16)
        return carry

    lax.fori_loop(0, slots - sampled, fill, 0, unroll=8)
    squares_copy.wait()
    for copy in copies[0]:
        copy.wait()
    chunk = 128

    def invert(r):
        at = slice(r * chunk, (r + 1) * chunk)
        x = pieces[0, at].astype(jnp.float32)
        sums = squares[at]
        lanes = sums.shape[1]
        for g in range(part // lanes):
            sums = sums + x[:, g * lanes : (g + 1) * lanes] * x[:, g * lanes : (g + 1) * lanes]
        mean = jnp.sum(sums, axis=1, keepdims=True) / (parts * part)
        squares[at] = jnp.broadcast_to(lax.rsqrt(mean + RMS_EPSILON), sums.shape)

    def normalize(i, r):
        at = slice(r * chunk, (r + 1) * chunk)
        three = pieces[i, rows : rows + 16].astype(jnp.float32)
        gain = three[0:1] + three[1:2] + three[2:3]
        x = pieces[i, at].astype(jnp.float32)
        normed[i, at] = (x * squares[at, 0:1] * gain).astype(jnp.bfloat16)

    chunks = rows // chunk
    for r in range(chunks):
        invert(r)
        normalize(0, r)
    tile = columns // TILES
    for i in range(parts):
        weights[i].wait()
        if i + 1 < parts:
            for copy in copies[i + 1]:
                copy.wait()
        else:
            taken_copy.wait()
        for n in range(TILES):
            at = slice(n * tile, (n + 1) * tile)
            product = jnp.dot(
                normed[i], frozen[i, :, at], preferred_element_type=jnp.float32
            )
            if i > 0:
                product = total[:, at] + product
            if i + 1 < parts:
                total[:, at] = product
                for r in range(n * chunks // TILES, (n + 1) * chunks // TILES):
                    normalize(i + 1, r)
            else:
                x = pieces[1, :rows, at].astype(jnp.float32)
                whole = (x + product).reshape(sampled, block_len, tile)
                gap[:, :, at] = (whole - taken[:, :, at].astype(jnp.float32)).astype(jnp.bfloat16)

    def place(j, carry):
        send[slot_of[j]] = gap[j]
        return carry

    lax.fori_loop(0, sampled, place, 0, unroll=8)
    copy = pltpu.make_async_copy(send, send_out, sem.at[0])
    copy.start()
    copy.wait()


def base_gap_slots(slot_of, order, mine, near, other, far, taken, squares, frozen):
    part = mine[0].shape[1]
    height = mine[0].shape[0] + mine[1].shape[0]
    width, columns = frozen.shape
    slots = slot_of.shape[0]
    sampled, *block = taken.shape
    rows = sampled * block[0]
    parts = width // part
    smem = pl.BlockSpec(memory_space=pltpu.SMEM)
    hbm = pl.BlockSpec(memory_space=pltpu.HBM)
    return pl.pallas_call(
        gap_kernel,
        out_shape=(
            jax.ShapeDtypeStruct((slots, *block), jnp.bfloat16),
            jax.ShapeDtypeStruct((1,), jnp.float32),
        ),
        in_specs=[smem, smem] + [hbm] * 11,
        out_specs=(hbm, smem),
        scratch_shapes=[
            pltpu.VMEM((parts, height, part), jnp.bfloat16),
            pltpu.VMEM(squares.shape, jnp.float32),
            pltpu.VMEM((parts, part, columns), jnp.bfloat16),
            pltpu.VMEM((sampled, *block), jnp.bfloat16),
            pltpu.VMEM((slots, *block), jnp.bfloat16),
            pltpu.VMEM((parts, rows, part), jnp.bfloat16),
            pltpu.VMEM((rows, columns), jnp.float32),
            pltpu.VMEM((sampled, *block), jnp.bfloat16),
            pltpu.SemaphoreType.DMA((3 * parts + 2,)),
        ],
        compiler_params=pltpu.CompilerParams(vmem_limit_bytes=VMEM_BYTES),
        cost_estimate=pl.CostEstimate(
            flops=2 * rows * width * columns, bytes_accessed=18 << 20, transcendentals=rows
        ),
        name="base_gap",
    )(
        slot_of, order, *far, *mine, *near, *other, squares, frozen, taken,
    )


def trainer_kernel(gap, lowered, up, facts, grad_up, back, sent, loss):
    step = pl.program_id(0)
    low = lowered[...]
    up_map = up[...]
    facts_now = facts[...]
    distance = gap[...].astype(jnp.float32) + lax.dot_general(
        low, up_map, CONTRACT_FIRST, preferred_element_type=jnp.float32
    )
    output_grad = (facts_now[:, NB : NB + 1] * distance).astype(jnp.bfloat16)
    squares = jnp.sum(distance * distance, axis=1, keepdims=True)
    part = jnp.sum(facts_now * squares, axis=0, keepdims=True)
    back_now = lax.dot_general(
        up_map, output_grad, CONTRACT_LAST, preferred_element_type=jnp.float32
    )
    back[...] = back_now
    sent[...] = back_now.astype(jnp.bfloat16)
    own = jnp.dot(low, output_grad, preferred_element_type=jnp.float32)

    @pl.when(step == 0)
    def _():
        grad_up[...] = own
        loss[...] = part

    @pl.when(step > 0)
    def _():
        grad_up[...] += own
        loss[...] += part


def trainer_step(gap, lowered, up, facts):
    rows, columns = gap.shape
    rank = up.shape[0]
    lanes = facts.shape[1]
    chunk = 256
    return pl.pallas_call(
        trainer_kernel,
        grid=(rows // chunk,),
        out_shape=(
            jax.ShapeDtypeStruct((rank, columns), jnp.float32),
            jax.ShapeDtypeStruct((rank, rows), jnp.float32),
            jax.ShapeDtypeStruct((rank, rows), jnp.bfloat16),
            jax.ShapeDtypeStruct((1, lanes), jnp.float32),
        ),
        in_specs=[
            pl.BlockSpec((chunk, columns), lambda i: (i, 0)),
            pl.BlockSpec((rank, chunk), lambda i: (0, i)),
            pl.BlockSpec((rank, columns), lambda i: (0, 0)),
            pl.BlockSpec((chunk, lanes), lambda i: (i, 0)),
        ],
        out_specs=(
            pl.BlockSpec((rank, columns), lambda i: (0, 0)),
            pl.BlockSpec((rank, chunk), lambda i: (0, i)),
            pl.BlockSpec((rank, chunk), lambda i: (0, i)),
            pl.BlockSpec((1, lanes), lambda i: (0, 0)),
        ),
        compiler_params=pltpu.CompilerParams(vmem_limit_bytes=VMEM_BYTES),
        cost_estimate=pl.CostEstimate(
            flops=6 * rows * rank * columns, bytes_accessed=4 << 20, transcendentals=0
        ),
        name="trainer_step",
    )(gap, lowered, up, facts)


def down_kernel(back, normed, floor_counts, grad_down, denominators):
    lowered_gradient = (ADAPTER_SCALING * back[...]).astype(jnp.bfloat16)
    grad_down[...] = jnp.dot(
        lowered_gradient, normed[...], preferred_element_type=jnp.float32
    )
    denominators[...] = floor_counts[...] * MODEL_PARTS * normed.shape[1]


def down_step(back, normed, floor_counts):
    rank, rows = back.shape
    columns = normed.shape[1]
    vmem = pl.BlockSpec(memory_space=pltpu.VMEM)
    return pl.pallas_call(
        down_kernel,
        out_shape=(
            jax.ShapeDtypeStruct((rank, columns), jnp.float32),
            jax.ShapeDtypeStruct((1, floor_counts.shape[0]), jnp.float32),
        ),
        in_specs=[vmem] * 3,
        out_specs=(vmem, vmem),
        compiler_params=pltpu.CompilerParams(vmem_limit_bytes=VMEM_BYTES),
        cost_estimate=pl.CostEstimate(
            flops=2 * rows * rank * columns, bytes_accessed=3 << 20, transcendentals=0
        ),
        name="down_step",
    )(back, normed, floor_counts[None, :])


def on_device(
    pool_inputs,
    pool_targets,
    frozen,
    gain,
    adapter_down,
    adapter_up,
    sample_ids,
    buckets,
    lengths,
    destinations,
    competence,
):
    trainers = lax.axis_size(DP)
    sampled = sample_ids.shape[0]
    _, block_len, part = pool_inputs.shape
    width = frozen.shape[0]
    slots = trainers * PER_PAIR
    rows = slots * block_len
    per_peer = PER_PAIR * block_len
    down_map = adapter_down[0]
    up_map = adapter_up[0]
    bucket_range = jnp.arange(NB, dtype=jnp.int32)

    send_x, own_first, own_last, slot_of = route(
        sample_ids, destinations[:, 0], buckets, lengths, pool_inputs, gain, trainers
    )
    got_x = lax.all_to_all(send_x, DP, 0, 0, tiled=True)
    mine = (own_first.reshape(-1, part), own_last.reshape(-1, part))
    near, other, far = from_parts(*mine, "mp")
    order = lax.axis_index("mp") ^ jnp.arange(lax.axis_size("mp"), dtype=jnp.int32)
    taken, near_squares = early_part(sample_ids, mine, near, other, pool_targets)
    send_gap, done = base_gap_slots(
        slot_of, order, mine, near, other, far, taken, near_squares, frozen
    )
    got_gap = lax.all_to_all(
        send_gap.reshape(trainers, per_peer, part), DP, 0, 0, tiled=True
    )

    got_info = got_x[:, -1, 0, : 2 * PER_PAIR].astype(jnp.float32).astype(jnp.int32)
    got_counts = got_x[:, -1, 1:3, :NB].astype(jnp.float32)
    counts = jnp.sum(16.0 * got_counts[:, 0] + got_counts[:, 1], axis=0)
    floor_counts = jnp.maximum(counts, 1.0)
    weights = jax.nn.sigmoid(
        SHARPNESS * (competence[0] - (bucket_range.astype(jnp.float32) + 0.5) / NB)
    )
    row_bucket = jnp.repeat(got_info[:, :PER_PAIR].reshape(slots), block_len)
    row_length = jnp.repeat(got_info[:, PER_PAIR:].reshape(slots), block_len)
    live = (jnp.arange(rows, dtype=jnp.int32) % block_len < row_length).astype(jnp.float32)
    onehot = (row_bucket[:, None] == bucket_range[None, :]).astype(jnp.float32) * live[:, None]
    coefficient = 2.0 * jnp.sum(onehot * (weights / floor_counts)[None, :], axis=1)
    facts = jnp.concatenate(
        [onehot, coefficient[:, None], jnp.zeros((rows, 128 - NB - 1), jnp.float32)], axis=1
    )

    mean_squares = over_parts(row_squares(got_x, done), "mp") / width
    normed, latent_part = latents(got_x, mean_squares, gain, down_map)
    lowered = (ADAPTER_SCALING * over_parts(latent_part, "mp")).astype(jnp.bfloat16)

    grad_up, back_part, back_sent, loss_part = trainer_step(
        got_gap.reshape(rows, part), lowered, up_map, facts
    )
    own_loss = over_parts(loss_part, "mp")[:, :NB]
    loss_sum = jnp.sum(
        lax.all_to_all(jnp.broadcast_to(own_loss, (trainers, 1, NB)), DP, 0, 0, tiled=True),
        axis=(0, 1),
    )
    back = rounded_over_parts(back_part, back_sent, "mp")
    grad_down, denominators = down_step(back, normed, floor_counts)
    bucket_loss = loss_sum / denominators[0]
    progress = jnp.sum(weights * bucket_loss) / jnp.sum(bucket_loss)
    competence_next = competence + 0.5 * (1.0 - competence) * progress
    return (grad_down[None], grad_up[None], bucket_loss, competence_next)


def solution(mesh):
    split = Mesh(mesh.devices.reshape(4, 8, 2, mesh.shape["mp"]), DP_MP)
    placed = (
        P(DP, None, "mp"),
        P(DP, None, "mp"),
        P(None, "mp"),
        P("mp"),
        P(DP, None, "mp"),
        P(DP, None, "mp"),
        P(DP),
        P(DP),
        P(DP),
        P(DP, None),
        P(),
    )
    return jax.shard_map(
        on_device,
        mesh=split,
        in_specs=placed,
        out_specs=(P(DP, None, "mp"), P(DP, None, "mp"), P(), P()),
        check_vma=False,
    )
```

```python
import jax
import jax.numpy as jnp
from jax import lax
from jax.experimental import pallas as pl
from jax.experimental.pallas import tpu as pltpu
from jax.sharding import Mesh
from jax.sharding import PartitionSpec as P

NB = 16
DP = ("dp_0", "dp_1", "dp_2")
DP_MP = ("dp_0", "dp_1", "dp_2", "mp")

RMS_EPSILON = 1e-05
SHARPNESS = 12.0
ADAPTER_SCALING = 2.0
PER_PAIR = 2
TILES = 1
LAST_CHUNK = 256
VMEM_BYTES = 62 * 1024 * 1024
CONTRACT_LAST = (((1,), (1,)), ((), ()))
CONTRACT_FIRST = (((0,), (0,)), ((), ()))


def swap(value, axis, distance):
    peers = lax.axis_size(axis)
    return lax.ppermute(value, axis, [(i, i ^ distance) for i in range(peers)])


def over_parts(value, axis):
    pair = value + swap(value, axis, 1)
    return pair + swap(pair, axis, 3)


def in_three(row, height):
    high = row.astype(jnp.bfloat16).astype(jnp.float32)
    middle = (row - high).astype(jnp.bfloat16).astype(jnp.float32)
    low = row - high - middle
    zeros = jnp.zeros((height - 3, row.shape[1]), jnp.float32)
    return jnp.concatenate([high, middle, low, zeros], axis=0).astype(jnp.bfloat16)


def from_parts(first, last, axis):
    other_first = swap(first, axis, 3)
    near_last = swap(last, axis, 1)
    near_first = swap(first, axis, 1)
    other_last = swap(last, axis, 3)
    far = (swap(other_first, axis, 1), swap(near_last, axis, 3))
    return (near_first, near_last), (other_first, other_last), far


def lane_group(packed, group, groups):
    slots = [packed[:, s * groups + group][:, None] for s in range(PER_PAIR)]
    whole = jnp.concatenate(slots, axis=1).astype(jnp.float32)
    return whole.reshape(-1, packed.shape[-1])


def square_kernel(packed, done, total):
    groups = (packed.shape[1] - 1) // PER_PAIR
    sums = None
    for g in range(groups):
        x = lane_group(packed, g, groups)
        sums = x * x if sums is None else sums + x * x
    total[...] = jnp.sum(sums.T, axis=0, keepdims=True) + done[0]


def row_squares(packed, done):
    peers, pieces, block_len, lanes = packed.shape
    rows = peers * PER_PAIR * block_len
    chunk = 16
    return pl.pallas_call(
        square_kernel,
        grid=(peers // chunk,),
        out_shape=jax.ShapeDtypeStruct((1, rows), jnp.float32),
        in_specs=[
            pl.BlockSpec((chunk, pieces, block_len, lanes), lambda i: (i, 0, 0, 0)),
            pl.BlockSpec(memory_space=pltpu.SMEM),
        ],
        out_specs=pl.BlockSpec((1, rows * chunk // peers), lambda i: (0, i)),
        compiler_params=pltpu.CompilerParams(vmem_limit_bytes=VMEM_BYTES),
        cost_estimate=pl.CostEstimate(flops=4 << 20, bytes_accessed=2 << 20, transcendentals=0),
        name="row_squares",
    )(packed, done)


def latent_kernel(packed, squares, gain, down, normed, latent):
    lanes = packed.shape[-1]
    groups = (packed.shape[1] - 1) // PER_PAIR
    inverse = lax.rsqrt(squares[...] + RMS_EPSILON)
    inverse = jnp.broadcast_to(inverse, (lanes, inverse.shape[1])).T
    for g in range(groups):
        at = slice(g * lanes, (g + 1) * lanes)
        x = lane_group(packed, g, groups)
        normed[:, at] = (x * inverse * gain[:, at]).astype(jnp.bfloat16)
    latent[...] = lax.dot_general(
        down[...], normed[...], CONTRACT_LAST, preferred_element_type=jnp.float32
    )


def latents(packed, mean_squares, gain, down):
    peers, pieces, block_len, lanes = packed.shape
    rows = peers * PER_PAIR * block_len
    rank, columns = down.shape
    chunk = 16
    part = rows * chunk // peers
    return pl.pallas_call(
        latent_kernel,
        grid=(peers // chunk,),
        out_shape=(
            jax.ShapeDtypeStruct((rows, columns), jnp.bfloat16),
            jax.ShapeDtypeStruct((rank, rows), jnp.float32),
        ),
        in_specs=[
            pl.BlockSpec((chunk, pieces, block_len, lanes), lambda i: (i, 0, 0, 0)),
            pl.BlockSpec((1, part), lambda i: (0, i)),
            pl.BlockSpec((1, columns), lambda i: (0, 0)),
            pl.BlockSpec((rank, columns), lambda i: (0, 0)),
        ],
        out_specs=(
            pl.BlockSpec((part, columns), lambda i: (i, 0)),
            pl.BlockSpec((rank, part), lambda i: (0, i)),
        ),
        compiler_params=pltpu.CompilerParams(vmem_limit_bytes=VMEM_BYTES),
        cost_estimate=pl.CostEstimate(
            flops=2 * rows * rank * columns, bytes_accessed=4 << 20, transcendentals=rows
        ),
        name="latents",
    )(packed, mean_squares, gain[None, :], down)


def route_kernel(
    ids_in, dest_in, buckets_in, lengths_in, pool_in, gain_in,
    send_out, first_out, last_out, slot_of,
    ids, dest, buckets, lengths, pool, gain, send, own, arrived, info, counts, sem,
):
    pairs = (
        (pool_in, pool),
        (ids_in, ids),
        (dest_in, dest),
        (buckets_in, buckets),
        (lengths_in, lengths),
        (gain_in, gain),
    )
    copies = [
        pltpu.make_async_copy(source, target, sem.at[i])
        for i, (source, target) in enumerate(pairs)
    ]
    for copy in copies:
        copy.start()
    sampled = ids.shape[0]
    trainers, pieces, block_len, lanes = send.shape
    groups = (pieces - 1) // PER_PAIR

    def clear(k, carry):
        arrived[k] = 0
        for s in range(PER_PAIR):
            info[s, k] = 0
            info[PER_PAIR + s, k] = 0
        return carry

    def clear_counts(b, carry):
        counts[b] = 0
        return carry

    lax.fori_loop(0, trainers, clear, 0)
    lax.fori_loop(0, NB, clear_counts, 0)
    for copy in copies:
        copy.wait()

    def place(j, carry):
        block = ids[j]
        trainer = dest[j]
        values = pool[block]
        own[j] = values
        order = arrived[trainer]
        arrived[trainer] = order + 1
        slot = trainer * PER_PAIR + order
        for g in range(groups):
            send[trainer, order * groups + g] = values[:, g * lanes : (g + 1) * lanes]
        slot_of[j] = slot
        bucket = buckets[block]
        length = lengths[block]
        info[order, trainer] = bucket
        info[PER_PAIR + order, trainer] = length
        counts[bucket] = counts[bucket] + length
        return carry

    lax.fori_loop(0, sampled, place, 0)

    row = lax.broadcasted_iota(jnp.int32, (block_len, lanes), 0)
    lane = lax.broadcasted_iota(jnp.int32, (block_len, lanes), 1)
    holder = jnp.zeros((block_len, lanes), jnp.int32)
    for b in range(NB):
        count = counts[b]
        holder = jnp.where((row == 1) & (lane == b), count // 16, holder)
        holder = jnp.where((row == 2) & (lane == b), count % 16, holder)

    def finish(k, found):
        for s in range(PER_PAIR):
            free = arrived[k] <= s

            @pl.when(free)
            def _():
                slot_of[sampled + found] = k * PER_PAIR + s
                for g in range(groups):
                    send[k, s * groups + g] = jnp.zeros((block_len, lanes), send.dtype)

            found = found + jnp.where(free, 1, 0)
        facts = holder
        for i in range(2 * PER_PAIR):
            facts = jnp.where((row == 0) & (lane == i), info[i, k], facts)
        send[k, pieces - 1] = facts.astype(jnp.float32).astype(send.dtype)
        return found

    lax.fori_loop(0, trainers, finish, 0)
    send_copy = pltpu.make_async_copy(send, send_out, sem.at[0])
    send_copy.start()
    whole = gain[...]
    high = whole.astype(jnp.bfloat16).astype(jnp.float32)
    middle = (whole - high).astype(jnp.bfloat16).astype(jnp.float32)
    low = whole - high - middle
    zeros = jnp.zeros((own.shape[1] - 3, whole.shape[1]), jnp.float32)
    own[sampled] = jnp.concatenate([high, middle, low, zeros], axis=0).astype(jnp.bfloat16)
    own[sampled + 1] = jnp.zeros(own.shape[1:], own.dtype)
    cut = first_out.shape[0]
    own_copies = (
        pltpu.make_async_copy(own.at[pl.ds(0, cut)], first_out, sem.at[1]),
        pltpu.make_async_copy(own.at[pl.ds(cut, last_out.shape[0])], last_out, sem.at[2]),
    )
    for copy in own_copies:
        copy.start()
    for copy in own_copies:
        copy.wait()
    send_copy.wait()


def route(ids, dest, buckets, lengths, pool, gain, trainers):
    sampled = ids.shape[0]
    slots = trainers * PER_PAIR
    block = pool.shape[1:]
    lanes = 128
    message = (trainers, PER_PAIR * (block[1] // lanes) + 1, block[0], lanes)
    smem = pl.BlockSpec(memory_space=pltpu.SMEM)
    hbm = pl.BlockSpec(memory_space=pltpu.HBM)
    return pl.pallas_call(
        route_kernel,
        out_shape=(
            jax.ShapeDtypeStruct(message, pool.dtype),
            jax.ShapeDtypeStruct((sampled // 2, *block), pool.dtype),
            jax.ShapeDtypeStruct((sampled - sampled // 2 + 2, *block), pool.dtype),
            jax.ShapeDtypeStruct((slots,), jnp.int32),
        ),
        in_specs=[hbm] * 6,
        out_specs=(hbm, hbm, hbm, smem),
        scratch_shapes=[
            pltpu.SMEM(ids.shape, jnp.int32),
            pltpu.SMEM(dest.shape, jnp.int32),
            pltpu.SMEM(buckets.shape, jnp.int32),
            pltpu.SMEM(lengths.shape, jnp.int32),
            pltpu.VMEM(pool.shape, pool.dtype),
            pltpu.VMEM((1, gain.shape[0]), jnp.float32),
            pltpu.VMEM(message, pool.dtype),
            pltpu.VMEM((sampled + 2, *block), pool.dtype),
            pltpu.SMEM((trainers,), jnp.int32),
            pltpu.SMEM((2 * PER_PAIR, trainers), jnp.int32),
            pltpu.SMEM((NB,), jnp.int32),
            pltpu.SemaphoreType.DMA((6,)),
        ],
        compiler_params=pltpu.CompilerParams(vmem_limit_bytes=VMEM_BYTES),
        cost_estimate=pl.CostEstimate(flops=0, bytes_accessed=5 << 20, transcendentals=0),
        name="route",
    )(ids, dest, buckets, lengths, pool, gain[None, :])


def early_kernel(
    ids, mine_first, mine_last, near_first, near_last, other_first, other_last, targets,
    taken, squares,
):
    step = pl.program_id(0)
    half = pl.num_programs(0) // 2
    part = near_first.shape[1]
    lanes = squares.shape[1]
    blocks = taken.shape[0]

    def add_squares(pieces):
        sums = jnp.zeros(squares.shape, jnp.float32)
        for g in range(part // lanes):
            at = slice(g * lanes, (g + 1) * lanes)
            for piece in pieces:
                x = piece[:, at].astype(jnp.float32)
                sums = sums + x * x
        squares[...] = sums

    @pl.when(step < half)
    def _():
        add_squares((mine_first, near_first, other_first))

    @pl.when(step >= half)
    def _():
        add_squares((mine_last, near_last, other_last))

    def take(j, carry):
        taken[j] = targets[ids[step * blocks + j]]
        return carry

    lax.fori_loop(0, blocks, take, 0, unroll=4)


def early_part(ids, mine, near, other, targets):
    part = near[0].shape[1]
    block = targets.shape[1:]
    sampled = ids.shape[0]
    rows = sampled * block[0]
    chunk = 128
    blocks = chunk // block[0]
    half = rows // chunk // 2
    lanes = 128
    first = pl.BlockSpec((chunk, part), lambda n: (jnp.minimum(n, half - 1), 0))
    last = pl.BlockSpec((chunk, part), lambda n: (jnp.maximum(n - half, 0), 0))
    return pl.pallas_call(
        early_kernel,
        grid=(rows // chunk,),
        out_shape=(
            jax.ShapeDtypeStruct((sampled, *block), jnp.bfloat16),
            jax.ShapeDtypeStruct((rows, lanes), jnp.float32),
        ),
        in_specs=[pl.BlockSpec(memory_space=pltpu.SMEM)]
        + [first, last] * 3
        + [pl.BlockSpec(targets.shape, lambda n: (0, 0, 0))],
        out_specs=(
            pl.BlockSpec((blocks, *block), lambda n: (n, 0, 0)),
            pl.BlockSpec((chunk, lanes), lambda n: (n, 0)),
        ),
        compiler_params=pltpu.CompilerParams(vmem_limit_bytes=VMEM_BYTES),
        cost_estimate=pl.CostEstimate(flops=6 << 20, bytes_accessed=7 << 20, transcendentals=0),
        name="early_part",
    )(ids, *mine, *near, *other, targets)


def gap_kernel(
    slot_of, order, far_first, far_last, mine_first, mine_last, near_first, near_last,
    other_first, other_last, squares_in, frozen_in, taken_in,
    send_out, done, pieces, squares, frozen, taken, send, normed, total, gap, sem,
):
    parts, _, part = pieces.shape
    sampled, block_len, columns = gap.shape
    rows = sampled * block_len
    cut = far_first.shape[0]
    slots = send.shape[0]
    places = (2, 0, 1, 3)
    halves = (
        (far_first, far_last),
        (mine_first, mine_last),
        (near_first, near_last),
        (other_first, other_last),
    )
    copies = [
        (
            pltpu.make_async_copy(first, pieces.at[i, pl.ds(0, cut)], sem.at[2 * i]),
            pltpu.make_async_copy(
                last, pieces.at[i, pl.ds(cut, last.shape[0])], sem.at[2 * i + 1]
            ),
        )
        for i, (first, last) in enumerate(halves)
    ]
    squares_copy = pltpu.make_async_copy(squares_in, squares, sem.at[2 * parts])
    taken_copy = pltpu.make_async_copy(taken_in, taken, sem.at[2 * parts + 1])
    weights = [
        pltpu.make_async_copy(
            frozen_in.at[pl.ds(pl.multiple_of(order[places[i]] * part, part), part)],
            frozen.at[i],
            sem.at[2 * parts + 2 + i],
        )
        for i in range(parts)
    ]
    squares_copy.start()
    for i in range(parts):
        for copy in copies[i]:
            copy.start()
        weights[i].start()
    taken_copy.start()
    done[0] = 0.0

    def fill(s, carry):
        send[slot_of[sampled + s]] = jnp.zeros((block_len, columns), jnp.bfloat16)
        return carry

    lax.fori_loop(0, slots - sampled, fill, 0, unroll=8)
    squares_copy.wait()
    for copy in copies[0]:
        copy.wait()
    chunk = 128

    def invert(r):
        at = slice(r * chunk, (r + 1) * chunk)
        x = pieces[0, at].astype(jnp.float32)
        sums = squares[at]
        lanes = sums.shape[1]
        for g in range(part // lanes):
            sums = sums + x[:, g * lanes : (g + 1) * lanes] * x[:, g * lanes : (g + 1) * lanes]
        mean = jnp.sum(sums, axis=1, keepdims=True) / (parts * part)
        squares[at] = jnp.broadcast_to(lax.rsqrt(mean + RMS_EPSILON), sums.shape)

    def normalize(i, r):
        at = slice(r * chunk, (r + 1) * chunk)
        three = pieces[i, rows : rows + 16].astype(jnp.float32)
        gain = three[0:1] + three[1:2] + three[2:3]
        x = pieces[i, at].astype(jnp.float32)
        normed[i, at] = (x * squares[at, 0:1] * gain).astype(jnp.bfloat16)

    chunks = rows // chunk
    for r in range(chunks):
        invert(r)
        normalize(0, r)
    tile = columns // TILES
    for i in range(parts):
        weights[i].wait()
        if i + 1 < parts:
            for copy in copies[i + 1]:
                copy.wait()
        else:
            taken_copy.wait()
        for n in range(TILES):
            at = slice(n * tile, (n + 1) * tile)
            product = jnp.dot(
                normed[i], frozen[i, :, at], preferred_element_type=jnp.float32
            )
            if i > 0:
                product = total[:, at] + product
            if i + 1 < parts:
                total[:, at] = product
                for r in range(n * chunks // TILES, (n + 1) * chunks // TILES):
                    normalize(i + 1, r)
            else:
                x = pieces[1, :rows, at].astype(jnp.float32)
                whole = (x + product).reshape(sampled, block_len, tile)
                gap[:, :, at] = (whole - taken[:, :, at].astype(jnp.float32)).astype(jnp.bfloat16)

    def place(j, carry):
        send[slot_of[j]] = gap[j]
        return carry

    lax.fori_loop(0, sampled, place, 0, unroll=8)
    copy = pltpu.make_async_copy(send, send_out, sem.at[0])
    copy.start()
    copy.wait()


def base_gap_slots(slot_of, order, mine, near, other, far, taken, squares, frozen):
    part = mine[0].shape[1]
    height = mine[0].shape[0] + mine[1].shape[0]
    width, columns = frozen.shape
    slots = slot_of.shape[0]
    sampled, *block = taken.shape
    rows = sampled * block[0]
    parts = width // part
    smem = pl.BlockSpec(memory_space=pltpu.SMEM)
    hbm = pl.BlockSpec(memory_space=pltpu.HBM)
    return pl.pallas_call(
        gap_kernel,
        out_shape=(
            jax.ShapeDtypeStruct((slots, *block), jnp.bfloat16),
            jax.ShapeDtypeStruct((1,), jnp.float32),
        ),
        in_specs=[smem, smem] + [hbm] * 11,
        out_specs=(hbm, smem),
        scratch_shapes=[
            pltpu.VMEM((parts, height, part), jnp.bfloat16),
            pltpu.VMEM(squares.shape, jnp.float32),
            pltpu.VMEM((parts, part, columns), jnp.bfloat16),
            pltpu.VMEM((sampled, *block), jnp.bfloat16),
            pltpu.VMEM((slots, *block), jnp.bfloat16),
            pltpu.VMEM((parts, rows, part), jnp.bfloat16),
            pltpu.VMEM((rows, columns), jnp.float32),
            pltpu.VMEM((sampled, *block), jnp.bfloat16),
            pltpu.SemaphoreType.DMA((3 * parts + 2,)),
        ],
        compiler_params=pltpu.CompilerParams(vmem_limit_bytes=VMEM_BYTES),
        cost_estimate=pl.CostEstimate(
            flops=2 * rows * width * columns, bytes_accessed=18 << 20, transcendentals=rows
        ),
        name="base_gap",
    )(
        slot_of, order, *far, *mine, *near, *other, squares, frozen, taken,
    )


def trainer_kernel(gap, lowered, up, facts, grad_up, back, sent, loss):
    step = pl.program_id(0)
    low = lowered[...]
    up_map = up[...]
    facts_now = facts[...]
    distance = gap[...].astype(jnp.float32) + lax.dot_general(
        low, up_map, CONTRACT_FIRST, preferred_element_type=jnp.float32
    )
    output_grad = (facts_now[:, NB : NB + 1] * distance).astype(jnp.bfloat16)
    squares = jnp.sum(distance * distance, axis=1, keepdims=True)
    part = jnp.sum(facts_now * squares, axis=0, keepdims=True)
    back_now = lax.dot_general(
        up_map, output_grad, CONTRACT_LAST, preferred_element_type=jnp.float32
    )
    back[...] = back_now
    rank = up_map.shape[0]
    lanes = loss.shape[1]
    sent[0:rank] = back_now.astype(jnp.bfloat16)
    sent[rank:] = jnp.zeros((sent.shape[0] - rank, sent.shape[1]), jnp.bfloat16)
    own = jnp.dot(low, output_grad, preferred_element_type=jnp.float32)

    @pl.when(step == 0)
    def _():
        grad_up[...] = own
        loss[...] = part

    @pl.when(step > 0)
    def _():
        grad_up[...] += own
        loss[...] += part

    @pl.when(step == pl.num_programs(0) - 1)
    def _():
        sent[rank:, 0:lanes] = in_three(loss[...], sent.shape[0] - rank)


def trainer_step(gap, lowered, up, facts):
    rows, columns = gap.shape
    rank = up.shape[0]
    lanes = facts.shape[1]
    chunk = LAST_CHUNK
    return pl.pallas_call(
        trainer_kernel,
        grid=(rows // chunk,),
        out_shape=(
            jax.ShapeDtypeStruct((rank, columns), jnp.float32),
            jax.ShapeDtypeStruct((rank, rows), jnp.float32),
            jax.ShapeDtypeStruct((rank + 16, rows), jnp.bfloat16),
            jax.ShapeDtypeStruct((1, lanes), jnp.float32),
        ),
        in_specs=[
            pl.BlockSpec((chunk, columns), lambda i: (i, 0)),
            pl.BlockSpec((rank, chunk), lambda i: (0, i)),
            pl.BlockSpec((rank, columns), lambda i: (0, 0)),
            pl.BlockSpec((chunk, lanes), lambda i: (i, 0)),
        ],
        out_specs=(
            pl.BlockSpec((rank, columns), lambda i: (0, 0)),
            pl.BlockSpec((rank, chunk), lambda i: (0, i)),
            pl.BlockSpec((rank + 16, chunk), lambda i: (0, i)),
            pl.BlockSpec((1, lanes), lambda i: (0, 0)),
        ),
        compiler_params=pltpu.CompilerParams(vmem_limit_bytes=VMEM_BYTES),
        cost_estimate=pl.CostEstimate(
            flops=6 * rows * rank * columns, bytes_accessed=4 << 20, transcendentals=0
        ),
        name="trainer_step",
    )(gap, lowered, up, facts)


def pair_kernel(back, loss, got, pair, pair_loss, sent):
    rank, rows = back.shape
    lanes = loss.shape[1]
    at = slice(rows - LAST_CHUNK, rows - LAST_CHUNK + lanes)
    total = back[...] + got[0:rank].astype(jnp.float32)
    pair[...] = total
    sent[0:rank] = total.astype(jnp.bfloat16)
    three = got[rank:, at].astype(jnp.float32)
    whole = loss[...] + (three[0:1] + three[1:2] + three[2:3])
    pair_loss[...] = whole
    height = sent.shape[0] - rank
    sent[rank:] = jnp.zeros((height, rows), jnp.bfloat16)
    sent[rank:, at] = in_three(whole, height)


def pair_step(back, loss, got):
    vmem = pl.BlockSpec(memory_space=pltpu.VMEM)
    return pl.pallas_call(
        pair_kernel,
        out_shape=(
            jax.ShapeDtypeStruct(back.shape, jnp.float32),
            jax.ShapeDtypeStruct(loss.shape, jnp.float32),
            jax.ShapeDtypeStruct(got.shape, jnp.bfloat16),
        ),
        in_specs=[vmem] * 3,
        out_specs=(vmem, vmem, vmem),
        compiler_params=pltpu.CompilerParams(vmem_limit_bytes=VMEM_BYTES),
        cost_estimate=pl.CostEstimate(flops=1 << 17, bytes_accessed=1 << 20, transcendentals=0),
        name="pair_step",
    )(back, loss, got)


def down_kernel(pair, got, normed, grad_down):
    rank = pair.shape[0]
    back = pair[...] + got[0:rank].astype(jnp.float32)
    lowered_gradient = (ADAPTER_SCALING * back).astype(jnp.bfloat16)
    grad_down[...] = jnp.dot(
        lowered_gradient, normed[...], preferred_element_type=jnp.float32
    )


def down_step(pair, got, normed):
    rank, rows = pair.shape
    columns = normed.shape[1]
    vmem = pl.BlockSpec(memory_space=pltpu.VMEM)
    return pl.pallas_call(
        down_kernel,
        out_shape=jax.ShapeDtypeStruct((rank, columns), jnp.float32),
        in_specs=[vmem] * 3,
        out_specs=vmem,
        compiler_params=pltpu.CompilerParams(vmem_limit_bytes=VMEM_BYTES),
        cost_estimate=pl.CostEstimate(
            flops=2 * rows * rank * columns, bytes_accessed=3 << 20, transcendentals=0
        ),
        name="down_step",
    )(pair, got, normed)


def on_device(
    pool_inputs,
    pool_targets,
    frozen,
    gain,
    adapter_down,
    adapter_up,
    sample_ids,
    buckets,
    lengths,
    destinations,
    competence,
):
    trainers = lax.axis_size(DP)
    sampled = sample_ids.shape[0]
    _, block_len, part = pool_inputs.shape
    width = frozen.shape[0]
    slots = trainers * PER_PAIR
    rows = slots * block_len
    per_peer = PER_PAIR * block_len
    down_map = adapter_down[0]
    up_map = adapter_up[0]
    bucket_range = jnp.arange(NB, dtype=jnp.int32)

    send_x, own_first, own_last, slot_of = route(
        sample_ids, destinations[:, 0], buckets, lengths, pool_inputs, gain, trainers
    )
    got_x = lax.all_to_all(send_x, DP, 0, 0, tiled=True)
    mine = (own_first.reshape(-1, part), own_last.reshape(-1, part))
    near, other, far = from_parts(*mine, "mp")
    order = lax.axis_index("mp") ^ jnp.arange(lax.axis_size("mp"), dtype=jnp.int32)
    taken, near_squares = early_part(sample_ids, mine, near, other, pool_targets)
    send_gap, done = base_gap_slots(
        slot_of, order, mine, near, other, far, taken, near_squares, frozen
    )
    got_gap = lax.all_to_all(
        send_gap.reshape(trainers, per_peer, part), DP, 0, 0, tiled=True
    )

    got_info = got_x[:, -1, 0, : 2 * PER_PAIR].astype(jnp.float32).astype(jnp.int32)
    got_counts = got_x[:, -1, 1:3, :NB].astype(jnp.float32)
    counts = jnp.sum(16.0 * got_counts[:, 0] + got_counts[:, 1], axis=0)
    floor_counts = jnp.maximum(counts, 1.0)
    weights = jax.nn.sigmoid(
        SHARPNESS * (competence[0] - (bucket_range.astype(jnp.float32) + 0.5) / NB)
    )
    row_bucket = jnp.repeat(got_info[:, :PER_PAIR].reshape(slots), block_len)
    row_length = jnp.repeat(got_info[:, PER_PAIR:].reshape(slots), block_len)
    live = (jnp.arange(rows, dtype=jnp.int32) % block_len < row_length).astype(jnp.float32)
    onehot = (row_bucket[:, None] == bucket_range[None, :]).astype(jnp.float32) * live[:, None]
    coefficient = 2.0 * jnp.sum(onehot * (weights / floor_counts)[None, :], axis=1)
    facts = jnp.concatenate(
        [onehot, coefficient[:, None], jnp.zeros((rows, 128 - NB - 1), jnp.float32)], axis=1
    )

    mean_squares = over_parts(row_squares(got_x, done), "mp") / width
    normed, latent_part = latents(got_x, mean_squares, gain, down_map)
    lowered = (ADAPTER_SCALING * over_parts(latent_part, "mp")).astype(jnp.bfloat16)

    grad_up, back_part, back_sent, loss_part = trainer_step(
        got_gap.reshape(rows, part), lowered, up_map, facts
    )
    pair, pair_loss, pair_sent = pair_step(back_part, loss_part, swap(back_sent, "mp", 1))
    got_pair = swap(pair_sent, "mp", 3)
    rank = up_map.shape[0]
    at = rows - LAST_CHUNK
    three = got_pair[rank : rank + 3, at : at + NB].astype(jnp.float32)
    own_loss = pair_loss[0, :NB] + (three[0] + three[1] + three[2])
    loss_sum = jnp.sum(
        lax.all_to_all(jnp.broadcast_to(own_loss, (trainers, 1, NB)), DP, 0, 0, tiled=True),
        axis=(0, 1),
    )
    grad_down = down_step(pair, got_pair, normed)
    bucket_loss = loss_sum / (floor_counts * width)
    progress = jnp.sum(weights * bucket_loss) / jnp.sum(bucket_loss)
    competence_next = competence + 0.5 * (1.0 - competence) * progress
    return (grad_down[None], grad_up[None], bucket_loss, competence_next)


def solution(mesh):
    split = Mesh(mesh.devices.reshape(4, 8, 2, mesh.shape["mp"]), DP_MP)
    placed = (
        P(DP, None, "mp"),
        P(DP, None, "mp"),
        P(None, "mp"),
        P("mp"),
        P(DP, None, "mp"),
        P(DP, None, "mp"),
        P(DP),
        P(DP),
        P(DP),
        P(DP, None),
        P(),
    )
    return jax.shard_map(
        on_device,
        mesh=split,
        in_specs=placed,
        out_specs=(P(DP, None, "mp"), P(DP, None, "mp"), P(), P()),
        check_vma=False,
    )
```

```python
import jax
import jax.numpy as jnp
from jax import lax
from jax.experimental import pallas as pl
from jax.experimental.pallas import tpu as pltpu
from jax.sharding import Mesh
from jax.sharding import PartitionSpec as P

NB = 16
DP = ("dp_0", "dp_1", "dp_2")
DP_MP = ("dp_0", "dp_1", "dp_2", "mp")

RMS_EPSILON = 1e-05
SHARPNESS = 12.0
ADAPTER_SCALING = 2.0
PER_PAIR = 2
TILES = 1
LAST_CHUNK = 512
VMEM_BYTES = 62 * 1024 * 1024
CONTRACT_LAST = (((1,), (1,)), ((), ()))
CONTRACT_FIRST = (((0,), (0,)), ((), ()))


def swap(value, axis, distance):
    peers = lax.axis_size(axis)
    return lax.ppermute(value, axis, [(i, i ^ distance) for i in range(peers)])


def over_parts(value, axis):
    pair = value + swap(value, axis, 1)
    return pair + swap(pair, axis, 3)


def in_three(row, height):
    high = row.astype(jnp.bfloat16).astype(jnp.float32)
    middle = (row - high).astype(jnp.bfloat16).astype(jnp.float32)
    low = row - high - middle
    zeros = jnp.zeros((height - 3, row.shape[1]), jnp.float32)
    return jnp.concatenate([high, middle, low, zeros], axis=0).astype(jnp.bfloat16)


def from_parts(first, last, axis):
    other_first = swap(first, axis, 3)
    near_last = swap(last, axis, 1)
    near_first = swap(first, axis, 1)
    other_last = swap(last, axis, 3)
    far = (swap(other_first, axis, 1), swap(near_last, axis, 3))
    return (near_first, near_last), (other_first, other_last), far


def lane_group(packed, group, groups):
    slots = [packed[:, s * groups + group][:, None] for s in range(PER_PAIR)]
    whole = jnp.concatenate(slots, axis=1).astype(jnp.float32)
    return whole.reshape(-1, packed.shape[-1])


def square_kernel(packed, done, total):
    groups = (packed.shape[1] - 1) // PER_PAIR
    sums = None
    for g in range(groups):
        x = lane_group(packed, g, groups)
        sums = x * x if sums is None else sums + x * x
    total[...] = jnp.sum(sums.T, axis=0, keepdims=True) + done[0]


def row_squares(packed, done):
    peers, pieces, block_len, lanes = packed.shape
    rows = peers * PER_PAIR * block_len
    chunk = 16
    return pl.pallas_call(
        square_kernel,
        grid=(peers // chunk,),
        out_shape=jax.ShapeDtypeStruct((1, rows), jnp.float32),
        in_specs=[
            pl.BlockSpec((chunk, pieces, block_len, lanes), lambda i: (i, 0, 0, 0)),
            pl.BlockSpec(memory_space=pltpu.SMEM),
        ],
        out_specs=pl.BlockSpec((1, rows * chunk // peers), lambda i: (0, i)),
        compiler_params=pltpu.CompilerParams(vmem_limit_bytes=VMEM_BYTES),
        cost_estimate=pl.CostEstimate(flops=4 << 20, bytes_accessed=2 << 20, transcendentals=0),
        name="row_squares",
    )(packed, done)


def latent_kernel(packed, squares, gain, down, normed, latent):
    lanes = packed.shape[-1]
    groups = (packed.shape[1] - 1) // PER_PAIR
    inverse = lax.rsqrt(squares[...] + RMS_EPSILON)
    inverse = jnp.broadcast_to(inverse, (lanes, inverse.shape[1])).T
    for g in range(groups):
        at = slice(g * lanes, (g + 1) * lanes)
        x = lane_group(packed, g, groups)
        normed[:, at] = (x * inverse * gain[:, at]).astype(jnp.bfloat16)
    latent[...] = lax.dot_general(
        down[...], normed[...], CONTRACT_LAST, preferred_element_type=jnp.float32
    )


def latents(packed, mean_squares, gain, down):
    peers, pieces, block_len, lanes = packed.shape
    rows = peers * PER_PAIR * block_len
    rank, columns = down.shape
    chunk = 16
    part = rows * chunk // peers
    return pl.pallas_call(
        latent_kernel,
        grid=(peers // chunk,),
        out_shape=(
            jax.ShapeDtypeStruct((rows, columns), jnp.bfloat16),
            jax.ShapeDtypeStruct((rank, rows), jnp.float32),
        ),
        in_specs=[
            pl.BlockSpec((chunk, pieces, block_len, lanes), lambda i: (i, 0, 0, 0)),
            pl.BlockSpec((1, part), lambda i: (0, i)),
            pl.BlockSpec((1, columns), lambda i: (0, 0)),
            pl.BlockSpec((rank, columns), lambda i: (0, 0)),
        ],
        out_specs=(
            pl.BlockSpec((part, columns), lambda i: (i, 0)),
            pl.BlockSpec((rank, part), lambda i: (0, i)),
        ),
        compiler_params=pltpu.CompilerParams(vmem_limit_bytes=VMEM_BYTES),
        cost_estimate=pl.CostEstimate(
            flops=2 * rows * rank * columns, bytes_accessed=4 << 20, transcendentals=rows
        ),
        name="latents",
    )(packed, mean_squares, gain[None, :], down)


def route_kernel(
    ids_in, dest_in, buckets_in, lengths_in, pool_in, gain_in,
    send_out, first_out, last_out, slot_of,
    ids, dest, buckets, lengths, pool, gain, send, own, arrived, info, counts, sem,
):
    pairs = (
        (pool_in, pool),
        (ids_in, ids),
        (dest_in, dest),
        (buckets_in, buckets),
        (lengths_in, lengths),
        (gain_in, gain),
    )
    copies = [
        pltpu.make_async_copy(source, target, sem.at[i])
        for i, (source, target) in enumerate(pairs)
    ]
    for copy in copies:
        copy.start()
    sampled = ids.shape[0]
    trainers, pieces, block_len, lanes = send.shape
    groups = (pieces - 1) // PER_PAIR

    def clear(k, carry):
        arrived[k] = 0
        for s in range(PER_PAIR):
            info[s, k] = 0
            info[PER_PAIR + s, k] = 0
        return carry

    def clear_counts(b, carry):
        counts[b] = 0
        return carry

    lax.fori_loop(0, trainers, clear, 0, unroll=8)
    lax.fori_loop(0, NB, clear_counts, 0, unroll=8)
    for copy in copies:
        copy.wait()

    def place(j, carry):
        block = ids[j]
        trainer = dest[j]
        values = pool[block]
        own[j] = values
        order = arrived[trainer]
        arrived[trainer] = order + 1
        slot = trainer * PER_PAIR + order
        for g in range(groups):
            send[trainer, order * groups + g] = values[:, g * lanes : (g + 1) * lanes]
        slot_of[j] = slot
        bucket = buckets[block]
        length = lengths[block]
        info[order, trainer] = bucket
        info[PER_PAIR + order, trainer] = length
        counts[bucket] = counts[bucket] + length
        return carry

    lax.fori_loop(0, sampled, place, 0, unroll=8)
    whole = gain[...]
    high = whole.astype(jnp.bfloat16).astype(jnp.float32)
    middle = (whole - high).astype(jnp.bfloat16).astype(jnp.float32)
    low = whole - high - middle
    zeros = jnp.zeros((own.shape[1] - 3, whole.shape[1]), jnp.float32)
    own[sampled] = jnp.concatenate([high, middle, low, zeros], axis=0).astype(jnp.bfloat16)
    own[sampled + 1] = jnp.zeros(own.shape[1:], own.dtype)
    cut = first_out.shape[0]
    own_copies = (
        pltpu.make_async_copy(own.at[pl.ds(0, cut)], first_out, sem.at[1]),
        pltpu.make_async_copy(own.at[pl.ds(cut, last_out.shape[0])], last_out, sem.at[2]),
    )
    for copy in own_copies:
        copy.start()

    row = lax.broadcasted_iota(jnp.int32, (block_len, lanes), 0)
    lane = lax.broadcasted_iota(jnp.int32, (block_len, lanes), 1)
    holder = jnp.zeros((block_len, lanes), jnp.int32)
    for b in range(NB):
        count = counts[b]
        holder = jnp.where((row == 1) & (lane == b), count // 16, holder)
        holder = jnp.where((row == 2) & (lane == b), count % 16, holder)

    def finish(k, found):
        for s in range(PER_PAIR):
            free = arrived[k] <= s

            @pl.when(free)
            def _():
                slot_of[sampled + found] = k * PER_PAIR + s
                for g in range(groups):
                    send[k, s * groups + g] = jnp.zeros((block_len, lanes), send.dtype)

            found = found + jnp.where(free, 1, 0)
        facts = holder
        for i in range(2 * PER_PAIR):
            facts = jnp.where((row == 0) & (lane == i), info[i, k], facts)
        send[k, pieces - 1] = facts.astype(jnp.float32).astype(send.dtype)
        return found

    lax.fori_loop(0, trainers, finish, 0, unroll=8)
    send_copy = pltpu.make_async_copy(send, send_out, sem.at[0])
    send_copy.start()
    for copy in own_copies:
        copy.wait()
    send_copy.wait()


def route(ids, dest, buckets, lengths, pool, gain, trainers):
    sampled = ids.shape[0]
    slots = trainers * PER_PAIR
    block = pool.shape[1:]
    lanes = 128
    message = (trainers, PER_PAIR * (block[1] // lanes) + 1, block[0], lanes)
    smem = pl.BlockSpec(memory_space=pltpu.SMEM)
    hbm = pl.BlockSpec(memory_space=pltpu.HBM)
    return pl.pallas_call(
        route_kernel,
        out_shape=(
            jax.ShapeDtypeStruct(message, pool.dtype),
            jax.ShapeDtypeStruct((sampled // 2, *block), pool.dtype),
            jax.ShapeDtypeStruct((sampled - sampled // 2 + 2, *block), pool.dtype),
            jax.ShapeDtypeStruct((slots,), jnp.int32),
        ),
        in_specs=[hbm] * 6,
        out_specs=(hbm, hbm, hbm, smem),
        scratch_shapes=[
            pltpu.SMEM(ids.shape, jnp.int32),
            pltpu.SMEM(dest.shape, jnp.int32),
            pltpu.SMEM(buckets.shape, jnp.int32),
            pltpu.SMEM(lengths.shape, jnp.int32),
            pltpu.VMEM(pool.shape, pool.dtype),
            pltpu.VMEM((1, gain.shape[0]), jnp.float32),
            pltpu.VMEM(message, pool.dtype),
            pltpu.VMEM((sampled + 2, *block), pool.dtype),
            pltpu.SMEM((trainers,), jnp.int32),
            pltpu.SMEM((2 * PER_PAIR, trainers), jnp.int32),
            pltpu.SMEM((NB,), jnp.int32),
            pltpu.SemaphoreType.DMA((6,)),
        ],
        compiler_params=pltpu.CompilerParams(vmem_limit_bytes=VMEM_BYTES),
        cost_estimate=pl.CostEstimate(flops=0, bytes_accessed=5 << 20, transcendentals=0),
        name="route",
    )(ids, dest, buckets, lengths, pool, gain[None, :])


def early_kernel(
    ids, mine_first, mine_last, near_first, near_last, other_first, other_last, targets,
    taken, squares,
):
    step = pl.program_id(0)
    half = pl.num_programs(0) // 2
    part = near_first.shape[1]
    lanes = squares.shape[1]
    blocks = taken.shape[0]

    def add_squares(pieces):
        sums = jnp.zeros(squares.shape, jnp.float32)
        for g in range(part // lanes):
            at = slice(g * lanes, (g + 1) * lanes)
            for piece in pieces:
                x = piece[:, at].astype(jnp.float32)
                sums = sums + x * x
        squares[...] = sums

    @pl.when(step < half)
    def _():
        add_squares((mine_first, near_first, other_first))

    @pl.when(step >= half)
    def _():
        add_squares((mine_last, near_last, other_last))

    def take(j, carry):
        taken[j] = targets[ids[step * blocks + j]]
        return carry

    lax.fori_loop(0, blocks, take, 0, unroll=4)


def early_part(ids, mine, near, other, targets):
    part = near[0].shape[1]
    block = targets.shape[1:]
    sampled = ids.shape[0]
    rows = sampled * block[0]
    chunk = 128
    blocks = chunk // block[0]
    half = rows // chunk // 2
    lanes = 128
    first = pl.BlockSpec((chunk, part), lambda n: (jnp.minimum(n, half - 1), 0))
    last = pl.BlockSpec((chunk, part), lambda n: (jnp.maximum(n - half, 0), 0))
    return pl.pallas_call(
        early_kernel,
        grid=(rows // chunk,),
        out_shape=(
            jax.ShapeDtypeStruct((sampled, *block), jnp.bfloat16),
            jax.ShapeDtypeStruct((rows, lanes), jnp.float32),
        ),
        in_specs=[pl.BlockSpec(memory_space=pltpu.SMEM)]
        + [first, last] * 3
        + [pl.BlockSpec(targets.shape, lambda n: (0, 0, 0))],
        out_specs=(
            pl.BlockSpec((blocks, *block), lambda n: (n, 0, 0)),
            pl.BlockSpec((chunk, lanes), lambda n: (n, 0)),
        ),
        compiler_params=pltpu.CompilerParams(vmem_limit_bytes=VMEM_BYTES),
        cost_estimate=pl.CostEstimate(flops=6 << 20, bytes_accessed=7 << 20, transcendentals=0),
        name="early_part",
    )(ids, *mine, *near, *other, targets)


def gap_kernel(
    slot_of, order, far_first, far_last, mine_first, mine_last, near_first, near_last,
    other_first, other_last, squares_in, frozen_in, taken_in,
    send_out, done, pieces, squares, frozen, taken, send, normed, total, gap, sem,
):
    parts, _, part = pieces.shape
    sampled, block_len, columns = gap.shape
    rows = sampled * block_len
    cut = far_first.shape[0]
    slots = send.shape[0]
    places = (2, 0, 1, 3)
    halves = (
        (far_first, far_last),
        (mine_first, mine_last),
        (near_first, near_last),
        (other_first, other_last),
    )
    copies = [
        (
            pltpu.make_async_copy(first, pieces.at[i, pl.ds(0, cut)], sem.at[2 * i]),
            pltpu.make_async_copy(
                last, pieces.at[i, pl.ds(cut, last.shape[0])], sem.at[2 * i + 1]
            ),
        )
        for i, (first, last) in enumerate(halves)
    ]
    squares_copy = pltpu.make_async_copy(squares_in, squares, sem.at[2 * parts])
    taken_copy = pltpu.make_async_copy(taken_in, taken, sem.at[2 * parts + 1])
    weights = [
        pltpu.make_async_copy(
            frozen_in.at[pl.ds(pl.multiple_of(order[places[i]] * part, part), part)],
            frozen.at[i],
            sem.at[2 * parts + 2 + i],
        )
        for i in range(parts)
    ]
    squares_copy.start()
    for i in range(parts):
        for copy in copies[i]:
            copy.start()
        weights[i].start()
    taken_copy.start()
    done[0] = 0.0

    def fill(s, carry):
        send[slot_of[sampled + s]] = jnp.zeros((block_len, columns), jnp.bfloat16)
        return carry

    lax.fori_loop(0, slots - sampled, fill, 0, unroll=8)
    squares_copy.wait()
    for copy in copies[0]:
        copy.wait()
    chunk = 128

    def invert(r):
        at = slice(r * chunk, (r + 1) * chunk)
        x = pieces[0, at].astype(jnp.float32)
        sums = squares[at]
        lanes = sums.shape[1]
        for g in range(part // lanes):
            sums = sums + x[:, g * lanes : (g + 1) * lanes] * x[:, g * lanes : (g + 1) * lanes]
        mean = jnp.sum(sums, axis=1, keepdims=True) / (parts * part)
        squares[at] = jnp.broadcast_to(lax.rsqrt(mean + RMS_EPSILON), sums.shape)

    def normalize(i, r):
        at = slice(r * chunk, (r + 1) * chunk)
        three = pieces[i, rows : rows + 16].astype(jnp.float32)
        gain = three[0:1] + three[1:2] + three[2:3]
        x = pieces[i, at].astype(jnp.float32)
        normed[i, at] = (x * squares[at, 0:1] * gain).astype(jnp.bfloat16)

    chunks = rows // chunk
    for r in range(chunks):
        invert(r)
        normalize(0, r)
    tile = columns // TILES
    for i in range(parts):
        weights[i].wait()
        if i + 1 < parts:
            for copy in copies[i + 1]:
                copy.wait()
        else:
            taken_copy.wait()
        for n in range(TILES):
            at = slice(n * tile, (n + 1) * tile)
            product = jnp.dot(
                normed[i], frozen[i, :, at], preferred_element_type=jnp.float32
            )
            if i > 0:
                product = total[:, at] + product
            if i + 1 < parts:
                total[:, at] = product
                for r in range(n * chunks // TILES, (n + 1) * chunks // TILES):
                    normalize(i + 1, r)
            else:
                x = pieces[1, :rows, at].astype(jnp.float32)
                whole = (x + product).reshape(sampled, block_len, tile)
                gap[:, :, at] = (whole - taken[:, :, at].astype(jnp.float32)).astype(jnp.bfloat16)

    def place(j, carry):
        send[slot_of[j]] = gap[j]
        return carry

    lax.fori_loop(0, sampled, place, 0, unroll=8)
    copy = pltpu.make_async_copy(send, send_out, sem.at[0])
    copy.start()
    copy.wait()


def base_gap_slots(slot_of, order, mine, near, other, far, taken, squares, frozen):
    part = mine[0].shape[1]
    height = mine[0].shape[0] + mine[1].shape[0]
    width, columns = frozen.shape
    slots = slot_of.shape[0]
    sampled, *block = taken.shape
    rows = sampled * block[0]
    parts = width // part
    smem = pl.BlockSpec(memory_space=pltpu.SMEM)
    hbm = pl.BlockSpec(memory_space=pltpu.HBM)
    return pl.pallas_call(
        gap_kernel,
        out_shape=(
            jax.ShapeDtypeStruct((slots, *block), jnp.bfloat16),
            jax.ShapeDtypeStruct((1,), jnp.float32),
        ),
        in_specs=[smem, smem] + [hbm] * 11,
        out_specs=(hbm, smem),
        scratch_shapes=[
            pltpu.VMEM((parts, height, part), jnp.bfloat16),
            pltpu.VMEM(squares.shape, jnp.float32),
            pltpu.VMEM((parts, part, columns), jnp.bfloat16),
            pltpu.VMEM((sampled, *block), jnp.bfloat16),
            pltpu.VMEM((slots, *block), jnp.bfloat16),
            pltpu.VMEM((parts, rows, part), jnp.bfloat16),
            pltpu.VMEM((rows, columns), jnp.float32),
            pltpu.VMEM((sampled, *block), jnp.bfloat16),
            pltpu.SemaphoreType.DMA((3 * parts + 2,)),
        ],
        compiler_params=pltpu.CompilerParams(vmem_limit_bytes=VMEM_BYTES),
        cost_estimate=pl.CostEstimate(
            flops=2 * rows * width * columns, bytes_accessed=18 << 20, transcendentals=rows
        ),
        name="base_gap",
    )(
        slot_of, order, *far, *mine, *near, *other, squares, frozen, taken,
    )


def trainer_kernel(gap, lowered, up, facts, grad_up, back, sent, loss):
    step = pl.program_id(0)
    low = lowered[...]
    up_map = up[...]
    facts_now = facts[...]
    distance = gap[...].astype(jnp.float32) + lax.dot_general(
        low, up_map, CONTRACT_FIRST, preferred_element_type=jnp.float32
    )
    output_grad = (facts_now[:, NB : NB + 1] * distance).astype(jnp.bfloat16)
    squares = jnp.sum(distance * distance, axis=1, keepdims=True)
    part = jnp.sum(facts_now * squares, axis=0, keepdims=True)
    back_now = lax.dot_general(
        up_map, output_grad, CONTRACT_LAST, preferred_element_type=jnp.float32
    )
    back[...] = back_now
    rank = up_map.shape[0]
    lanes = loss.shape[1]
    sent[0:rank] = back_now.astype(jnp.bfloat16)
    sent[rank:] = jnp.zeros((sent.shape[0] - rank, sent.shape[1]), jnp.bfloat16)
    own = jnp.dot(low, output_grad, preferred_element_type=jnp.float32)

    @pl.when(step == 0)
    def _():
        grad_up[...] = own
        loss[...] = part

    @pl.when(step > 0)
    def _():
        grad_up[...] += own
        loss[...] += part

    @pl.when(step == pl.num_programs(0) - 1)
    def _():
        sent[rank:, 0:lanes] = in_three(loss[...], sent.shape[0] - rank)


def trainer_step(gap, lowered, up, facts):
    rows, columns = gap.shape
    rank = up.shape[0]
    lanes = facts.shape[1]
    chunk = LAST_CHUNK
    return pl.pallas_call(
        trainer_kernel,
        grid=(rows // chunk,),
        out_shape=(
            jax.ShapeDtypeStruct((rank, columns), jnp.float32),
            jax.ShapeDtypeStruct((rank, rows), jnp.float32),
            jax.ShapeDtypeStruct((rank + 16, rows), jnp.bfloat16),
            jax.ShapeDtypeStruct((1, lanes), jnp.float32),
        ),
        in_specs=[
            pl.BlockSpec((chunk, columns), lambda i: (i, 0)),
            pl.BlockSpec((rank, chunk), lambda i: (0, i)),
            pl.BlockSpec((rank, columns), lambda i: (0, 0)),
            pl.BlockSpec((chunk, lanes), lambda i: (i, 0)),
        ],
        out_specs=(
            pl.BlockSpec((rank, columns), lambda i: (0, 0)),
            pl.BlockSpec((rank, chunk), lambda i: (0, i)),
            pl.BlockSpec((rank + 16, chunk), lambda i: (0, i)),
            pl.BlockSpec((1, lanes), lambda i: (0, 0)),
        ),
        compiler_params=pltpu.CompilerParams(vmem_limit_bytes=VMEM_BYTES),
        cost_estimate=pl.CostEstimate(
            flops=6 * rows * rank * columns, bytes_accessed=4 << 20, transcendentals=0
        ),
        name="trainer_step",
    )(gap, lowered, up, facts)


def pair_kernel(back, loss, got, pair, pair_loss, sent):
    rank, rows = back.shape
    lanes = loss.shape[1]
    at = slice(rows - LAST_CHUNK, rows - LAST_CHUNK + lanes)
    total = back[...] + got[0:rank].astype(jnp.float32)
    pair[...] = total
    sent[0:rank] = total.astype(jnp.bfloat16)
    three = got[rank:, at].astype(jnp.float32)
    whole = loss[...] + (three[0:1] + three[1:2] + three[2:3])
    pair_loss[...] = whole
    height = sent.shape[0] - rank
    sent[rank:] = jnp.zeros((height, rows), jnp.bfloat16)
    sent[rank:, at] = in_three(whole, height)


def pair_step(back, loss, got):
    vmem = pl.BlockSpec(memory_space=pltpu.VMEM)
    return pl.pallas_call(
        pair_kernel,
        out_shape=(
            jax.ShapeDtypeStruct(back.shape, jnp.float32),
            jax.ShapeDtypeStruct(loss.shape, jnp.float32),
            jax.ShapeDtypeStruct(got.shape, jnp.bfloat16),
        ),
        in_specs=[vmem] * 3,
        out_specs=(vmem, vmem, vmem),
        compiler_params=pltpu.CompilerParams(vmem_limit_bytes=VMEM_BYTES),
        cost_estimate=pl.CostEstimate(flops=1 << 17, bytes_accessed=1 << 20, transcendentals=0),
        name="pair_step",
    )(back, loss, got)


def down_kernel(pair, got, normed, grad_down):
    rank = pair.shape[0]
    back = pair[...] + got[0:rank].astype(jnp.float32)
    lowered_gradient = (ADAPTER_SCALING * back).astype(jnp.bfloat16)
    grad_down[...] = jnp.dot(
        lowered_gradient, normed[...], preferred_element_type=jnp.float32
    )


def down_step(pair, got, normed):
    rank, rows = pair.shape
    columns = normed.shape[1]
    vmem = pl.BlockSpec(memory_space=pltpu.VMEM)
    return pl.pallas_call(
        down_kernel,
        out_shape=jax.ShapeDtypeStruct((rank, columns), jnp.float32),
        in_specs=[vmem] * 3,
        out_specs=vmem,
        compiler_params=pltpu.CompilerParams(vmem_limit_bytes=VMEM_BYTES),
        cost_estimate=pl.CostEstimate(
            flops=2 * rows * rank * columns, bytes_accessed=3 << 20, transcendentals=0
        ),
        name="down_step",
    )(pair, got, normed)


def on_device(
    pool_inputs,
    pool_targets,
    frozen,
    gain,
    adapter_down,
    adapter_up,
    sample_ids,
    buckets,
    lengths,
    destinations,
    competence,
):
    trainers = lax.axis_size(DP)
    sampled = sample_ids.shape[0]
    _, block_len, part = pool_inputs.shape
    width = frozen.shape[0]
    slots = trainers * PER_PAIR
    rows = slots * block_len
    per_peer = PER_PAIR * block_len
    down_map = adapter_down[0]
    up_map = adapter_up[0]
    bucket_range = jnp.arange(NB, dtype=jnp.int32)

    send_x, own_first, own_last, slot_of = route(
        sample_ids, destinations[:, 0], buckets, lengths, pool_inputs, gain, trainers
    )
    got_x = lax.all_to_all(send_x, DP, 0, 0, tiled=True)
    mine = (own_first.reshape(-1, part), own_last.reshape(-1, part))
    near, other, far = from_parts(*mine, "mp")
    order = lax.axis_index("mp") ^ jnp.arange(lax.axis_size("mp"), dtype=jnp.int32)
    taken, near_squares = early_part(sample_ids, mine, near, other, pool_targets)
    send_gap, done = base_gap_slots(
        slot_of, order, mine, near, other, far, taken, near_squares, frozen
    )
    got_gap = lax.all_to_all(
        send_gap.reshape(trainers, per_peer, part), DP, 0, 0, tiled=True
    )

    got_info = got_x[:, -1, 0, : 2 * PER_PAIR].astype(jnp.float32).astype(jnp.int32)
    got_counts = got_x[:, -1, 1:3, :NB].astype(jnp.float32)
    counts = jnp.sum(16.0 * got_counts[:, 0] + got_counts[:, 1], axis=0)
    floor_counts = jnp.maximum(counts, 1.0)
    weights = jax.nn.sigmoid(
        SHARPNESS * (competence[0] - (bucket_range.astype(jnp.float32) + 0.5) / NB)
    )
    row_bucket = jnp.repeat(got_info[:, :PER_PAIR].reshape(slots), block_len)
    row_length = jnp.repeat(got_info[:, PER_PAIR:].reshape(slots), block_len)
    live = (jnp.arange(rows, dtype=jnp.int32) % block_len < row_length).astype(jnp.float32)
    onehot = (row_bucket[:, None] == bucket_range[None, :]).astype(jnp.float32) * live[:, None]
    coefficient = 2.0 * jnp.sum(onehot * (weights / floor_counts)[None, :], axis=1)
    facts = jnp.concatenate(
        [onehot, coefficient[:, None], jnp.zeros((rows, 128 - NB - 1), jnp.float32)], axis=1
    )

    mean_squares = over_parts(row_squares(got_x, done), "mp") / width
    normed, latent_part = latents(got_x, mean_squares, gain, down_map)
    lowered = (ADAPTER_SCALING * over_parts(latent_part, "mp")).astype(jnp.bfloat16)

    grad_up, back_part, back_sent, loss_part = trainer_step(
        got_gap.reshape(rows, part), lowered, up_map, facts
    )
    pair, pair_loss, pair_sent = pair_step(back_part, loss_part, swap(back_sent, "mp", 1))
    got_pair = swap(pair_sent, "mp", 3)
    rank = up_map.shape[0]
    at = rows - LAST_CHUNK
    three = got_pair[rank : rank + 3, at : at + NB].astype(jnp.float32)
    own_loss = pair_loss[0, :NB] + (three[0] + three[1] + three[2])
    loss_sum = jnp.sum(
        lax.all_to_all(jnp.broadcast_to(own_loss, (trainers, 1, NB)), DP, 0, 0, tiled=True),
        axis=(0, 1),
    )
    grad_down = down_step(pair, got_pair, normed)
    bucket_loss = loss_sum / (floor_counts * width)
    progress = jnp.sum(weights * bucket_loss) / jnp.sum(bucket_loss)
    competence_next = competence + 0.5 * (1.0 - competence) * progress
    return (grad_down[None], grad_up[None], bucket_loss, competence_next)


def solution(mesh):
    split = Mesh(mesh.devices.reshape(4, 8, 2, mesh.shape["mp"]), DP_MP)
    placed = (
        P(DP, None, "mp"),
        P(DP, None, "mp"),
        P(None, "mp"),
        P("mp"),
        P(DP, None, "mp"),
        P(DP, None, "mp"),
        P(DP),
        P(DP),
        P(DP),
        P(DP, None),
        P(),
    )
    return jax.shard_map(
        on_device,
        mesh=split,
        in_specs=placed,
        out_specs=(P(DP, None, "mp"), P(DP, None, "mp"), P(), P()),
        check_vma=False,
    )
```

```python
import jax
import jax.numpy as jnp
from jax import lax
from jax.experimental import pallas as pl
from jax.experimental.pallas import tpu as pltpu
from jax.sharding import Mesh
from jax.sharding import PartitionSpec as P

NB = 16
DP = ("dp_0", "dp_1", "dp_2")
DP_MP = ("dp_0", "dp_1", "dp_2", "mp")

RMS_EPSILON = 1e-05
SHARPNESS = 12.0
ADAPTER_SCALING = 2.0
PER_PAIR = 2
TILES = 1
LAST_CHUNK = 512
VMEM_BYTES = 62 * 1024 * 1024
CONTRACT_LAST = (((1,), (1,)), ((), ()))
CONTRACT_FIRST = (((0,), (0,)), ((), ()))


def swap(value, axis, distance):
    peers = lax.axis_size(axis)
    return lax.ppermute(value, axis, [(i, i ^ distance) for i in range(peers)])


def over_parts(value, axis):
    pair = value + swap(value, axis, 1)
    return pair + swap(pair, axis, 3)


def in_three(row, height):
    high = row.astype(jnp.bfloat16).astype(jnp.float32)
    middle = (row - high).astype(jnp.bfloat16).astype(jnp.float32)
    low = row - high - middle
    zeros = jnp.zeros((height - 3, row.shape[1]), jnp.float32)
    return jnp.concatenate([high, middle, low, zeros], axis=0).astype(jnp.bfloat16)


def from_parts(first, last, axis):
    other_first = swap(first, axis, 3)
    near_last = swap(last, axis, 1)
    near_first = swap(first, axis, 1)
    other_last = swap(last, axis, 3)
    far = (swap(other_first, axis, 1), swap(near_last, axis, 3))
    return (near_first, near_last), (other_first, other_last), far


def lane_group(packed, group, groups):
    slots = [packed[:, s * groups + group][:, None] for s in range(PER_PAIR)]
    whole = jnp.concatenate(slots, axis=1).astype(jnp.float32)
    return whole.reshape(-1, packed.shape[-1])


def square_kernel(packed, done, total):
    groups = (packed.shape[1] - 1) // PER_PAIR
    sums = None
    for g in range(groups):
        x = lane_group(packed, g, groups)
        sums = x * x if sums is None else sums + x * x
    total[...] = jnp.sum(sums.T, axis=0, keepdims=True) + done[0]


def row_squares(packed, done):
    peers, pieces, block_len, lanes = packed.shape
    rows = peers * PER_PAIR * block_len
    chunk = 16
    return pl.pallas_call(
        square_kernel,
        grid=(peers // chunk,),
        out_shape=jax.ShapeDtypeStruct((1, rows), jnp.float32),
        in_specs=[
            pl.BlockSpec((chunk, pieces, block_len, lanes), lambda i: (i, 0, 0, 0)),
            pl.BlockSpec(memory_space=pltpu.SMEM),
        ],
        out_specs=pl.BlockSpec((1, rows * chunk // peers), lambda i: (0, i)),
        compiler_params=pltpu.CompilerParams(vmem_limit_bytes=VMEM_BYTES),
        cost_estimate=pl.CostEstimate(flops=4 << 20, bytes_accessed=2 << 20, transcendentals=0),
        name="row_squares",
    )(packed, done)


def latent_kernel(packed, squares, gain, down, normed, latent):
    lanes = packed.shape[-1]
    groups = (packed.shape[1] - 1) // PER_PAIR
    inverse = lax.rsqrt(squares[...] + RMS_EPSILON)
    inverse = jnp.broadcast_to(inverse, (lanes, inverse.shape[1])).T
    for g in range(groups):
        at = slice(g * lanes, (g + 1) * lanes)
        x = lane_group(packed, g, groups)
        normed[:, at] = (x * inverse * gain[:, at]).astype(jnp.bfloat16)
    latent[...] = lax.dot_general(
        down[...], normed[...], CONTRACT_LAST, preferred_element_type=jnp.float32
    )


def latents(packed, mean_squares, gain, down):
    peers, pieces, block_len, lanes = packed.shape
    rows = peers * PER_PAIR * block_len
    rank, columns = down.shape
    chunk = 16
    part = rows * chunk // peers
    return pl.pallas_call(
        latent_kernel,
        grid=(peers // chunk,),
        out_shape=(
            jax.ShapeDtypeStruct((rows, columns), jnp.bfloat16),
            jax.ShapeDtypeStruct((rank, rows), jnp.float32),
        ),
        in_specs=[
            pl.BlockSpec((chunk, pieces, block_len, lanes), lambda i: (i, 0, 0, 0)),
            pl.BlockSpec((1, part), lambda i: (0, i)),
            pl.BlockSpec((1, columns), lambda i: (0, 0)),
            pl.BlockSpec((rank, columns), lambda i: (0, 0)),
        ],
        out_specs=(
            pl.BlockSpec((part, columns), lambda i: (i, 0)),
            pl.BlockSpec((rank, part), lambda i: (0, i)),
        ),
        compiler_params=pltpu.CompilerParams(vmem_limit_bytes=VMEM_BYTES),
        cost_estimate=pl.CostEstimate(
            flops=2 * rows * rank * columns, bytes_accessed=4 << 20, transcendentals=rows
        ),
        name="latents",
    )(packed, mean_squares, gain[None, :], down)


def route_kernel(
    ids_in, dest_in, buckets_in, lengths_in, pool_in, gain_in,
    send_out, first_out, last_out, slot_of,
    ids, dest, buckets, lengths, pool, gain, send, own, arrived, info, counts, sem,
):
    pairs = (
        (pool_in, pool),
        (ids_in, ids),
        (dest_in, dest),
        (buckets_in, buckets),
        (lengths_in, lengths),
        (gain_in, gain),
    )
    copies = [
        pltpu.make_async_copy(source, target, sem.at[i])
        for i, (source, target) in enumerate(pairs)
    ]
    for copy in copies:
        copy.start()
    sampled = ids.shape[0]
    trainers, pieces, block_len, lanes = send.shape
    groups = (pieces - 1) // PER_PAIR

    def clear(k, carry):
        arrived[k] = 0
        for s in range(PER_PAIR):
            info[s, k] = 0
            info[PER_PAIR + s, k] = 0
        return carry

    def clear_counts(b, carry):
        counts[b] = 0
        return carry

    lax.fori_loop(0, trainers, clear, 0, unroll=8)
    lax.fori_loop(0, NB, clear_counts, 0, unroll=8)
    for copy in copies:
        copy.wait()

    def place(j, carry):
        block = ids[j]
        trainer = dest[j]
        values = pool[block]
        own[j] = values
        order = arrived[trainer]
        arrived[trainer] = order + 1
        slot = trainer * PER_PAIR + order
        for g in range(groups):
            send[trainer, order * groups + g] = values[:, g * lanes : (g + 1) * lanes]
        slot_of[j] = slot
        bucket = buckets[block]
        length = lengths[block]
        info[order, trainer] = bucket
        info[PER_PAIR + order, trainer] = length
        counts[bucket] = counts[bucket] + length
        return carry

    lax.fori_loop(0, sampled, place, 0, unroll=8)
    whole = gain[...]
    high = whole.astype(jnp.bfloat16).astype(jnp.float32)
    middle = (whole - high).astype(jnp.bfloat16).astype(jnp.float32)
    low = whole - high - middle
    zeros = jnp.zeros((own.shape[1] - 3, whole.shape[1]), jnp.float32)
    own[sampled] = jnp.concatenate([high, middle, low, zeros], axis=0).astype(jnp.bfloat16)
    own[sampled + 1] = jnp.zeros(own.shape[1:], own.dtype)
    cut = first_out.shape[0]
    own_copies = (
        pltpu.make_async_copy(own.at[pl.ds(0, cut)], first_out, sem.at[1]),
        pltpu.make_async_copy(own.at[pl.ds(cut, last_out.shape[0])], last_out, sem.at[2]),
    )
    for copy in own_copies:
        copy.start()

    row = lax.broadcasted_iota(jnp.int32, (block_len, lanes), 0)
    lane = lax.broadcasted_iota(jnp.int32, (block_len, lanes), 1)
    holder = jnp.zeros((block_len, lanes), jnp.int32)
    for b in range(NB):
        count = counts[b]
        holder = jnp.where((row == 1) & (lane == b), count // 16, holder)
        holder = jnp.where((row == 2) & (lane == b), count % 16, holder)

    def finish(k, found):
        for s in range(PER_PAIR):
            free = arrived[k] <= s

            @pl.when(free)
            def _():
                slot_of[sampled + found] = k * PER_PAIR + s
                for g in range(groups):
                    send[k, s * groups + g] = jnp.zeros((block_len, lanes), send.dtype)

            found = found + jnp.where(free, 1, 0)
        facts = holder
        for i in range(2 * PER_PAIR):
            facts = jnp.where((row == 0) & (lane == i), info[i, k], facts)
        send[k, pieces - 1] = facts.astype(jnp.float32).astype(send.dtype)
        return found

    quarter = trainers // 4
    found = 0
    send_copies = []
    for q in range(4):
        found = lax.fori_loop(q * quarter, (q + 1) * quarter, finish, found, unroll=8)
        part = pl.ds(q * quarter, quarter)
        copy = pltpu.make_async_copy(send.at[part], send_out.at[part], sem.at[3 + q])
        copy.start()
        send_copies.append(copy)
    for copy in (*own_copies, *send_copies):
        copy.wait()


def route(ids, dest, buckets, lengths, pool, gain, trainers):
    sampled = ids.shape[0]
    slots = trainers * PER_PAIR
    block = pool.shape[1:]
    lanes = 128
    message = (trainers, PER_PAIR * (block[1] // lanes) + 1, block[0], lanes)
    smem = pl.BlockSpec(memory_space=pltpu.SMEM)
    hbm = pl.BlockSpec(memory_space=pltpu.HBM)
    return pl.pallas_call(
        route_kernel,
        out_shape=(
            jax.ShapeDtypeStruct(message, pool.dtype),
            jax.ShapeDtypeStruct((sampled // 2, *block), pool.dtype),
            jax.ShapeDtypeStruct((sampled - sampled // 2 + 2, *block), pool.dtype),
            jax.ShapeDtypeStruct((slots,), jnp.int32),
        ),
        in_specs=[hbm] * 6,
        out_specs=(hbm, hbm, hbm, smem),
        scratch_shapes=[
            pltpu.SMEM(ids.shape, jnp.int32),
            pltpu.SMEM(dest.shape, jnp.int32),
            pltpu.SMEM(buckets.shape, jnp.int32),
            pltpu.SMEM(lengths.shape, jnp.int32),
            pltpu.VMEM(pool.shape, pool.dtype),
            pltpu.VMEM((1, gain.shape[0]), jnp.float32),
            pltpu.VMEM(message, pool.dtype),
            pltpu.VMEM((sampled + 2, *block), pool.dtype),
            pltpu.SMEM((trainers,), jnp.int32),
            pltpu.SMEM((2 * PER_PAIR, trainers), jnp.int32),
            pltpu.SMEM((NB,), jnp.int32),
            pltpu.SemaphoreType.DMA((7,)),
        ],
        compiler_params=pltpu.CompilerParams(vmem_limit_bytes=VMEM_BYTES),
        cost_estimate=pl.CostEstimate(flops=0, bytes_accessed=5 << 20, transcendentals=0),
        name="route",
    )(ids, dest, buckets, lengths, pool, gain[None, :])


def early_kernel(
    ids, mine_first, mine_last, near_first, near_last, other_first, other_last, targets,
    taken, squares,
):
    step = pl.program_id(0)
    half = pl.num_programs(0) // 2
    part = near_first.shape[1]
    lanes = squares.shape[1]
    blocks = taken.shape[0]

    def add_squares(pieces):
        sums = jnp.zeros(squares.shape, jnp.float32)
        for g in range(part // lanes):
            at = slice(g * lanes, (g + 1) * lanes)
            for piece in pieces:
                x = piece[:, at].astype(jnp.float32)
                sums = sums + x * x
        squares[...] = sums

    @pl.when(step < half)
    def _():
        add_squares((mine_first, near_first, other_first))

    @pl.when(step >= half)
    def _():
        add_squares((mine_last, near_last, other_last))

    def take(j, carry):
        taken[j] = targets[ids[step * blocks + j]]
        return carry

    lax.fori_loop(0, blocks, take, 0, unroll=4)


def early_part(ids, mine, near, other, targets):
    part = near[0].shape[1]
    block = targets.shape[1:]
    sampled = ids.shape[0]
    rows = sampled * block[0]
    chunk = 128
    blocks = chunk // block[0]
    half = rows // chunk // 2
    lanes = 128
    first = pl.BlockSpec((chunk, part), lambda n: (jnp.minimum(n, half - 1), 0))
    last = pl.BlockSpec((chunk, part), lambda n: (jnp.maximum(n - half, 0), 0))
    return pl.pallas_call(
        early_kernel,
        grid=(rows // chunk,),
        out_shape=(
            jax.ShapeDtypeStruct((sampled, *block), jnp.bfloat16),
            jax.ShapeDtypeStruct((rows, lanes), jnp.float32),
        ),
        in_specs=[pl.BlockSpec(memory_space=pltpu.SMEM)]
        + [first, last] * 3
        + [pl.BlockSpec(targets.shape, lambda n: (0, 0, 0))],
        out_specs=(
            pl.BlockSpec((blocks, *block), lambda n: (n, 0, 0)),
            pl.BlockSpec((chunk, lanes), lambda n: (n, 0)),
        ),
        compiler_params=pltpu.CompilerParams(vmem_limit_bytes=VMEM_BYTES),
        cost_estimate=pl.CostEstimate(flops=6 << 20, bytes_accessed=7 << 20, transcendentals=0),
        name="early_part",
    )(ids, *mine, *near, *other, targets)


def gap_kernel(
    slot_of, order, far_first, far_last, mine_first, mine_last, near_first, near_last,
    other_first, other_last, squares_in, frozen_in, taken_in,
    send_out, done, pieces, squares, frozen, taken, send, normed, total, gap, sem,
):
    parts, _, part = pieces.shape
    sampled, block_len, columns = gap.shape
    rows = sampled * block_len
    cut = far_first.shape[0]
    slots = send.shape[0]
    places = (2, 0, 1, 3)
    halves = (
        (far_first, far_last),
        (mine_first, mine_last),
        (near_first, near_last),
        (other_first, other_last),
    )
    copies = [
        (
            pltpu.make_async_copy(first, pieces.at[i, pl.ds(0, cut)], sem.at[2 * i]),
            pltpu.make_async_copy(
                last, pieces.at[i, pl.ds(cut, last.shape[0])], sem.at[2 * i + 1]
            ),
        )
        for i, (first, last) in enumerate(halves)
    ]
    squares_copy = pltpu.make_async_copy(squares_in, squares, sem.at[2 * parts])
    taken_copy = pltpu.make_async_copy(taken_in, taken, sem.at[2 * parts + 1])
    weights = [
        pltpu.make_async_copy(
            frozen_in.at[pl.ds(pl.multiple_of(order[places[i]] * part, part), part)],
            frozen.at[i],
            sem.at[2 * parts + 2 + i],
        )
        for i in range(parts)
    ]
    squares_copy.start()
    for i in range(parts):
        for copy in copies[i]:
            copy.start()
        weights[i].start()
    taken_copy.start()
    done[0] = 0.0

    def fill(s, carry):
        send[slot_of[sampled + s]] = jnp.zeros((block_len, columns), jnp.bfloat16)
        return carry

    lax.fori_loop(0, slots - sampled, fill, 0, unroll=8)
    squares_copy.wait()
    for copy in copies[0]:
        copy.wait()
    chunk = 128

    def invert(r):
        at = slice(r * chunk, (r + 1) * chunk)
        x = pieces[0, at].astype(jnp.float32)
        sums = squares[at]
        lanes = sums.shape[1]
        for g in range(part // lanes):
            sums = sums + x[:, g * lanes : (g + 1) * lanes] * x[:, g * lanes : (g + 1) * lanes]
        mean = jnp.sum(sums, axis=1, keepdims=True) / (parts * part)
        squares[at] = jnp.broadcast_to(lax.rsqrt(mean + RMS_EPSILON), sums.shape)

    def normalize(i, r):
        at = slice(r * chunk, (r + 1) * chunk)
        three = pieces[i, rows : rows + 16].astype(jnp.float32)
        gain = three[0:1] + three[1:2] + three[2:3]
        x = pieces[i, at].astype(jnp.float32)
        normed[i, at] = (x * squares[at, 0:1] * gain).astype(jnp.bfloat16)

    chunks = rows // chunk
    for r in range(chunks):
        invert(r)
        normalize(0, r)
    tile = columns // TILES
    for i in range(parts):
        weights[i].wait()
        if i + 1 < parts:
            for copy in copies[i + 1]:
                copy.wait()
        else:
            taken_copy.wait()
        for n in range(TILES):
            at = slice(n * tile, (n + 1) * tile)
            product = jnp.dot(
                normed[i], frozen[i, :, at], preferred_element_type=jnp.float32
            )
            if i > 0:
                product = total[:, at] + product
            if i + 1 < parts:
                total[:, at] = product
                for r in range(n * chunks // TILES, (n + 1) * chunks // TILES):
                    normalize(i + 1, r)
            else:
                x = pieces[1, :rows, at].astype(jnp.float32)
                whole = (x + product).reshape(sampled, block_len, tile)
                gap[:, :, at] = (whole - taken[:, :, at].astype(jnp.float32)).astype(jnp.bfloat16)

    def place(j, carry):
        send[slot_of[j]] = gap[j]
        return carry

    lax.fori_loop(0, sampled, place, 0, unroll=8)
    copy = pltpu.make_async_copy(send, send_out, sem.at[0])
    copy.start()
    copy.wait()


def base_gap_slots(slot_of, order, mine, near, other, far, taken, squares, frozen):
    part = mine[0].shape[1]
    height = mine[0].shape[0] + mine[1].shape[0]
    width, columns = frozen.shape
    slots = slot_of.shape[0]
    sampled, *block = taken.shape
    rows = sampled * block[0]
    parts = width // part
    smem = pl.BlockSpec(memory_space=pltpu.SMEM)
    hbm = pl.BlockSpec(memory_space=pltpu.HBM)
    return pl.pallas_call(
        gap_kernel,
        out_shape=(
            jax.ShapeDtypeStruct((slots, *block), jnp.bfloat16),
            jax.ShapeDtypeStruct((1,), jnp.float32),
        ),
        in_specs=[smem, smem] + [hbm] * 11,
        out_specs=(hbm, smem),
        scratch_shapes=[
            pltpu.VMEM((parts, height, part), jnp.bfloat16),
            pltpu.VMEM(squares.shape, jnp.float32),
            pltpu.VMEM((parts, part, columns), jnp.bfloat16),
            pltpu.VMEM((sampled, *block), jnp.bfloat16),
            pltpu.VMEM((slots, *block), jnp.bfloat16),
            pltpu.VMEM((parts, rows, part), jnp.bfloat16),
            pltpu.VMEM((rows, columns), jnp.float32),
            pltpu.VMEM((sampled, *block), jnp.bfloat16),
            pltpu.SemaphoreType.DMA((3 * parts + 2,)),
        ],
        compiler_params=pltpu.CompilerParams(vmem_limit_bytes=VMEM_BYTES),
        cost_estimate=pl.CostEstimate(
            flops=2 * rows * width * columns, bytes_accessed=18 << 20, transcendentals=rows
        ),
        name="base_gap",
    )(
        slot_of, order, *far, *mine, *near, *other, squares, frozen, taken,
    )


def trainer_kernel(gap, lowered, up, facts, grad_up, back, sent, loss):
    step = pl.program_id(0)
    low = lowered[...]
    up_map = up[...]
    facts_now = facts[...]
    distance = gap[...].astype(jnp.float32) + lax.dot_general(
        low, up_map, CONTRACT_FIRST, preferred_element_type=jnp.float32
    )
    output_grad = (facts_now[:, NB : NB + 1] * distance).astype(jnp.bfloat16)
    squares = jnp.sum(distance * distance, axis=1, keepdims=True)
    part = jnp.sum(facts_now * squares, axis=0, keepdims=True)
    back_now = lax.dot_general(
        up_map, output_grad, CONTRACT_LAST, preferred_element_type=jnp.float32
    )
    back[...] = back_now
    rank = up_map.shape[0]
    lanes = loss.shape[1]
    sent[0:rank] = back_now.astype(jnp.bfloat16)
    sent[rank:] = jnp.zeros((sent.shape[0] - rank, sent.shape[1]), jnp.bfloat16)
    own = jnp.dot(low, output_grad, preferred_element_type=jnp.float32)

    @pl.when(step == 0)
    def _():
        grad_up[...] = own
        loss[...] = part

    @pl.when(step > 0)
    def _():
        grad_up[...] += own
        loss[...] += part

    @pl.when(step == pl.num_programs(0) - 1)
    def _():
        sent[rank:, 0:lanes] = in_three(loss[...], sent.shape[0] - rank)


def trainer_step(gap, lowered, up, facts):
    rows, columns = gap.shape
    rank = up.shape[0]
    lanes = facts.shape[1]
    chunk = LAST_CHUNK
    return pl.pallas_call(
        trainer_kernel,
        grid=(rows // chunk,),
        out_shape=(
            jax.ShapeDtypeStruct((rank, columns), jnp.float32),
            jax.ShapeDtypeStruct((rank, rows), jnp.float32),
            jax.ShapeDtypeStruct((rank + 16, rows), jnp.bfloat16),
            jax.ShapeDtypeStruct((1, lanes), jnp.float32),
        ),
        in_specs=[
            pl.BlockSpec((chunk, columns), lambda i: (i, 0)),
            pl.BlockSpec((rank, chunk), lambda i: (0, i)),
            pl.BlockSpec((rank, columns), lambda i: (0, 0)),
            pl.BlockSpec((chunk, lanes), lambda i: (i, 0)),
        ],
        out_specs=(
            pl.BlockSpec((rank, columns), lambda i: (0, 0)),
            pl.BlockSpec((rank, chunk), lambda i: (0, i)),
            pl.BlockSpec((rank + 16, chunk), lambda i: (0, i)),
            pl.BlockSpec((1, lanes), lambda i: (0, 0)),
        ),
        compiler_params=pltpu.CompilerParams(vmem_limit_bytes=VMEM_BYTES),
        cost_estimate=pl.CostEstimate(
            flops=6 * rows * rank * columns, bytes_accessed=4 << 20, transcendentals=0
        ),
        name="trainer_step",
    )(gap, lowered, up, facts)


def pair_kernel(back, loss, got, pair, pair_loss, sent):
    rank, rows = back.shape
    lanes = loss.shape[1]
    at = slice(rows - LAST_CHUNK, rows - LAST_CHUNK + lanes)
    total = back[...] + got[0:rank].astype(jnp.float32)
    pair[...] = total
    sent[0:rank] = total.astype(jnp.bfloat16)
    three = got[rank:, at].astype(jnp.float32)
    whole = loss[...] + (three[0:1] + three[1:2] + three[2:3])
    pair_loss[...] = whole
    height = sent.shape[0] - rank
    sent[rank:] = jnp.zeros((height, rows), jnp.bfloat16)
    sent[rank:, at] = in_three(whole, height)


def pair_step(back, loss, got):
    vmem = pl.BlockSpec(memory_space=pltpu.VMEM)
    return pl.pallas_call(
        pair_kernel,
        out_shape=(
            jax.ShapeDtypeStruct(back.shape, jnp.float32),
            jax.ShapeDtypeStruct(loss.shape, jnp.float32),
            jax.ShapeDtypeStruct(got.shape, jnp.bfloat16),
        ),
        in_specs=[vmem] * 3,
        out_specs=(vmem, vmem, vmem),
        compiler_params=pltpu.CompilerParams(vmem_limit_bytes=VMEM_BYTES),
        cost_estimate=pl.CostEstimate(flops=1 << 17, bytes_accessed=1 << 20, transcendentals=0),
        name="pair_step",
    )(back, loss, got)


def down_kernel(pair, got, normed, grad_down):
    rank = pair.shape[0]
    back = pair[...] + got[0:rank].astype(jnp.float32)
    lowered_gradient = (ADAPTER_SCALING * back).astype(jnp.bfloat16)
    grad_down[...] = jnp.dot(
        lowered_gradient, normed[...], preferred_element_type=jnp.float32
    )


def down_step(pair, got, normed):
    rank, rows = pair.shape
    columns = normed.shape[1]
    vmem = pl.BlockSpec(memory_space=pltpu.VMEM)
    return pl.pallas_call(
        down_kernel,
        out_shape=jax.ShapeDtypeStruct((rank, columns), jnp.float32),
        in_specs=[vmem] * 3,
        out_specs=vmem,
        compiler_params=pltpu.CompilerParams(vmem_limit_bytes=VMEM_BYTES),
        cost_estimate=pl.CostEstimate(
            flops=2 * rows * rank * columns, bytes_accessed=3 << 20, transcendentals=0
        ),
        name="down_step",
    )(pair, got, normed)


def on_device(
    pool_inputs,
    pool_targets,
    frozen,
    gain,
    adapter_down,
    adapter_up,
    sample_ids,
    buckets,
    lengths,
    destinations,
    competence,
):
    trainers = lax.axis_size(DP)
    sampled = sample_ids.shape[0]
    _, block_len, part = pool_inputs.shape
    width = frozen.shape[0]
    slots = trainers * PER_PAIR
    rows = slots * block_len
    per_peer = PER_PAIR * block_len
    down_map = adapter_down[0]
    up_map = adapter_up[0]
    bucket_range = jnp.arange(NB, dtype=jnp.int32)

    send_x, own_first, own_last, slot_of = route(
        sample_ids, destinations[:, 0], buckets, lengths, pool_inputs, gain, trainers
    )
    got_x = lax.all_to_all(send_x, DP, 0, 0, tiled=True)
    mine = (own_first.reshape(-1, part), own_last.reshape(-1, part))
    near, other, far = from_parts(*mine, "mp")
    order = lax.axis_index("mp") ^ jnp.arange(lax.axis_size("mp"), dtype=jnp.int32)
    taken, near_squares = early_part(sample_ids, mine, near, other, pool_targets)
    send_gap, done = base_gap_slots(
        slot_of, order, mine, near, other, far, taken, near_squares, frozen
    )
    got_gap = lax.all_to_all(
        send_gap.reshape(trainers, per_peer, part), DP, 0, 0, tiled=True
    )

    got_info = got_x[:, -1, 0, : 2 * PER_PAIR].astype(jnp.float32).astype(jnp.int32)
    got_counts = got_x[:, -1, 1:3, :NB].astype(jnp.float32)
    counts = jnp.sum(16.0 * got_counts[:, 0] + got_counts[:, 1], axis=0)
    floor_counts = jnp.maximum(counts, 1.0)
    weights = jax.nn.sigmoid(
        SHARPNESS * (competence[0] - (bucket_range.astype(jnp.float32) + 0.5) / NB)
    )
    row_bucket = jnp.repeat(got_info[:, :PER_PAIR].reshape(slots), block_len)
    row_length = jnp.repeat(got_info[:, PER_PAIR:].reshape(slots), block_len)
    live = (jnp.arange(rows, dtype=jnp.int32) % block_len < row_length).astype(jnp.float32)
    onehot = (row_bucket[:, None] == bucket_range[None, :]).astype(jnp.float32) * live[:, None]
    coefficient = 2.0 * jnp.sum(onehot * (weights / floor_counts)[None, :], axis=1)
    facts = jnp.concatenate(
        [onehot, coefficient[:, None], jnp.zeros((rows, 128 - NB - 1), jnp.float32)], axis=1
    )

    mean_squares = over_parts(row_squares(got_x, done), "mp") / width
    normed, latent_part = latents(got_x, mean_squares, gain, down_map)
    lowered = (ADAPTER_SCALING * over_parts(latent_part, "mp")).astype(jnp.bfloat16)

    grad_up, back_part, back_sent, loss_part = trainer_step(
        got_gap.reshape(rows, part), lowered, up_map, facts
    )
    pair, pair_loss, pair_sent = pair_step(back_part, loss_part, swap(back_sent, "mp", 1))
    got_pair = swap(pair_sent, "mp", 3)
    rank = up_map.shape[0]
    at = rows - LAST_CHUNK
    three = got_pair[rank : rank + 3, at : at + NB].astype(jnp.float32)
    own_loss = pair_loss[0, :NB] + (three[0] + three[1] + three[2])
    loss_sum = jnp.sum(
        lax.all_to_all(jnp.broadcast_to(own_loss, (trainers, 1, NB)), DP, 0, 0, tiled=True),
        axis=(0, 1),
    )
    grad_down = down_step(pair, got_pair, normed)
    bucket_loss = loss_sum / (floor_counts * width)
    progress = jnp.sum(weights * bucket_loss) / jnp.sum(bucket_loss)
    competence_next = competence + 0.5 * (1.0 - competence) * progress
    return (grad_down[None], grad_up[None], bucket_loss, competence_next)


def solution(mesh):
    split = Mesh(mesh.devices.reshape(4, 8, 2, mesh.shape["mp"]), DP_MP)
    placed = (
        P(DP, None, "mp"),
        P(DP, None, "mp"),
        P(None, "mp"),
        P("mp"),
        P(DP, None, "mp"),
        P(DP, None, "mp"),
        P(DP),
        P(DP),
        P(DP),
        P(DP, None),
        P(),
    )
    return jax.shard_map(
        on_device,
        mesh=split,
        in_specs=placed,
        out_specs=(P(DP, None, "mp"), P(DP, None, "mp"), P(), P()),
        check_vma=False,
    )
```

```python
import jax
import jax.numpy as jnp
from jax import lax
from jax.experimental import pallas as pl
from jax.experimental.pallas import tpu as pltpu
from jax.sharding import Mesh
from jax.sharding import PartitionSpec as P

NB = 16
DP = ("dp_0", "dp_1", "dp_2")
DP_MP = ("dp_0", "dp_1", "dp_2", "mp")

RMS_EPSILON = 1e-05
SHARPNESS = 12.0
ADAPTER_SCALING = 2.0
PER_PAIR = 2
TILES = 1
LAST_CHUNK = 512
VMEM_BYTES = 62 * 1024 * 1024
SMALL_VMEM_BYTES = 16 * 1024 * 1024
CONTRACT_LAST = (((1,), (1,)), ((), ()))
CONTRACT_FIRST = (((0,), (0,)), ((), ()))


def swap(value, axis, distance):
    peers = lax.axis_size(axis)
    return lax.ppermute(value, axis, [(i, i ^ distance) for i in range(peers)])


def over_parts(value, axis):
    pair = value + swap(value, axis, 1)
    return pair + swap(pair, axis, 3)


def in_three(row, height):
    high = row.astype(jnp.bfloat16).astype(jnp.float32)
    middle = (row - high).astype(jnp.bfloat16).astype(jnp.float32)
    low = row - high - middle
    zeros = jnp.zeros((height - 3, row.shape[1]), jnp.float32)
    return jnp.concatenate([high, middle, low, zeros], axis=0).astype(jnp.bfloat16)


def from_parts(first, last, axis):
    other_first = swap(first, axis, 3)
    near_last = swap(last, axis, 1)
    near_first = swap(first, axis, 1)
    other_last = swap(last, axis, 3)
    far = (swap(other_first, axis, 1), swap(near_last, axis, 3))
    return (near_first, near_last), (other_first, other_last), far


def lane_group(packed, group, groups):
    slots = [packed[:, s * groups + group][:, None] for s in range(PER_PAIR)]
    whole = jnp.concatenate(slots, axis=1).astype(jnp.float32)
    return whole.reshape(-1, packed.shape[-1])


def square_kernel(packed, done, total):
    groups = (packed.shape[1] - 1) // PER_PAIR
    sums = None
    for g in range(groups):
        x = lane_group(packed, g, groups)
        sums = x * x if sums is None else sums + x * x
    total[...] = jnp.sum(sums.T, axis=0, keepdims=True) + done[0]


def row_squares(packed, done):
    peers, pieces, block_len, lanes = packed.shape
    rows = peers * PER_PAIR * block_len
    chunk = 16
    return pl.pallas_call(
        square_kernel,
        grid=(peers // chunk,),
        out_shape=jax.ShapeDtypeStruct((1, rows), jnp.float32),
        in_specs=[
            pl.BlockSpec((chunk, pieces, block_len, lanes), lambda i: (i, 0, 0, 0)),
            pl.BlockSpec(memory_space=pltpu.SMEM),
        ],
        out_specs=pl.BlockSpec((1, rows * chunk // peers), lambda i: (0, i)),
        compiler_params=pltpu.CompilerParams(vmem_limit_bytes=VMEM_BYTES),
        cost_estimate=pl.CostEstimate(flops=4 << 20, bytes_accessed=2 << 20, transcendentals=0),
        name="row_squares",
    )(packed, done)


def latent_kernel(packed, squares, gain, down, normed, latent):
    lanes = packed.shape[-1]
    groups = (packed.shape[1] - 1) // PER_PAIR
    inverse = lax.rsqrt(squares[...] + RMS_EPSILON)
    inverse = jnp.broadcast_to(inverse, (lanes, inverse.shape[1])).T
    for g in range(groups):
        at = slice(g * lanes, (g + 1) * lanes)
        x = lane_group(packed, g, groups)
        normed[:, at] = (x * inverse * gain[:, at]).astype(jnp.bfloat16)
    latent[...] = lax.dot_general(
        down[...], normed[...], CONTRACT_LAST, preferred_element_type=jnp.float32
    )


def latents(packed, mean_squares, gain, down):
    peers, pieces, block_len, lanes = packed.shape
    rows = peers * PER_PAIR * block_len
    rank, columns = down.shape
    chunk = 16
    part = rows * chunk // peers
    return pl.pallas_call(
        latent_kernel,
        grid=(peers // chunk,),
        out_shape=(
            jax.ShapeDtypeStruct((rows, columns), jnp.bfloat16),
            jax.ShapeDtypeStruct((rank, rows), jnp.float32),
        ),
        in_specs=[
            pl.BlockSpec((chunk, pieces, block_len, lanes), lambda i: (i, 0, 0, 0)),
            pl.BlockSpec((1, part), lambda i: (0, i)),
            pl.BlockSpec((1, columns), lambda i: (0, 0)),
            pl.BlockSpec((rank, columns), lambda i: (0, 0)),
        ],
        out_specs=(
            pl.BlockSpec((part, columns), lambda i: (i, 0)),
            pl.BlockSpec((rank, part), lambda i: (0, i)),
        ),
        compiler_params=pltpu.CompilerParams(vmem_limit_bytes=VMEM_BYTES),
        cost_estimate=pl.CostEstimate(
            flops=2 * rows * rank * columns, bytes_accessed=4 << 20, transcendentals=rows
        ),
        name="latents",
    )(packed, mean_squares, gain[None, :], down)


def route_kernel(
    ids_in, dest_in, buckets_in, lengths_in, pool_in, gain_in,
    send_out, first_out, last_out, slot_of,
    ids, dest, buckets, lengths, pool, gain, send, own, arrived, info, counts, sem,
):
    pairs = (
        (pool_in, pool),
        (ids_in, ids),
        (dest_in, dest),
        (buckets_in, buckets),
        (lengths_in, lengths),
        (gain_in, gain),
    )
    copies = [
        pltpu.make_async_copy(source, target, sem.at[i])
        for i, (source, target) in enumerate(pairs)
    ]
    for copy in copies:
        copy.start()
    sampled = ids.shape[0]
    trainers, pieces, block_len, lanes = send.shape
    groups = (pieces - 1) // PER_PAIR

    def clear(k, carry):
        arrived[k] = 0
        for s in range(PER_PAIR):
            info[s, k] = 0
            info[PER_PAIR + s, k] = 0
        return carry

    def clear_counts(b, carry):
        counts[b] = 0
        return carry

    lax.fori_loop(0, trainers, clear, 0, unroll=8)
    lax.fori_loop(0, NB, clear_counts, 0, unroll=8)
    for copy in copies:
        copy.wait()

    def place(j, carry):
        block = ids[j]
        trainer = dest[j]
        values = pool[block]
        own[j] = values
        order = arrived[trainer]
        arrived[trainer] = order + 1
        slot = trainer * PER_PAIR + order
        for g in range(groups):
            send[trainer, order * groups + g] = values[:, g * lanes : (g + 1) * lanes]
        slot_of[j] = slot
        bucket = buckets[block]
        length = lengths[block]
        info[order, trainer] = bucket
        info[PER_PAIR + order, trainer] = length
        counts[bucket] = counts[bucket] + length
        return carry

    lax.fori_loop(0, sampled, place, 0, unroll=8)
    whole = gain[...]
    high = whole.astype(jnp.bfloat16).astype(jnp.float32)
    middle = (whole - high).astype(jnp.bfloat16).astype(jnp.float32)
    low = whole - high - middle
    zeros = jnp.zeros((own.shape[1] - 3, whole.shape[1]), jnp.float32)
    own[sampled] = jnp.concatenate([high, middle, low, zeros], axis=0).astype(jnp.bfloat16)
    own[sampled + 1] = jnp.zeros(own.shape[1:], own.dtype)
    cut = first_out.shape[0]
    own_copies = (
        pltpu.make_async_copy(own.at[pl.ds(0, cut)], first_out, sem.at[1]),
        pltpu.make_async_copy(own.at[pl.ds(cut, last_out.shape[0])], last_out, sem.at[2]),
    )
    for copy in own_copies:
        copy.start()

    row = lax.broadcasted_iota(jnp.int32, (block_len, lanes), 0)
    lane = lax.broadcasted_iota(jnp.int32, (block_len, lanes), 1)
    holder = jnp.zeros((block_len, lanes), jnp.int32)
    for b in range(NB):
        count = counts[b]
        holder = jnp.where((row == 1) & (lane == b), count // 16, holder)
        holder = jnp.where((row == 2) & (lane == b), count % 16, holder)

    def finish(k, found):
        for s in range(PER_PAIR):
            free = arrived[k] <= s

            @pl.when(free)
            def _():
                slot_of[sampled + found] = k * PER_PAIR + s
                for g in range(groups):
                    send[k, s * groups + g] = jnp.zeros((block_len, lanes), send.dtype)

            found = found + jnp.where(free, 1, 0)
        facts = holder
        for i in range(2 * PER_PAIR):
            facts = jnp.where((row == 0) & (lane == i), info[i, k], facts)
        send[k, pieces - 1] = facts.astype(jnp.float32).astype(send.dtype)
        return found

    quarter = trainers // 4
    found = 0
    send_copies = []
    for q in range(4):
        found = lax.fori_loop(q * quarter, (q + 1) * quarter, finish, found, unroll=8)
        part = pl.ds(q * quarter, quarter)
        copy = pltpu.make_async_copy(send.at[part], send_out.at[part], sem.at[3 + q])
        copy.start()
        send_copies.append(copy)
    for copy in (*own_copies, *send_copies):
        copy.wait()


def route(ids, dest, buckets, lengths, pool, gain, trainers):
    sampled = ids.shape[0]
    slots = trainers * PER_PAIR
    block = pool.shape[1:]
    lanes = 128
    message = (trainers, PER_PAIR * (block[1] // lanes) + 1, block[0], lanes)
    smem = pl.BlockSpec(memory_space=pltpu.SMEM)
    hbm = pl.BlockSpec(memory_space=pltpu.HBM)
    return pl.pallas_call(
        route_kernel,
        out_shape=(
            jax.ShapeDtypeStruct(message, pool.dtype),
            jax.ShapeDtypeStruct((sampled // 2, *block), pool.dtype),
            jax.ShapeDtypeStruct((sampled - sampled // 2 + 2, *block), pool.dtype),
            jax.ShapeDtypeStruct((slots,), jnp.int32),
        ),
        in_specs=[hbm] * 6,
        out_specs=(hbm, hbm, hbm, smem),
        scratch_shapes=[
            pltpu.SMEM(ids.shape, jnp.int32),
            pltpu.SMEM(dest.shape, jnp.int32),
            pltpu.SMEM(buckets.shape, jnp.int32),
            pltpu.SMEM(lengths.shape, jnp.int32),
            pltpu.VMEM(pool.shape, pool.dtype),
            pltpu.VMEM((1, gain.shape[0]), jnp.float32),
            pltpu.VMEM(message, pool.dtype),
            pltpu.VMEM((sampled + 2, *block), pool.dtype),
            pltpu.SMEM((trainers,), jnp.int32),
            pltpu.SMEM((2 * PER_PAIR, trainers), jnp.int32),
            pltpu.SMEM((NB,), jnp.int32),
            pltpu.SemaphoreType.DMA((7,)),
        ],
        compiler_params=pltpu.CompilerParams(vmem_limit_bytes=VMEM_BYTES),
        cost_estimate=pl.CostEstimate(flops=0, bytes_accessed=5 << 20, transcendentals=0),
        name="route",
    )(ids, dest, buckets, lengths, pool, gain[None, :])


def early_kernel(
    ids, mine_first, mine_last, near_first, near_last, other_first, other_last, targets,
    taken, squares,
):
    step = pl.program_id(0)
    half = pl.num_programs(0) // 2
    part = near_first.shape[1]
    lanes = squares.shape[1]
    blocks = taken.shape[0]

    def add_squares(pieces):
        sums = jnp.zeros(squares.shape, jnp.float32)
        for g in range(part // lanes):
            at = slice(g * lanes, (g + 1) * lanes)
            for piece in pieces:
                x = piece[:, at].astype(jnp.float32)
                sums = sums + x * x
        squares[...] = sums

    @pl.when(step < half)
    def _():
        add_squares((mine_first, near_first, other_first))

    @pl.when(step >= half)
    def _():
        add_squares((mine_last, near_last, other_last))

    def take(j, carry):
        taken[j] = targets[ids[step * blocks + j]]
        return carry

    lax.fori_loop(0, blocks, take, 0, unroll=4)


def early_part(ids, mine, near, other, targets):
    part = near[0].shape[1]
    block = targets.shape[1:]
    sampled = ids.shape[0]
    rows = sampled * block[0]
    chunk = 128
    blocks = chunk // block[0]
    half = rows // chunk // 2
    lanes = 128
    first = pl.BlockSpec((chunk, part), lambda n: (jnp.minimum(n, half - 1), 0))
    last = pl.BlockSpec((chunk, part), lambda n: (jnp.maximum(n - half, 0), 0))
    return pl.pallas_call(
        early_kernel,
        grid=(rows // chunk,),
        out_shape=(
            jax.ShapeDtypeStruct((sampled, *block), jnp.bfloat16),
            jax.ShapeDtypeStruct((rows, lanes), jnp.float32),
        ),
        in_specs=[pl.BlockSpec(memory_space=pltpu.SMEM)]
        + [first, last] * 3
        + [pl.BlockSpec(targets.shape, lambda n: (0, 0, 0))],
        out_specs=(
            pl.BlockSpec((blocks, *block), lambda n: (n, 0, 0)),
            pl.BlockSpec((chunk, lanes), lambda n: (n, 0)),
        ),
        compiler_params=pltpu.CompilerParams(vmem_limit_bytes=VMEM_BYTES),
        cost_estimate=pl.CostEstimate(flops=6 << 20, bytes_accessed=7 << 20, transcendentals=0),
        name="early_part",
    )(ids, *mine, *near, *other, targets)


def gap_kernel(
    slot_of, order, far_first, far_last, mine_first, mine_last, near_first, near_last,
    other_first, other_last, squares_in, frozen_in, taken_in,
    send_out, done, pieces, squares, frozen, taken, send, normed, total, gap, sem,
):
    parts, _, part = pieces.shape
    sampled, block_len, columns = gap.shape
    rows = sampled * block_len
    cut = far_first.shape[0]
    slots = send.shape[0]
    places = (2, 0, 1, 3)
    halves = (
        (far_first, far_last),
        (mine_first, mine_last),
        (near_first, near_last),
        (other_first, other_last),
    )
    copies = [
        (
            pltpu.make_async_copy(first, pieces.at[i, pl.ds(0, cut)], sem.at[2 * i]),
            pltpu.make_async_copy(
                last, pieces.at[i, pl.ds(cut, last.shape[0])], sem.at[2 * i + 1]
            ),
        )
        for i, (first, last) in enumerate(halves)
    ]
    squares_copy = pltpu.make_async_copy(squares_in, squares, sem.at[2 * parts])
    taken_copy = pltpu.make_async_copy(taken_in, taken, sem.at[2 * parts + 1])
    weights = [
        pltpu.make_async_copy(
            frozen_in.at[pl.ds(pl.multiple_of(order[places[i]] * part, part), part)],
            frozen.at[i],
            sem.at[2 * parts + 2 + i],
        )
        for i in range(parts)
    ]
    squares_copy.start()
    for i in range(parts):
        for copy in copies[i]:
            copy.start()
        weights[i].start()
    taken_copy.start()
    done[0] = 0.0

    def fill(s, carry):
        send[slot_of[sampled + s]] = jnp.zeros((block_len, columns), jnp.bfloat16)
        return carry

    lax.fori_loop(0, slots - sampled, fill, 0, unroll=8)
    squares_copy.wait()
    for copy in copies[0]:
        copy.wait()
    chunk = 128

    def invert(r):
        at = slice(r * chunk, (r + 1) * chunk)
        x = pieces[0, at].astype(jnp.float32)
        sums = squares[at]
        lanes = sums.shape[1]
        for g in range(part // lanes):
            sums = sums + x[:, g * lanes : (g + 1) * lanes] * x[:, g * lanes : (g + 1) * lanes]
        mean = jnp.sum(sums, axis=1, keepdims=True) / (parts * part)
        squares[at] = jnp.broadcast_to(lax.rsqrt(mean + RMS_EPSILON), sums.shape)

    def normalize(i, r):
        at = slice(r * chunk, (r + 1) * chunk)
        three = pieces[i, rows : rows + 16].astype(jnp.float32)
        gain = three[0:1] + three[1:2] + three[2:3]
        x = pieces[i, at].astype(jnp.float32)
        normed[i, at] = (x * squares[at, 0:1] * gain).astype(jnp.bfloat16)

    chunks = rows // chunk
    for r in range(chunks):
        invert(r)
        normalize(0, r)
    tile = columns // TILES
    for i in range(parts):
        weights[i].wait()
        if i + 1 < parts:
            for copy in copies[i + 1]:
                copy.wait()
        else:
            taken_copy.wait()
        for n in range(TILES):
            at = slice(n * tile, (n + 1) * tile)
            product = jnp.dot(
                normed[i], frozen[i, :, at], preferred_element_type=jnp.float32
            )
            if i > 0:
                product = total[:, at] + product
            if i + 1 < parts:
                total[:, at] = product
                for r in range(n * chunks // TILES, (n + 1) * chunks // TILES):
                    normalize(i + 1, r)
            else:
                x = pieces[1, :rows, at].astype(jnp.float32)
                whole = (x + product).reshape(sampled, block_len, tile)
                gap[:, :, at] = (whole - taken[:, :, at].astype(jnp.float32)).astype(jnp.bfloat16)

    def place(j, carry):
        send[slot_of[j]] = gap[j]
        return carry

    lax.fori_loop(0, sampled, place, 0, unroll=8)
    copy = pltpu.make_async_copy(send, send_out, sem.at[0])
    copy.start()
    copy.wait()


def base_gap_slots(slot_of, order, mine, near, other, far, taken, squares, frozen):
    part = mine[0].shape[1]
    height = mine[0].shape[0] + mine[1].shape[0]
    width, columns = frozen.shape
    slots = slot_of.shape[0]
    sampled, *block = taken.shape
    rows = sampled * block[0]
    parts = width // part
    smem = pl.BlockSpec(memory_space=pltpu.SMEM)
    hbm = pl.BlockSpec(memory_space=pltpu.HBM)
    return pl.pallas_call(
        gap_kernel,
        out_shape=(
            jax.ShapeDtypeStruct((slots, *block), jnp.bfloat16),
            jax.ShapeDtypeStruct((1,), jnp.float32),
        ),
        in_specs=[smem, smem] + [hbm] * 11,
        out_specs=(hbm, smem),
        scratch_shapes=[
            pltpu.VMEM((parts, height, part), jnp.bfloat16),
            pltpu.VMEM(squares.shape, jnp.float32),
            pltpu.VMEM((parts, part, columns), jnp.bfloat16),
            pltpu.VMEM((sampled, *block), jnp.bfloat16),
            pltpu.VMEM((slots, *block), jnp.bfloat16),
            pltpu.VMEM((parts, rows, part), jnp.bfloat16),
            pltpu.VMEM((rows, columns), jnp.float32),
            pltpu.VMEM((sampled, *block), jnp.bfloat16),
            pltpu.SemaphoreType.DMA((3 * parts + 2,)),
        ],
        compiler_params=pltpu.CompilerParams(vmem_limit_bytes=VMEM_BYTES),
        cost_estimate=pl.CostEstimate(
            flops=2 * rows * width * columns, bytes_accessed=18 << 20, transcendentals=rows
        ),
        name="base_gap",
    )(
        slot_of, order, *far, *mine, *near, *other, squares, frozen, taken,
    )


def trainer_kernel(gap, lowered, up, facts, grad_up, back, sent, loss):
    step = pl.program_id(0)
    low = lowered[...]
    up_map = up[...]
    facts_now = facts[...]
    distance = gap[...].astype(jnp.float32) + lax.dot_general(
        low, up_map, CONTRACT_FIRST, preferred_element_type=jnp.float32
    )
    output_grad = (facts_now[:, NB : NB + 1] * distance).astype(jnp.bfloat16)
    squares = jnp.sum(distance * distance, axis=1, keepdims=True)
    part = jnp.sum(facts_now * squares, axis=0, keepdims=True)
    back_now = lax.dot_general(
        up_map, output_grad, CONTRACT_LAST, preferred_element_type=jnp.float32
    )
    back[...] = back_now
    rank = up_map.shape[0]
    lanes = loss.shape[1]
    sent[0:rank] = back_now.astype(jnp.bfloat16)
    sent[rank:] = jnp.zeros((sent.shape[0] - rank, sent.shape[1]), jnp.bfloat16)
    own = jnp.dot(low, output_grad, preferred_element_type=jnp.float32)

    @pl.when(step == 0)
    def _():
        grad_up[...] = own
        loss[...] = part

    @pl.when(step > 0)
    def _():
        grad_up[...] += own
        loss[...] += part

    @pl.when(step == pl.num_programs(0) - 1)
    def _():
        sent[rank:, 0:lanes] = in_three(loss[...], sent.shape[0] - rank)


def trainer_step(gap, lowered, up, facts):
    rows, columns = gap.shape
    rank = up.shape[0]
    lanes = facts.shape[1]
    chunk = LAST_CHUNK
    return pl.pallas_call(
        trainer_kernel,
        grid=(rows // chunk,),
        out_shape=(
            jax.ShapeDtypeStruct((rank, columns), jnp.float32),
            jax.ShapeDtypeStruct((rank, rows), jnp.float32),
            jax.ShapeDtypeStruct((rank + 16, rows), jnp.bfloat16),
            jax.ShapeDtypeStruct((1, lanes), jnp.float32),
        ),
        in_specs=[
            pl.BlockSpec((chunk, columns), lambda i: (i, 0)),
            pl.BlockSpec((rank, chunk), lambda i: (0, i)),
            pl.BlockSpec((rank, columns), lambda i: (0, 0)),
            pl.BlockSpec((chunk, lanes), lambda i: (i, 0)),
        ],
        out_specs=(
            pl.BlockSpec((rank, columns), lambda i: (0, 0)),
            pl.BlockSpec((rank, chunk), lambda i: (0, i)),
            pl.BlockSpec((rank + 16, chunk), lambda i: (0, i)),
            pl.BlockSpec((1, lanes), lambda i: (0, 0)),
        ),
        compiler_params=pltpu.CompilerParams(vmem_limit_bytes=VMEM_BYTES),
        cost_estimate=pl.CostEstimate(
            flops=6 * rows * rank * columns, bytes_accessed=4 << 20, transcendentals=0
        ),
        name="trainer_step",
    )(gap, lowered, up, facts)


def pair_kernel(back, loss, got, pair, pair_loss, sent):
    rank, rows = back.shape
    lanes = loss.shape[1]
    at = slice(rows - LAST_CHUNK, rows - LAST_CHUNK + lanes)
    total = back[...] + got[0:rank].astype(jnp.float32)
    pair[...] = total
    sent[0:rank] = total.astype(jnp.bfloat16)
    three = got[rank:, at].astype(jnp.float32)
    whole = loss[...] + (three[0:1] + three[1:2] + three[2:3])
    pair_loss[...] = whole
    height = sent.shape[0] - rank
    sent[rank:] = jnp.zeros((height, rows), jnp.bfloat16)
    sent[rank:, at] = in_three(whole, height)


def pair_step(back, loss, got):
    vmem = pl.BlockSpec(memory_space=pltpu.VMEM)
    return pl.pallas_call(
        pair_kernel,
        out_shape=(
            jax.ShapeDtypeStruct(back.shape, jnp.float32),
            jax.ShapeDtypeStruct(loss.shape, jnp.float32),
            jax.ShapeDtypeStruct(got.shape, jnp.bfloat16),
        ),
        in_specs=[vmem] * 3,
        out_specs=(vmem, vmem, vmem),
        compiler_params=pltpu.CompilerParams(vmem_limit_bytes=SMALL_VMEM_BYTES),
        cost_estimate=pl.CostEstimate(flops=1 << 17, bytes_accessed=1 << 20, transcendentals=0),
        name="pair_step",
    )(back, loss, got)


def down_kernel(pair, got, normed, grad_down):
    rank = pair.shape[0]
    back = pair[...] + got[0:rank].astype(jnp.float32)
    lowered_gradient = (ADAPTER_SCALING * back).astype(jnp.bfloat16)
    grad_down[...] = jnp.dot(
        lowered_gradient, normed[...], preferred_element_type=jnp.float32
    )


def down_step(pair, got, normed):
    rank, rows = pair.shape
    columns = normed.shape[1]
    vmem = pl.BlockSpec(memory_space=pltpu.VMEM)
    return pl.pallas_call(
        down_kernel,
        out_shape=jax.ShapeDtypeStruct((rank, columns), jnp.float32),
        in_specs=[vmem] * 3,
        out_specs=vmem,
        compiler_params=pltpu.CompilerParams(vmem_limit_bytes=SMALL_VMEM_BYTES),
        cost_estimate=pl.CostEstimate(
            flops=2 * rows * rank * columns, bytes_accessed=3 << 20, transcendentals=0
        ),
        name="down_step",
    )(pair, got, normed)


def on_device(
    pool_inputs,
    pool_targets,
    frozen,
    gain,
    adapter_down,
    adapter_up,
    sample_ids,
    buckets,
    lengths,
    destinations,
    competence,
):
    trainers = lax.axis_size(DP)
    sampled = sample_ids.shape[0]
    _, block_len, part = pool_inputs.shape
    width = frozen.shape[0]
    slots = trainers * PER_PAIR
    rows = slots * block_len
    per_peer = PER_PAIR * block_len
    down_map = adapter_down[0]
    up_map = adapter_up[0]
    bucket_range = jnp.arange(NB, dtype=jnp.int32)

    send_x, own_first, own_last, slot_of = route(
        sample_ids, destinations[:, 0], buckets, lengths, pool_inputs, gain, trainers
    )
    got_x = lax.all_to_all(send_x, DP, 0, 0, tiled=True)
    mine = (own_first.reshape(-1, part), own_last.reshape(-1, part))
    near, other, far = from_parts(*mine, "mp")
    order = lax.axis_index("mp") ^ jnp.arange(lax.axis_size("mp"), dtype=jnp.int32)
    taken, near_squares = early_part(sample_ids, mine, near, other, pool_targets)
    send_gap, done = base_gap_slots(
        slot_of, order, mine, near, other, far, taken, near_squares, frozen
    )
    got_gap = lax.all_to_all(
        send_gap.reshape(trainers, per_peer, part), DP, 0, 0, tiled=True
    )

    got_info = got_x[:, -1, 0, : 2 * PER_PAIR].astype(jnp.float32).astype(jnp.int32)
    got_counts = got_x[:, -1, 1:3, :NB].astype(jnp.float32)
    counts = jnp.sum(16.0 * got_counts[:, 0] + got_counts[:, 1], axis=0)
    floor_counts = jnp.maximum(counts, 1.0)
    weights = jax.nn.sigmoid(
        SHARPNESS * (competence[0] - (bucket_range.astype(jnp.float32) + 0.5) / NB)
    )
    row_bucket = jnp.repeat(got_info[:, :PER_PAIR].reshape(slots), block_len)
    row_length = jnp.repeat(got_info[:, PER_PAIR:].reshape(slots), block_len)
    live = (jnp.arange(rows, dtype=jnp.int32) % block_len < row_length).astype(jnp.float32)
    onehot = (row_bucket[:, None] == bucket_range[None, :]).astype(jnp.float32) * live[:, None]
    coefficient = 2.0 * jnp.sum(onehot * (weights / floor_counts)[None, :], axis=1)
    facts = jnp.concatenate(
        [onehot, coefficient[:, None], jnp.zeros((rows, 128 - NB - 1), jnp.float32)], axis=1
    )

    mean_squares = over_parts(row_squares(got_x, done), "mp") / width
    normed, latent_part = latents(got_x, mean_squares, gain, down_map)
    lowered = (ADAPTER_SCALING * over_parts(latent_part, "mp")).astype(jnp.bfloat16)

    grad_up, back_part, back_sent, loss_part = trainer_step(
        got_gap.reshape(rows, part), lowered, up_map, facts
    )
    pair, pair_loss, pair_sent = pair_step(back_part, loss_part, swap(back_sent, "mp", 1))
    got_pair = swap(pair_sent, "mp", 3)
    rank = up_map.shape[0]
    at = rows - LAST_CHUNK
    three = got_pair[rank : rank + 3, at : at + NB].astype(jnp.float32)
    own_loss = pair_loss[0, :NB] + (three[0] + three[1] + three[2])
    loss_sum = jnp.sum(
        lax.all_to_all(jnp.broadcast_to(own_loss, (trainers, 1, NB)), DP, 0, 0, tiled=True),
        axis=(0, 1),
    )
    grad_down = down_step(pair, got_pair, normed)
    bucket_loss = loss_sum / (floor_counts * width)
    progress = jnp.sum(weights * bucket_loss) / jnp.sum(bucket_loss)
    competence_next = competence + 0.5 * (1.0 - competence) * progress
    return (grad_down[None], grad_up[None], bucket_loss, competence_next)


def solution(mesh):
    split = Mesh(mesh.devices.reshape(4, 8, 2, mesh.shape["mp"]), DP_MP)
    placed = (
        P(DP, None, "mp"),
        P(DP, None, "mp"),
        P(None, "mp"),
        P("mp"),
        P(DP, None, "mp"),
        P(DP, None, "mp"),
        P(DP),
        P(DP),
        P(DP),
        P(DP, None),
        P(),
    )
    return jax.shard_map(
        on_device,
        mesh=split,
        in_specs=placed,
        out_specs=(P(DP, None, "mp"), P(DP, None, "mp"), P(), P()),
        check_vma=False,
    )
```
